32 devices in a mesh: gz: 8 (over z, y), gx: 2 (over x), gy: 2 (over core).
Axes of the slice: x: 2, y: 2, z: 4, core: 2. Of those that a mesh axis runs over, the one named last changes fastest.
Arguments:
- electric: float32 [3, 128, 32, 256], P(None, 'gz', 'gx', 'gy'), may hold values from -6 to 6
- magnetic: float32 [3, 128, 32, 256], P(None, 'gz', 'gx', 'gy'), may hold values from -6 to 6
- aux_state: float32 [4, 2, 8, 32, 256], P(None, None, None, 'gx', 'gy'), may hold values from -6 to 6
- material: int32 [32, 256], P('gx', 'gy'), may hold values 0 or 1
- kerr_strength: float32 [2], replicated, may hold values from 0.1 to 1
Outputs:
- electric_out: float32 [3, 128, 32, 256], P(None, 'gz', 'gx', 'gy')
- magnetic_out: float32 [3, 128, 32, 256], P(None, 'gz', 'gx', 'gy')
The draws below stay inside these ranges and needn't reach their ends.
Inputs may be any that keep to these rules, and one draw needn't show every extreme that they name: `material`: 0 marks cladding, 1 the waveguide core.
All inputs are finite; a program needn't handle non-finite values. No bound on the sum of `material` on one device may be relied on, other than what follows from the above.
Results may differ from the reference program's by a relative error of at most 0.00002.
Values sent between devices are 32-bit elements; how exact they have to be, the bound alone decides.
A program may use at most 128 MiB of HBM per device.

```python
import math
import jax
import jax.numpy as jnp

PML = 8
STEPS = 4
NZ = 128
NX = 32
NY = 256


def plant(drawn, rng, least, high):
    longest = drawn.shape.index(max(drawn.shape))
    spots = []
    for shift in (0, 1):
        where = [jax.random.randint(jax.random.fold_in(rng, axis), (), 0, length) for axis, length in enumerate(drawn.shape)]
        where[longest] = (where[longest] + shift) % drawn.shape[longest]
        spots.append(tuple(where))
    return drawn.at[spots[0]].set(least).at[spots[1]].set(high)


def shard_levels(stream_key, shape, split, smallest, high):
    gain, own = 1.0, jax.random.fold_in(stream_key, 6)
    for axis_at, parts in split:
        draws = jnp.exp(jax.random.uniform(jax.random.fold_in(own, axis_at), (parts,), jnp.float32, smallest / len(split), high / len(split)))
        gain = gain * jnp.repeat(draws, shape[axis_at] // parts).reshape([-1 if axis == axis_at else 1 for axis in range(len(shape))])
    return gain


def gaussian(key, shape, deviation, reach, split=(), kind=jnp.bfloat16):
    level = shard_levels(key, shape, split, -0.22, 0.18) if split else 1.0
    entries = jax.random.normal(key, shape, jnp.float32) * deviation * level
    return jnp.minimum(jnp.maximum(entries, -reach), reach).astype(kind)


def setup_inputs(seed: int = 0) -> dict:
    key_list = jax.random.split(jax.random.key(seed), 6)
    return {
        "electric": gaussian(key_list[0], (3, NZ, NX, NY), 1.0, 6.0, ((1, 8), (2, 2), (3, 2)), jnp.float32),
        "magnetic": gaussian(key_list[1], (3, NZ, NX, NY), 1.0, 6.0, ((1, 8), (2, 2), (3, 2)), jnp.float32),
        "aux_state": gaussian(key_list[2], (4, 2, PML, NX, NY), 1.0, 6.0, ((3, 2), (4, 2)), jnp.float32),
        "material": plant((jax.random.randint(key_list[3], (NX, NY), 0, 3) < 1).astype(jnp.int32), jax.random.fold_in(key_list[3], 1), 0, 1),
        "kerr_strength": jnp.clip(jnp.exp(jax.random.uniform(key_list[4], (2,), jnp.float32, math.log(0.1), math.log(1.0))), 0.1, 1.0),
    }


courant = 0.5
pml_rate = 3.0
eps_clad = 2.085
eps_core = 4.0


def decay_rates(layer):
    depth_front = (layer - jnp.arange(layer)).astype(jnp.float32) / layer
    depth_back = (jnp.arange(layer) + 1).astype(jnp.float32) / layer
    depth = jnp.stack([depth_front, depth_back])
    return jnp.exp(-pml_rate * depth ** 3)


def forward_open(values):
    return jnp.concatenate([values[1:], jnp.zeros_like(values[:1])], 0) - values


def backward_open(values):
    return values - jnp.concatenate([jnp.zeros_like(values[:1]), values[:-1]], 0)


def forward_loop(values, axis):
    return jnp.roll(values, -1, axis) - values


def backward_loop(values, axis):
    return values - jnp.roll(values, 1, axis)


def absorb(derivative, state_pair, rates):
    layer = state_pair.shape[1]
    total = derivative.shape[0]
    front = rates[0][:, None, None] * state_pair[0] + (rates[0] - 1.0)[:, None, None] * derivative[:layer]
    back = rates[1][:, None, None] * state_pair[1] + (rates[1] - 1.0)[:, None, None] * derivative[total - layer:]
    merged = jnp.concatenate([derivative[:layer] + front, derivative[layer:total - layer], derivative[total - layer:] + back], 0)
    return merged, jnp.stack([front, back])


def reference(electric, magnetic, aux_state, material, kerr_strength):
    rates = decay_rates(PML)
    core = material == 1
    eps_lin = jnp.where(core, eps_core, eps_clad)
    kerr_cell = jnp.where(core, kerr_strength[1], kerr_strength[0])
    elec_x, elec_y, elec_z = electric[0], electric[1], electric[2]
    magn_x, magn_y, magn_z = magnetic[0], magnetic[1], magnetic[2]
    aux_list = [aux_state[0], aux_state[1], aux_state[2], aux_state[3]]
    for step_index in range(STEPS):
        slope_y, aux_list[0] = absorb(forward_open(elec_y), aux_list[0], rates)
        slope_x, aux_list[1] = absorb(forward_open(elec_x), aux_list[1], rates)
        magn_x = magn_x - courant * (forward_loop(elec_z, 2) - slope_y)
        magn_y = magn_y - courant * (slope_x - forward_loop(elec_z, 1))
        magn_z = magn_z - courant * (forward_loop(elec_y, 1) - forward_loop(elec_x, 2))
        factor = courant / (eps_lin + kerr_cell * (elec_x * elec_x + elec_y * elec_y + elec_z * elec_z))
        slope_hy, aux_list[2] = absorb(backward_open(magn_y), aux_list[2], rates)
        slope_hx, aux_list[3] = absorb(backward_open(magn_x), aux_list[3], rates)
        new_x = elec_x + factor * (backward_loop(magn_z, 2) - slope_hy)
        new_y = elec_y + factor * (slope_hx - backward_loop(magn_z, 1))
        new_z = elec_z + factor * (backward_loop(magn_y, 1) - backward_loop(magn_x, 2))
        fields = jnp.stack([new_x, new_y, new_z, magn_x, magn_y, magn_z])
        fields = jnp.concatenate([fields[:, 1:], jnp.zeros_like(fields[:, :1])], 1)
        elec_x, elec_y, elec_z = fields[0], fields[1], fields[2]
        magn_x, magn_y, magn_z = fields[3], fields[4], fields[5]
    return jnp.stack([elec_x, elec_y, elec_z]), jnp.stack([magn_x, magn_y, magn_z])
```

```python
import functools

import jax
import jax.numpy as jnp
import numpy as np
from jax import lax
from jax.experimental import pallas as pl
from jax.experimental.pallas import tpu as pltpu
from jax.sharding import PartitionSpec as P

PML = 8
STEPS = 4
HALO = 2 * STEPS
COLS = STEPS

courant = 0.5
pml_rate = 3.0
eps_clad = 2.085
eps_core = 4.0

MESH = pl.DeviceIdType.MESH
DEPTH_RATES = [
    float(np.exp(np.float32(-pml_rate) * np.float32((m + 1) / PML) ** 3)) for m in range(PML)
]


def kernel(
    sizes,
    kerr_ref, elec, magn, aux, material,
    elec_out, magn_out,
    F, A, eps_ref, kap_ref, mat,
    pack, pack_aux, pack_mat,
    halo, halo_aux, halo_mat,
    local_sem, send_sem, recv_sem,
):
    n_gz, n_gx, n_gy = sizes
    planes, cols, rows = elec.shape[1:]
    wide = cols + 2 * COLS
    pairs = planes // 2
    first = HALO // 2
    gz, gx, gy = lax.axis_index("gz"), lax.axis_index("gx"), lax.axis_index("gy")
    has_pred, has_succ = gz > 0, gz < n_gz - 1
    at_front, at_back = gz == 0, gz == n_gz - 1
    at_edge = jnp.logical_or(at_front, at_back)
    left = {"gx": lax.rem(gx + n_gx - 1, n_gx)}
    right = {"gx": lax.rem(gx + 1, n_gx)}
    other = {"gy": lax.rem(gy + 1, n_gy)}
    pred = {"gz": jnp.maximum(gz - 1, 0)}
    succ = {"gz": jnp.minimum(gz + 1, n_gz - 1)}
    own, far = pl.ds(0, rows), pl.ds(rows, rows)

    side = jnp.where(at_front, 0, 1)
    loads = [
        pltpu.make_async_copy(elec, F.at[pl.ds(0, 3), pl.ds(0, planes), pl.ds(0, cols), own], local_sem.at[0]),
        pltpu.make_async_copy(magn, F.at[pl.ds(3, 3), pl.ds(0, planes), pl.ds(0, cols), own], local_sem.at[1]),
    ]
    load_aux = pltpu.make_async_copy(
        aux.at[:, side], A.at[:, :, pl.ds(0, cols), own], local_sem.at[2]
    )
    for load in loads:
        load.start()

    @pl.when(at_edge)
    def _():
        load_aux.start()

    barrier = pltpu.get_barrier_semaphore()
    for peer in (left, right, other):
        pl.semaphore_signal(barrier, inc=1, device_id=peer, device_id_type=MESH)

    @pl.when(has_pred)
    def _():
        pl.semaphore_signal(barrier, inc=1, device_id=pred, device_id_type=MESH)

    @pl.when(has_succ)
    def _():
        pl.semaphore_signal(barrier, inc=1, device_id=succ, device_id_type=MESH)

    pl.semaphore_wait(barrier, 3 + has_pred.astype(jnp.int32) + has_succ.astype(jnp.int32))

    count = [0]

    def remote(src, dst, peer):
        at = count[0]
        count[0] += 1
        return pltpu.make_async_remote_copy(
            src_ref=src, dst_ref=dst, send_sem=send_sem.at[at], recv_sem=recv_sem.at[at],
            device_id=peer, device_id_type=MESH,
        )

    def fields(lo, n, at, width, lanes):
        return F.at[pl.ds(lo, 3), pl.ds(at, n), pl.ds(0, width), lanes]

    x_first = [remote(pack.at[d, pl.ds(0, first)], halo.at[d, pl.ds(0, first), :, :, own], p) for d, p in ((0, left), (1, right))]
    x_mat = [remote(pack_mat.at[d], halo_mat.at[d, :, own], p) for d, p in ((0, left), (1, right))]
    x_aux = [remote(pack_aux.at[d], halo_aux.at[d, :, :, :, own], p) for d, p in ((0, left), (1, right))]
    x_rest = [
        remote(pack.at[d, pl.ds(first, pairs - first)], halo.at[d, pl.ds(first, pairs - first), :, :, own], p)
        for d, p in ((0, left), (1, right))
    ]
    z_own = [
        remote(src.at[:, pl.ds(0, HALO)], fields(lo, HALO, planes, cols, own), pred)
        for lo, src in ((0, elec), (3, magn))
    ]
    z_far = [
        remote(halo.at[d, pl.ds(0, first), :, :, own], halo.at[d, pl.ds(pairs, first), :, :, own], pred)
        for d in (0, 1)
    ]
    y_own = [remote(src, fields(lo, planes, 0, cols, far), other) for lo, src in ((0, elec), (3, magn))]
    y_x = [
        remote(halo.at[d, pl.ds(0, pairs), :, :, own], halo.at[d, pl.ds(0, pairs), :, :, far], other)
        for d in (0, 1)
    ]
    y_xz = [
        remote(halo.at[d, pl.ds(pairs, first), :, :, own], halo.at[d, pl.ds(pairs, first), :, :, far], other)
        for d in (0, 1)
    ]
    y_z = [
        remote(fields(lo, HALO, planes, cols, own), fields(lo, HALO, planes, cols, far), other)
        for lo in (0, 3)
    ]
    y_aux = remote(aux.at[:, side], A.at[:, :, pl.ds(0, cols), far], other)
    y_haux = [remote(halo_aux.at[d, :, :, :, own], halo_aux.at[d, :, :, :, far], other) for d in (0, 1)]
    y_hmat = [remote(halo_mat.at[d, :, own], halo_mat.at[d, :, far], other) for d in (0, 1)]
    y_m = remote(mat.at[pl.ds(0, cols), own], mat.at[pl.ds(0, cols), far], other)

    @pl.when(has_pred)
    def _():
        for copy in z_own:
            copy.start()

    for load in loads:
        load.wait()

    def pack_pair(q, _):
        for c in range(6):
            pack[0, q, c, 0:COLS] = F[c, 2 * q, 0:COLS, 0:rows]
            pack[0, q, c, COLS:] = F[c, 2 * q + 1, 0:COLS, 0:rows]
            pack[1, q, c, 0:COLS] = F[c, 2 * q + 1, cols - COLS : cols, 0:rows]
            pack[1, q, c, COLS:] = F[c, 2 * q, cols - COLS : cols, 0:rows]
        return _

    lax.fori_loop(0, first, pack_pair, 0)
    for copy in x_first:
        copy.start()
    m = (material[...] == 1).astype(jnp.float32)
    mat[0:cols, 0:rows] = m
    pack_mat[0] = m[0 : 2 * COLS]
    pack_mat[1] = m[cols - 2 * COLS : cols]
    for copy in x_mat:
        copy.start()
    y_m.start()

    @pl.when(at_edge)
    def _():
        load_aux.wait()

        def pack_aux_pair(q, _):
            for c in range(4):
                pack_aux[0, q, c, 0:COLS] = A[c, 2 * q, 0:COLS, 0:rows]
                pack_aux[0, q, c, COLS:] = A[c, 2 * q + 1, 0:COLS, 0:rows]
                pack_aux[1, q, c, 0:COLS] = A[c, 2 * q + 1, cols - COLS : cols, 0:rows]
                pack_aux[1, q, c, COLS:] = A[c, 2 * q, cols - COLS : cols, 0:rows]
            return _

        lax.fori_loop(0, PML // 2, pack_aux_pair, 0)
        for copy in x_aux:
            copy.start()
        y_aux.start()

    lax.fori_loop(first, pairs, pack_pair, 0)
    for copy in x_rest:
        copy.start()
    for copy in y_own:
        copy.start()

    for copy in x_first:
        copy.wait()

    @pl.when(has_pred)
    def _():
        for copy in z_far:
            copy.start()

    for copy, on in zip(x_mat, y_hmat):
        copy.wait()
        on.start()
    for copy, on in zip(x_rest, y_x):
        copy.wait()
        on.start()

    @pl.when(at_edge)
    def _():
        for copy, on in zip(x_aux, y_haux):
            copy.wait()
            on.start()

    def unpack(q, _):
        low = lax.broadcasted_iota(jnp.int32, (2 * COLS, 2 * rows), 0) < COLS
        for c in range(6):
            r, l = halo[0, q, c], halo[1, q, c]
            F[c, 2 * q, cols:wide] = jnp.where(low, r, l)
            F[c, 2 * q + 1, cols:wide] = pltpu.roll(jnp.where(low, l, r), COLS, 0)
        return _

    def unpack_aux(q, _):
        low = lax.broadcasted_iota(jnp.int32, (2 * COLS, 2 * rows), 0) < COLS
        for c in range(4):
            r, l = halo_aux[0, q, c], halo_aux[1, q, c]
            A[c, 2 * q, cols:wide] = jnp.where(low, r, l)
            A[c, 2 * q + 1, cols:wide] = pltpu.roll(jnp.where(low, l, r), COLS, 0)
        return _

    def sweep(s, lo, hi):
        shift = s + jnp.where(at_front, 0, planes - PML)

        def plane(a, absorbing):
            ex, ey, ez = F[0, a], F[1, a], F[2, a]
            gy_, gx_ = F[1, a + 1] - ey, F[0, a + 1] - ex
            if absorbing:
                k = a - shift
                m = jnp.where(at_front, PML - 1 - k, k)
                b = jnp.float32(DEPTH_RATES[0])
                for i in range(1, PML):
                    b = jnp.where(m == i, jnp.float32(DEPTH_RATES[i]), b)

                def absorb(c, g):
                    s_new = b * A[c, k] + (b - 1.0) * g
                    A[c, k] = s_new
                    return g + s_new

                gy_, gx_ = absorb(0, gy_), absorb(1, gx_)
            nx, ny = wide - 1, 2 * rows - 1
            hx = F[3, a] - courant * ((pltpu.roll(ez, ny, 1) - ez) - gy_)
            hy = F[4, a] - courant * (gx_ - (pltpu.roll(ez, nx, 0) - ez))
            hz = F[5, a] - courant * ((pltpu.roll(ey, nx, 0) - ey) - (pltpu.roll(ex, ny, 1) - ex))
            F[3, a], F[4, a], F[5, a] = hx, hy, hz
            factor = courant / (eps_ref[...] + kap_ref[...] * (ex * ex + ey * ey + ez * ez))
            before = jnp.maximum(a - 1, 0)
            hy_, hx_ = hy - F[4, before], hx - F[3, before]
            if absorbing:
                hy_, hx_ = absorb(2, hy_), absorb(3, hx_)
            F[0, a] = ex + factor * ((hz - pltpu.roll(hz, 1, 1)) - hy_)
            F[1, a] = ey + factor * (hx_ - (hz - pltpu.roll(hz, 1, 0)))
            F[2, a] = ez + factor * ((hy - pltpu.roll(hy, 1, 0)) - (hx - pltpu.roll(hx, 1, 1)))

        def body(a, _):
            inside = jnp.logical_and(at_edge, jnp.logical_and(a >= shift, a < shift + PML))

            @pl.when(inside)
            def _():
                plane(a, True)

            @pl.when(jnp.logical_not(inside))
            def _():
                plane(a, False)

            return _

        lax.fori_loop(lo, hi, body, None)

    for copy in y_hmat + y_x + y_own + [y_m]:
        copy.wait()

    @pl.when(at_edge)
    def _():
        for copy in y_haux + [y_aux]:
            copy.wait()
        lax.fori_loop(0, PML // 2, unpack_aux, 0)

    lax.fori_loop(0, pairs, unpack, 0)
    low = lax.broadcasted_iota(jnp.int32, (2 * COLS, 2 * rows), 0) < COLS
    mat[cols:wide] = jnp.where(low, halo_mat[0], halo_mat[1])
    core = mat[...] > 0.5
    eps_ref[...] = jnp.where(core, jnp.float32(eps_core), jnp.float32(eps_clad))
    kap_ref[...] = jnp.where(core, kerr_ref[1], kerr_ref[0])

    def early(s, _):
        sweep(s, s, planes - 1 - s)
        return _

    @pl.when(has_succ)
    def _():
        for copy in z_own + z_far:
            copy.wait_recv()
        for copy in y_z + y_xz:
            copy.start()

    lax.fori_loop(0, STEPS, early, 0)

    @pl.when(has_pred)
    def _():
        for copy in z_own + z_far:
            copy.wait_send()

    @pl.when(has_succ)
    def _():
        for copy in y_z + y_xz:
            copy.wait()
        lax.fori_loop(pairs, pairs + first, unpack, 0)

    @pl.when(at_back)
    def _():
        def clear(a, _):
            for c in range(6):
                F[c, a] = jnp.zeros((wide, 2 * rows), jnp.float32)
            return _

        lax.fori_loop(planes, planes + HALO, clear, 0)

    def late(s, _):
        hi = jnp.where(at_back, jnp.minimum(planes + s, planes + HALO - 1 - s), planes + HALO - 1 - s)
        sweep(s, planes - 1 - s, hi)
        return _

    lax.fori_loop(0, STEPS, late, 0)

    stores = [
        pltpu.make_async_copy(fields(lo, planes, STEPS, cols, own), out, local_sem.at[at])
        for at, (lo, out) in enumerate(((0, elec_out), (3, magn_out)))
    ]
    for store in stores:
        store.start()
    for store in stores:
        store.wait()


def shards(sizes, electric, magnetic, aux_state, material, kerr_strength):
    _, planes, cols, rows = electric.shape
    wide, deep = cols + 2 * COLS, planes + HALO
    f32 = jnp.float32
    any_space = pl.BlockSpec(memory_space=pl.ANY)
    vmem = pl.BlockSpec(memory_space=pltpu.VMEM)
    shape = jax.ShapeDtypeStruct(electric.shape, f32)
    return pl.pallas_call(
        functools.partial(kernel, sizes),
        out_shape=(shape, shape),
        in_specs=[pl.BlockSpec(memory_space=pltpu.SMEM), any_space, any_space, any_space, vmem],
        out_specs=(any_space, any_space),
        scratch_shapes=[
            pltpu.VMEM((6, deep, wide, 2 * rows), f32),
            pltpu.VMEM((4, PML, wide, 2 * rows), f32),
            pltpu.VMEM((wide, 2 * rows), f32),
            pltpu.VMEM((wide, 2 * rows), f32),
            pltpu.VMEM((wide, 2 * rows), f32),
            pltpu.VMEM((2, planes // 2, 6, 2 * COLS, rows), f32),
            pltpu.VMEM((2, PML // 2, 4, 2 * COLS, rows), f32),
            pltpu.VMEM((2, 2 * COLS, rows), f32),
            pltpu.VMEM((2, deep // 2, 6, 2 * COLS, 2 * rows), f32),
            pltpu.VMEM((2, PML // 2, 4, 2 * COLS, 2 * rows), f32),
            pltpu.VMEM((2, 2 * COLS, 2 * rows), f32),
            pltpu.SemaphoreType.DMA((3,)),
            pltpu.SemaphoreType.DMA((32,)),
            pltpu.SemaphoreType.DMA((32,)),
        ],
        compiler_params=pltpu.CompilerParams(
            collective_id=0, has_side_effects=True, vmem_limit_bytes=40 * 2**20
        ),
    )(kerr_strength, electric, magnetic, aux_state, material)


def solution(mesh):
    sizes = tuple(mesh.shape[axis] for axis in ("gz", "gx", "gy"))
    in_specs = (
        P(None, "gz", "gx", "gy"),
        P(None, "gz", "gx", "gy"),
        P(None, None, None, "gx", "gy"),
        P("gx", "gy"),
        P(),
    )
    out_specs = (P(None, "gz", "gx", "gy"), P(None, "gz", "gx", "gy"))
    return jax.shard_map(
        functools.partial(shards, sizes),
        mesh=mesh, in_specs=in_specs, out_specs=out_specs, check_vma=False,
    )
```

```python
import functools

import jax
import jax.numpy as jnp
import numpy as np
from jax import lax
from jax.experimental import pallas as pl
from jax.experimental.pallas import tpu as pltpu
from jax.sharding import PartitionSpec as P

PML = 8
STEPS = 4
HALO = 2 * STEPS
COLS = STEPS
PAD = 4
GROUP = 4

courant = 0.5
pml_rate = 3.0
eps_clad = 2.085
eps_core = 4.0

MESH = pl.DeviceIdType.MESH
DEPTH_RATES = [
    float(np.exp(np.float32(-pml_rate) * np.float32((m + 1) / PML) ** 3)) for m in range(PML)
]


def kernel(
    sizes,
    kerr_ref, elec, magn, aux, material,
    elec_out, magn_out,
    F, A, eps_ref, kap_ref, mat, mat_own, own_fields,
    pack, pack_aux, pack_mat,
    halo, halo_aux, halo_mat,
    local_sem, send_sem, recv_sem, z_send_sem, z_recv_sem,
):
    n_gz, n_gx, n_gy = sizes
    planes, cols, rows = elec.shape[1:]
    wide = cols + 2 * COLS
    half = planes // 2
    quads = half // 2
    pairs = planes // 2
    gz, gx, gy = lax.axis_index("gz"), lax.axis_index("gx"), lax.axis_index("gy")
    low_part, high_part = gy == 0, gy == 1
    has_pred = gz > 0
    takes_z = jnp.logical_and(high_part, gz < n_gz - 1)
    at_front, at_back = gz == 0, gz == n_gz - 1
    at_edge = jnp.logical_or(at_front, at_back)
    left = {"gx": lax.rem(gx + n_gx - 1, n_gx)}
    right = {"gx": lax.rem(gx + 1, n_gx)}
    other = {"gy": 1 - gy}
    pred = {"gz": jnp.maximum(gz - 1, 0), "gy": 1}
    succ = [{"gz": jnp.minimum(gz + 1, n_gz - 1), "gy": part} for part in (0, 1)]
    own, far = pl.ds(0, rows), pl.ds(rows, rows)
    z_lanes = pl.ds(pl.multiple_of((1 - gy) * rows, rows), rows)
    start = half * gy
    side = jnp.where(at_front, 0, 1)
    args = ((0, elec), (3, magn))

    def fields(lo, at, n, width, lanes):
        return F.at[pl.ds(lo, 3), pl.ds(PAD + at, n), pl.ds(0, width), lanes]

    def when(condition, work):
        pl.when(condition)(work)

    def each(copies, method):
        def work():
            for copy in copies:
                getattr(copy, method)()

        return work

    count = [0]

    def local(src, dst):
        count[0] += 1
        return pltpu.make_async_copy(src, dst, local_sem.at[count[0] - 1])

    stage_low = [local(r.at[:, pl.ds(0, half)], own_fields.at[pl.ds(lo, 3), pl.ds(0, half)]) for lo, r in args]
    stage_high = [local(r.at[:, pl.ds(half, half)], own_fields.at[pl.ds(lo, 3), pl.ds(half, half)]) for lo, r in args]
    load_mat = local(material, mat_own)
    load_aux = local(aux.at[:, side], A.at[:, pl.ds(0, PML), pl.ds(0, cols), own])
    load_low = [local(r.at[:, pl.ds(0, half)], fields(lo, 0, half, cols, own)) for lo, r in args]
    load_high = [local(r.at[:, pl.ds(half, half)], fields(lo, half - start, half, cols, own)) for lo, r in args]
    for copy in stage_low + stage_high + [load_mat]:
        copy.start()
    when(at_edge, each([load_aux], "start"))
    when(low_part, each(load_low, "start"))
    each(load_high, "start")()

    barrier = pltpu.get_barrier_semaphore()

    def greet(peers):
        def work():
            for peer in peers:
                pl.semaphore_signal(barrier, inc=1, device_id=peer, device_id_type=MESH)

        return work

    greet([left, right, other])()
    when(has_pred, greet([pred]))
    when(takes_z, greet(succ))
    pl.semaphore_wait(barrier, 3 + has_pred.astype(jnp.int32) + 2 * takes_z.astype(jnp.int32))

    numbered = [0]

    def remote(src, dst, peer):
        at = numbered[0]
        numbered[0] += 1
        return pltpu.make_async_remote_copy(
            src_ref=src, dst_ref=dst, send_sem=send_sem.at[at], recv_sem=recv_sem.at[at],
            device_id=peer, device_id_type=MESH,
        )

    z_numbered = [0]

    def z_remote(src, dst, sender):
        at = z_numbered[0]
        z_numbered[0] += 1
        return pltpu.make_async_remote_copy(
            src_ref=src, dst_ref=dst, send_sem=z_send_sem.at[at], recv_sem=z_recv_sem.at[at, sender],
            device_id=pred, device_id_type=MESH,
        )

    def tiles(d, at, n, lanes):
        return halo.at[d, pl.ds(at, n), :, :, lanes]

    both = ((0, left), (1, right))
    x_low = [remote(pack.at[d, pl.ds(0, quads)], tiles(d, 0, quads, own), p) for d, p in both]
    x_high = [remote(pack.at[d, pl.ds(quads, quads)], tiles(d, quads, quads, own), p) for d, p in both]
    x_mat = [remote(pack_mat.at[d], halo_mat.at[d, :, own], p) for d, p in both]
    x_aux = [remote(pack_aux.at[d], halo_aux.at[d, :, :, :, own], p) for d, p in both]
    y_low = [remote(r.at[:, pl.ds(0, half)], fields(lo, 0, half, cols, far), other) for lo, r in args]
    y_high = [remote(r.at[:, pl.ds(half, half)], fields(lo, start, half, cols, far), other) for lo, r in args]
    yx_low = [remote(tiles(d, 0, quads, own), tiles(d, 0, quads, far), other) for d in (0, 1)]
    yx_high = [remote(tiles(d, quads, quads, own), tiles(d, quads, quads, far), other) for d in (0, 1)]
    y_aux = [remote(aux.at[:, side], A.at[:, pl.ds(0, PML), pl.ds(0, cols), far], other)]
    yx_aux = [remote(halo_aux.at[d, :, :, :, own], halo_aux.at[d, :, :, :, far], other) for d in (0, 1)]
    y_mat = [remote(mat.at[pl.ds(0, cols), own], mat.at[pl.ds(0, cols), far], other)]
    yx_mat = [remote(halo_mat.at[d, :, own], halo_mat.at[d, :, far], other) for d in (0, 1)]

    def z_copies(sender, lanes):
        z_numbered[0] = 0
        sent = [z_remote(r.at[:, pl.ds(0, half)], fields(lo, half, half, cols, lanes), sender) for lo, r in args]
        passed = [z_remote(tiles(d, 0, quads, own), tiles(d, pairs, quads, lanes), sender) for d in (0, 1)]
        return sent, passed

    z_own, z_passed = z_copies(gy, z_lanes)
    z_from = [copy for sender, lanes in ((0, far), (1, own)) for part in z_copies(sender, lanes) for copy in part]

    when(has_pred, each(z_own, "start"))

    def pack_pair(q, carry):
        for c in range(6):
            pack[0, q, c, 0:COLS] = own_fields[c, 2 * q, 0:COLS]
            pack[0, q, c, COLS:] = own_fields[c, 2 * q + 1, 0:COLS]
            pack[1, q, c, 0:COLS] = own_fields[c, 2 * q + 1, cols - COLS : cols]
            pack[1, q, c, COLS:] = own_fields[c, 2 * q, cols - COLS : cols]
        return carry

    each(stage_low, "wait")()
    lax.fori_loop(0, quads, pack_pair, 0)
    each(x_low, "start")()
    each(stage_high, "wait")()
    lax.fori_loop(quads, pairs, pack_pair, 0)
    each(x_high, "start")()
    load_mat.wait()
    m = (mat_own[...] == 1).astype(jnp.float32)
    mat[0:cols, 0:rows] = m
    pack_mat[0] = m[0 : 2 * COLS]
    pack_mat[1] = m[cols - 2 * COLS : cols]
    each(x_mat + y_mat, "start")()

    @pl.when(at_edge)
    def _():
        load_aux.wait()

        def pack_aux_pair(q, carry):
            for c in range(4):
                pack_aux[0, q, c, 0:COLS] = A[c, 2 * q, 0:COLS, 0:rows]
                pack_aux[0, q, c, COLS:] = A[c, 2 * q + 1, 0:COLS, 0:rows]
                pack_aux[1, q, c, 0:COLS] = A[c, 2 * q + 1, cols - COLS : cols, 0:rows]
                pack_aux[1, q, c, COLS:] = A[c, 2 * q, cols - COLS : cols, 0:rows]
            return carry

        lax.fori_loop(0, PML // 2, pack_aux_pair, 0)
        each(x_aux + y_aux, "start")()

    when(high_part, each(y_low, "start"))
    each(y_high, "start")()

    def clear(lo, n):
        def plane(a, carry):
            for c in range(6):
                F[c, a] = jnp.zeros((wide, 2 * rows), jnp.float32)
            return carry

        lax.fori_loop(lo, lo + n, plane, 0)

    clear(0, PAD)
    when(jnp.logical_and(at_back, high_part), lambda: clear(PAD + half, half))

    each(x_low, "wait")()
    when(has_pred, each(z_passed, "start"))
    when(high_part, each(yx_low, "start"))
    each(x_mat, "wait")()
    each(yx_mat, "start")()

    @pl.when(at_edge)
    def _():
        each(x_aux, "wait")()
        each(yx_aux, "start")()

    each(x_high, "wait")()
    each(yx_high, "start")()

    def joined(r, l):
        low = lax.broadcasted_iota(jnp.int32, (2 * COLS, 2 * rows), 0) < COLS
        return jnp.where(low, r, l), pltpu.roll(jnp.where(low, l, r), COLS, 0)

    def unpack(q, carry):
        at = PAD + 2 * q - start
        for c in range(6):
            F[c, at, cols:wide], F[c, at + 1, cols:wide] = joined(halo[0, q, c], halo[1, q, c])
        return carry

    def unpack_aux(q, carry):
        for c in range(4):
            A[c, 2 * q, cols:wide], A[c, 2 * q + 1, cols:wide] = joined(halo_aux[0, q, c], halo_aux[1, q, c])
        return carry

    nx, ny = wide - 1, 2 * rows - 1

    def group(a, s, shift, absorbing):
        E = [[F[c, a + i] for c in range(3)] for i in range(GROUP + 1)]
        H = [[F[c, a + i] for c in range(3, 6)] for i in range(GROUP)]
        before = F[3, a - 1], F[4, a - 1]
        rates = []
        states = []
        if absorbing:
            for i in range(GROUP):
                k = a + i - shift
                inside = jnp.logical_and(k >= 0, k < PML)
                at = jnp.where(inside, k, PML)
                m = jnp.where(at_front, PML - 1 - k, k)
                b = jnp.float32(DEPTH_RATES[0])
                for j in range(1, PML):
                    b = jnp.where(m == j, jnp.float32(DEPTH_RATES[j]), b)
                rates.append((inside, at, b))
                states.append([A[c, at] for c in range(4)])

        new_states = []

        def absorb(c, i, g):
            if not absorbing:
                return g
            inside, at, b = rates[i]
            s_new = b * states[i][c] + (b - 1.0) * g
            new_states.append((c, at, s_new))
            return jnp.where(inside, g + s_new, g)

        new_h = []
        for i in range(GROUP):
            ex, ey, ez = E[i]
            slope_y = absorb(0, i, E[i + 1][1] - ey)
            slope_x = absorb(1, i, E[i + 1][0] - ex)
            hx = H[i][0] - courant * ((pltpu.roll(ez, ny, 1) - ez) - slope_y)
            hy = H[i][1] - courant * (slope_x - (pltpu.roll(ez, nx, 0) - ez))
            hz = H[i][2] - courant * ((pltpu.roll(ey, nx, 0) - ey) - (pltpu.roll(ex, ny, 1) - ex))
            new_h.append((hx, hy, hz))
        new_e = []
        for i in range(GROUP):
            ex, ey, ez = E[i]
            hx, hy, hz = new_h[i]
            below = before if i == 0 else new_h[i - 1]
            factor = courant / (eps_ref[...] + kap_ref[...] * (ex * ex + ey * ey + ez * ez))
            slope_hy = absorb(2, i, hy - below[1])
            slope_hx = absorb(3, i, hx - below[0])
            new_e.append((
                ex + factor * ((hz - pltpu.roll(hz, 1, 1)) - slope_hy),
                ey + factor * (slope_hx - (hz - pltpu.roll(hz, 1, 0))),
                ez + factor * ((hy - pltpu.roll(hy, 1, 0)) - (hx - pltpu.roll(hx, 1, 1))),
            ))
        for i in range(GROUP):
            for c in range(3):
                F[c, a + i] = new_e[i][c]
                F[3 + c, a + i] = new_h[i][c]
        for c, at, value in new_states:
            A[c, at] = value

    def sweep(s, lo, n_groups, top):
        shift = PAD + s + jnp.where(at_front, 0, planes - PML) - start

        def body(g, carry):
            a = PAD + lo + GROUP * g
            inside = jnp.logical_and(at_edge, jnp.logical_and(a + GROUP > shift, a < shift + PML))
            when(inside, lambda: group(a, s, shift, True))
            when(jnp.logical_not(inside), lambda: group(a, s, shift, False))

            if top is not None:
                @pl.when(jnp.logical_and(at_back, high_part))
                def _():
                    def plane(p, carry):
                        for c in range(3):
                            F[c, p] = jnp.zeros((wide, 2 * rows), jnp.float32)
                        return carry

                    lax.fori_loop(jnp.maximum(a, PAD + top), a + GROUP, plane, 0)

            return carry

        lax.fori_loop(0, n_groups, body, 0)

    each(load_high, "wait")()

    @pl.when(low_part)
    def _():
        each(load_low, "wait")()
        each(y_low + yx_low, "wait_recv")()

    when(high_part, each(y_high + yx_high, "wait_recv"))
    each(y_mat + yx_mat, "wait")()

    @pl.when(at_edge)
    def _():
        each(y_aux + yx_aux, "wait")()
        lax.fori_loop(0, PML // 2, unpack_aux, 0)

    lax.fori_loop(quads * gy, quads * gy + quads, unpack, 0)
    low = lax.broadcasted_iota(jnp.int32, (2 * COLS, 2 * rows), 0) < COLS
    mat[cols:wide] = jnp.where(low, halo_mat[0], halo_mat[1])
    core = mat[...] > 0.5
    eps_ref[...] = jnp.where(core, jnp.float32(eps_core), jnp.float32(eps_clad))
    kap_ref[...] = jnp.where(core, kerr_ref[1], kerr_ref[0])

    def early(s, carry):
        n_groups = (half - 1 - 2 * s + GROUP - 1) // GROUP
        sweep(s, half - 1 - s - GROUP * n_groups, n_groups, None)
        return carry

    lax.fori_loop(0, STEPS, early, 0)

    when(low_part, each(y_high + yx_high, "wait_recv"))
    when(takes_z, each(z_from, "wait_recv"))

    @pl.when(jnp.logical_or(low_part, takes_z))
    def _():
        lax.fori_loop(quads * gy + quads, quads * gy + 2 * quads, unpack, 0)

    def late(s, carry):
        sweep(s, half - 1 - s, half // GROUP, half + s)
        return carry

    lax.fori_loop(0, STEPS, late, 0)

    results = ((0, elec_out), (3, magn_out))
    store = [local(fields(lo, STEPS, half, cols, own), r.at[:, pl.ds(start, half)]) for lo, r in results]
    hand = [remote(fields(lo, STEPS, half, cols, far), r.at[:, pl.ds(start, half)], other) for lo, r in results]
    each(hand + store, "start")()
    when(has_pred, each(z_own + z_passed, "wait_send"))
    when(high_part, each(y_low + yx_low, "wait_send"))
    each(y_high + yx_high, "wait_send")()
    each(hand + store, "wait")()


def shards(sizes, electric, magnetic, aux_state, material, kerr_strength):
    _, planes, cols, rows = electric.shape
    wide, deep = cols + 2 * COLS, planes + HALO
    f32 = jnp.float32
    any_space = pl.BlockSpec(memory_space=pl.ANY)
    shape = jax.ShapeDtypeStruct(electric.shape, f32)
    return pl.pallas_call(
        functools.partial(kernel, sizes),
        out_shape=(shape, shape),
        in_specs=[pl.BlockSpec(memory_space=pltpu.SMEM), any_space, any_space, any_space, any_space],
        out_specs=(any_space, any_space),
        scratch_shapes=[
            pltpu.VMEM((6, PAD + planes, wide, 2 * rows), f32),
            pltpu.VMEM((4, PML + 1, wide, 2 * rows), f32),
            pltpu.VMEM((wide, 2 * rows), f32),
            pltpu.VMEM((wide, 2 * rows), f32),
            pltpu.VMEM((wide, 2 * rows), f32),
            pltpu.VMEM((cols, rows), jnp.int32),
            pltpu.VMEM((6, planes, cols, rows), f32),
            pltpu.VMEM((2, planes // 2, 6, 2 * COLS, rows), f32),
            pltpu.VMEM((2, PML // 2, 4, 2 * COLS, rows), f32),
            pltpu.VMEM((2, 2 * COLS, rows), f32),
            pltpu.VMEM((2, deep // 2, 6, 2 * COLS, 2 * rows), f32),
            pltpu.VMEM((2, PML // 2, 4, 2 * COLS, 2 * rows), f32),
            pltpu.VMEM((2, 2 * COLS, 2 * rows), f32),
            pltpu.SemaphoreType.DMA((12,)),
            pltpu.SemaphoreType.DMA((24,)),
            pltpu.SemaphoreType.DMA((24,)),
            pltpu.SemaphoreType.DMA((4,)),
            pltpu.SemaphoreType.DMA((4, 2)),
        ],
        compiler_params=pltpu.CompilerParams(
            collective_id=0, has_side_effects=True, vmem_limit_bytes=60 * 2**20
        ),
    )(kerr_strength, electric, magnetic, aux_state, material)


def solution(mesh):
    sizes = tuple(mesh.shape[axis] for axis in ("gz", "gx", "gy"))
    in_specs = (
        P(None, "gz", "gx", "gy"),
        P(None, "gz", "gx", "gy"),
        P(None, None, None, "gx", "gy"),
        P("gx", "gy"),
        P(),
    )
    out_specs = (P(None, "gz", "gx", "gy"), P(None, "gz", "gx", "gy"))
    return jax.shard_map(
        functools.partial(shards, sizes),
        mesh=mesh, in_specs=in_specs, out_specs=out_specs, check_vma=False,
    )
```

```python
import functools

import jax
import jax.numpy as jnp
import numpy as np
from jax import lax
from jax.experimental import pallas as pl
from jax.experimental.pallas import tpu as pltpu
from jax.sharding import PartitionSpec as P

PML = 8
STEPS = 4
HALO = 2 * STEPS
COLS = STEPS
PAD = 4
GROUP = SPAN = 4
PAIRS = SPAN // 2

courant = 0.5
pml_rate = 3.0
eps_clad = 2.085
eps_core = 4.0

MESH = pl.DeviceIdType.MESH
DEPTH_RATES = [
    float(np.exp(np.float32(-pml_rate) * np.float32((m + 1) / PML) ** 3)) for m in range(PML)
]


def kernel(
    sizes,
    kerr_ref, elec, magn, aux, material,
    elec_out, magn_out,
    F, A, eps_ref, kap_ref, mat, mat_own, own_fields,
    pack, pack_aux, pack_mat,
    halo, halo_aux, halo_mat,
    local_sem, send_sem, recv_sem, z_send_sem, z_recv_sem,
):
    n_gz, n_gx, n_gy = sizes
    planes, cols, rows = elec.shape[1:]
    wide = cols + 2 * COLS
    half = planes // 2
    quads = half // 2
    pairs = planes // 2
    gz, gx, gy = lax.axis_index("gz"), lax.axis_index("gx"), lax.axis_index("gy")
    low_part, high_part = gy == 0, gy == 1
    has_pred = gz > 0
    takes_z = jnp.logical_and(high_part, gz < n_gz - 1)
    at_front, at_back = gz == 0, gz == n_gz - 1
    at_edge = jnp.logical_or(at_front, at_back)
    left = {"gx": lax.rem(gx + n_gx - 1, n_gx)}
    right = {"gx": lax.rem(gx + 1, n_gx)}
    other = {"gy": 1 - gy}
    pred = {"gz": jnp.maximum(gz - 1, 0), "gy": 1}
    succ = [{"gz": jnp.minimum(gz + 1, n_gz - 1), "gy": part} for part in (0, 1)]
    own, far = pl.ds(0, rows), pl.ds(rows, rows)
    z_lanes = pl.ds(pl.multiple_of((1 - gy) * rows, rows), rows)
    start = half * gy
    side = jnp.where(at_front, 0, 1)
    args = ((0, elec), (3, magn))

    def fields(lo, at, n, width, lanes):
        return F.at[pl.ds(lo, 3), pl.ds(PAD + at, n), pl.ds(0, width), lanes]

    def when(condition, work):
        pl.when(condition)(work)

    def each(copies, method):
        def work():
            for copy in copies:
                getattr(copy, method)()

        return work

    count = [0]

    def local(src, dst):
        count[0] += 1
        return pltpu.make_async_copy(src, dst, local_sem.at[count[0] - 1])

    stage_low = [local(r.at[:, pl.ds(0, half)], own_fields.at[pl.ds(lo, 3), pl.ds(0, half)]) for lo, r in args]
    stage_high = [local(r.at[:, pl.ds(half, half)], own_fields.at[pl.ds(lo, 3), pl.ds(half, half)]) for lo, r in args]
    load_mat = local(material, mat_own)
    load_aux = local(aux.at[:, side], A.at[:, pl.ds(0, PML), pl.ds(0, cols), own])
    load_low = [local(r.at[:, pl.ds(0, half)], fields(lo, 0, half, cols, own)) for lo, r in args]
    load_high = [local(r.at[:, pl.ds(half, half)], fields(lo, half - start, half, cols, own)) for lo, r in args]
    for copy in stage_low + stage_high + [load_mat]:
        copy.start()
    when(at_edge, each([load_aux], "start"))
    when(low_part, each(load_low, "start"))
    each(load_high, "start")()

    barrier = pltpu.get_barrier_semaphore()

    def greet(peers):
        def work():
            for peer in peers:
                pl.semaphore_signal(barrier, inc=1, device_id=peer, device_id_type=MESH)

        return work

    greet([left, right, other])()
    when(has_pred, greet([pred]))
    when(takes_z, greet(succ))
    pl.semaphore_wait(barrier, 3 + has_pred.astype(jnp.int32) + 2 * takes_z.astype(jnp.int32))

    numbered = [0]

    def remote(src, dst, peer):
        at = numbered[0]
        numbered[0] += 1
        return pltpu.make_async_remote_copy(
            src_ref=src, dst_ref=dst, send_sem=send_sem.at[at], recv_sem=recv_sem.at[at],
            device_id=peer, device_id_type=MESH,
        )

    z_numbered = [0]

    def z_remote(src, dst, sender):
        at = z_numbered[0]
        z_numbered[0] += 1
        return pltpu.make_async_remote_copy(
            src_ref=src, dst_ref=dst, send_sem=z_send_sem.at[at], recv_sem=z_recv_sem.at[at, sender],
            device_id=pred, device_id_type=MESH,
        )

    def tiles(d, at, n, lanes):
        return halo.at[d, pl.ds(at, n), :, :, lanes]

    both = ((0, left), (1, right))
    chunks = [(k * PAIRS, PAIRS) for k in range(pairs // PAIRS)]
    x_halo = [[remote(pack.at[d, pl.ds(at, n)], tiles(d, at, n, own), p) for d, p in both] for at, n in chunks]
    x_mat = [remote(pack_mat.at[d], halo_mat.at[d, :, own], p) for d, p in both]
    x_aux = [remote(pack_aux.at[d], halo_aux.at[d, :, :, :, own], p) for d, p in both]
    y_low = [remote(r.at[:, pl.ds(0, half)], fields(lo, 0, half, cols, far), other) for lo, r in args]
    y_high = [remote(r.at[:, pl.ds(half, half)], fields(lo, start, half, cols, far), other) for lo, r in args]
    yx = [[remote(tiles(d, at, n, own), tiles(d, at, n, far), other) for d in (0, 1)] for at, n in chunks]
    y_aux = [remote(aux.at[:, side], A.at[:, pl.ds(0, PML), pl.ds(0, cols), far], other)]
    yx_aux = [remote(halo_aux.at[d, :, :, :, own], halo_aux.at[d, :, :, :, far], other) for d in (0, 1)]
    y_mat = [remote(mat.at[pl.ds(0, cols), own], mat.at[pl.ds(0, cols), far], other)]
    yx_mat = [remote(halo_mat.at[d, :, own], halo_mat.at[d, :, far], other) for d in (0, 1)]

    def z_copies(sender, lanes):
        z_numbered[0] = 0
        sent, passed = [], []
        for k in range(half // SPAN):
            sent.append([
                z_remote(r.at[:, pl.ds(k * SPAN, SPAN)], fields(lo, half + k * SPAN, SPAN, cols, lanes), sender)
                for lo, r in args
            ])
            at, n = chunks[k]
            passed.append([z_remote(tiles(d, at, n, own), tiles(d, pairs + at, n, lanes), sender) for d in (0, 1)])
        return sent, passed

    z_own, z_passed = z_copies(gy, z_lanes)
    z_from = [z_copies(0, far), z_copies(1, own)]

    when(has_pred, each(z_own[0], "start"))

    def pack_pair(q, carry):
        for c in range(6):
            pack[0, q, c, 0:COLS] = own_fields[c, 2 * q, 0:COLS]
            pack[0, q, c, COLS:] = own_fields[c, 2 * q + 1, 0:COLS]
            pack[1, q, c, 0:COLS] = own_fields[c, 2 * q + 1, cols - COLS : cols]
            pack[1, q, c, COLS:] = own_fields[c, 2 * q, cols - COLS : cols]
        return carry

    def pack_aux_pair(q, carry):
        for c in range(4):
            pack_aux[0, q, c, 0:COLS] = A[c, 2 * q, 0:COLS, 0:rows]
            pack_aux[0, q, c, COLS:] = A[c, 2 * q + 1, 0:COLS, 0:rows]
            pack_aux[1, q, c, 0:COLS] = A[c, 2 * q + 1, cols - COLS : cols, 0:rows]
            pack_aux[1, q, c, COLS:] = A[c, 2 * q, cols - COLS : cols, 0:rows]
        return carry

    def send_aux():
        load_aux.wait()
        lax.fori_loop(0, PML // 2, pack_aux_pair, 0)
        each(x_aux + y_aux, "start")()

    load_mat.wait()
    m = (mat_own[...] == 1).astype(jnp.float32)
    mat[0:cols, 0:rows] = m
    pack_mat[0] = m[0 : 2 * COLS]
    pack_mat[1] = m[cols - 2 * COLS : cols]
    each(x_mat + y_mat, "start")()
    when(at_front, send_aux)
    for k, (at, n) in enumerate(chunks):
        if k == 0:
            each(stage_low, "wait")()
        if 2 * at == half:
            when(at_back, send_aux)
            each(stage_high, "wait")()
        lax.fori_loop(at, at + n, pack_pair, 0)
        each(x_halo[k], "start")()
        if k == 0:
            when(high_part, each(y_low, "start"))
            each(y_high, "start")()

    def clear(lo, n):
        def plane(a, carry):
            for c in range(6):
                F[c, a] = jnp.zeros((wide, 2 * rows), jnp.float32)
            return carry

        lax.fori_loop(lo, lo + n, plane, 0)

    clear(0, PAD)
    when(jnp.logical_and(at_back, high_part), lambda: clear(PAD + half, half))

    def joined(r, l):
        low = lax.broadcasted_iota(jnp.int32, (2 * COLS, 2 * rows), 0) < COLS
        return jnp.where(low, r, l), pltpu.roll(jnp.where(low, l, r), COLS, 0)

    def unpack(q, carry):
        at = PAD + 2 * q - start
        for c in range(6):
            F[c, at, cols:wide], F[c, at + 1, cols:wide] = joined(halo[0, q, c], halo[1, q, c])
        return carry

    def unpack_aux(q, carry):
        for c in range(4):
            A[c, 2 * q, cols:wide], A[c, 2 * q + 1, cols:wide] = joined(halo_aux[0, q, c], halo_aux[1, q, c])
        return carry

    nx, ny = wide - 1, 2 * rows - 1

    def group(a, s, shift, absorbing):
        E = [[F[c, a + i] for c in range(3)] for i in range(GROUP + 1)]
        H = [[F[c, a + i] for c in range(3, 6)] for i in range(GROUP)]
        before = F[3, a - 1], F[4, a - 1]
        rates = []
        states = []
        if absorbing:
            for i in range(GROUP):
                k = a + i - shift
                inside = jnp.logical_and(k >= 0, k < PML)
                at = jnp.where(inside, k, PML)
                m = jnp.where(at_front, PML - 1 - k, k)
                b = jnp.float32(DEPTH_RATES[0])
                for j in range(1, PML):
                    b = jnp.where(m == j, jnp.float32(DEPTH_RATES[j]), b)
                rates.append((inside, at, b))
                states.append([A[c, at] for c in range(4)])

        new_states = []

        def absorb(c, i, g):
            if not absorbing:
                return g
            inside, at, b = rates[i]
            g_new = jnp.where(inside, b * (g + states[i][c]), g)
            new_states.append((c, at, g_new - g))
            return g_new

        new_h = []
        for i in range(GROUP):
            ex, ey, ez = E[i]
            slope_y = absorb(0, i, E[i + 1][1] - ey)
            slope_x = absorb(1, i, E[i + 1][0] - ex)
            hx = H[i][0] - courant * ((pltpu.roll(ez, ny, 1) - ez) - slope_y)
            hy = H[i][1] - courant * (slope_x - (pltpu.roll(ez, nx, 0) - ez))
            hz = H[i][2] - courant * ((pltpu.roll(ey, nx, 0) - ey) - (pltpu.roll(ex, ny, 1) - ex))
            new_h.append((hx, hy, hz))
        new_e = []
        for i in range(GROUP):
            ex, ey, ez = E[i]
            hx, hy, hz = new_h[i]
            below = before if i == 0 else new_h[i - 1]
            factor = courant / (eps_ref[...] + kap_ref[...] * (ex * ex + ey * ey + ez * ez))
            slope_hy = absorb(2, i, hy - below[1])
            slope_hx = absorb(3, i, hx - below[0])
            new_e.append((
                ex + factor * ((hz - pltpu.roll(hz, 1, 1)) - slope_hy),
                ey + factor * (slope_hx - (hz - pltpu.roll(hz, 1, 0))),
                ez + factor * ((hy - pltpu.roll(hy, 1, 0)) - (hx - pltpu.roll(hx, 1, 1))),
            ))
        for i in range(GROUP):
            for c in range(3):
                F[c, a + i] = new_e[i][c]
                F[3 + c, a + i] = new_h[i][c]
        for c, at, value in new_states:
            A[c, at] = value

    def sweep(s, lo):
        shift = PAD + s + jnp.where(at_front, 0, planes - PML) - start
        a = PAD + lo
        inside = jnp.logical_and(at_edge, jnp.logical_and(a + GROUP > shift, a < shift + PML))
        when(inside, lambda: group(a, s, shift, True))
        when(jnp.logical_not(inside), lambda: group(a, s, shift, False))

        @pl.when(jnp.logical_and(at_back, high_part))
        def _():
            def plane(p, carry):
                for c in range(3):
                    F[c, p] = jnp.zeros((wide, 2 * rows), jnp.float32)
                return carry

            lax.fori_loop(jnp.maximum(a, PAD + half + s), a + GROUP, plane, 0)

    def arrive(k):
        each(x_halo[k], "wait")()
        if k < half // SPAN:
            when(has_pred, each(z_passed[k], "start"))
            if k + 1 < half // SPAN:
                when(has_pred, each(z_own[k + 1], "start"))
            when(high_part, each(yx[k], "start"))
        else:
            each(yx[k], "start")()

    def pass_aux():
        each(x_aux, "wait")()
        each(yx_aux, "start")()

    def take_aux():
        each(y_aux + yx_aux, "wait")()
        lax.fori_loop(0, PML // 2, unpack_aux, 0)

    n_half = half // SPAN
    back_low = jnp.logical_and(at_back, low_part)
    back_high = jnp.logical_and(at_back, high_part)

    each(x_mat, "wait")()
    each(yx_mat, "start")()
    when(at_front, pass_aux)

    @pl.when(high_part)
    def _():
        for k in range(n_half):
            arrive(k)

    when(back_high, pass_aux)
    each(y_mat + yx_mat, "wait")()
    low = lax.broadcasted_iota(jnp.int32, (2 * COLS, 2 * rows), 0) < COLS
    mat[cols:wide] = jnp.where(low, halo_mat[0], halo_mat[1])
    core = mat[...] > 0.5
    eps_ref[...] = jnp.where(core, jnp.float32(eps_core), jnp.float32(eps_clad))
    kap_ref[...] = jnp.where(core, kerr_ref[1], kerr_ref[0])

    results = ((0, elec_out), (3, magn_out))
    store, hand = [], []
    for t in range(n_half):
        there = [r.at[:, pl.ds(start + t * SPAN, SPAN)] for _, r in results]
        store.append([local(fields(lo, STEPS + t * SPAN, SPAN, cols, own), r) for (lo, _), r in zip(results, there)])
        hand.append([remote(fields(lo, STEPS + t * SPAN, SPAN, cols, far), r, other) for (lo, _), r in zip(results, there)])

    def prepare(j):
        @pl.when(low_part)
        def _():
            if j == 0:
                each(load_low, "wait")()
            if j == n_half:
                each(load_high, "wait")()
                when(at_back, pass_aux)
            arrive(j)
            if j == 0:
                each(y_low, "wait_recv")()
                when(at_front, take_aux)
            if j == n_half:
                each(y_high, "wait_recv")()
                when(at_back, take_aux)
            each(yx[j], "wait_recv")()

        if j < n_half:
            @pl.when(high_part)
            def _():
                if j == 0:
                    each(load_high, "wait")()
                arrive(j + n_half)
                if j == 0:
                    each(y_high, "wait_recv")()
                    when(at_edge, take_aux)
                each(yx[j + n_half], "wait_recv")()
        else:
            @pl.when(takes_z)
            def _():
                for sent, passed in z_from:
                    each(sent[j - n_half] + passed[j - n_half], "wait_recv")()

    def stage(j, carry):
        for k in range(2 * n_half):
            when(j == k, functools.partial(prepare, k))

        @pl.when(jnp.logical_not(jnp.logical_and(back_high, j >= n_half)))
        def _():
            at = quads * gy + PAIRS * j
            lax.fori_loop(at, at + PAIRS, unpack, 0)

        def step(s, carry):
            sweep(s, SPAN * j - 1 - s)
            return carry

        lax.fori_loop(0, jnp.where(j == 0, STEPS // 2, STEPS), step, 0)
        for t in range(n_half):
            when(j == t + n_half, each(hand[t] + store[t], "start"))
        return carry

    lax.fori_loop(0, 2 * n_half, stage, 0)

    @pl.when(has_pred)
    def _():
        for k in range(n_half):
            each(z_own[k] + z_passed[k], "wait_send")()

    @pl.when(high_part)
    def _():
        each(y_low, "wait_send")()
        for k in range(n_half):
            each(yx[k], "wait_send")()

    each(y_high, "wait_send")()
    for k in range(n_half, 2 * n_half):
        each(yx[k], "wait_send")()
    for t in range(n_half):
        each(hand[t] + store[t], "wait")()


def write_out(e_ref, h_ref, elec_out, magn_out, sem):
    copies = [
        pltpu.make_async_copy(src.at[c], dst.at[c], sem.at[i, c])
        for i, (src, dst) in enumerate(((e_ref, elec_out), (h_ref, magn_out)))
        for c in range(3)
    ]
    for copy in copies:
        copy.start()
    for copy in copies:
        copy.wait()


def shards(sizes, electric, magnetic, aux_state, material, kerr_strength):
    _, planes, cols, rows = electric.shape
    wide, deep = cols + 2 * COLS, planes + HALO
    f32 = jnp.float32
    any_space = pl.BlockSpec(memory_space=pl.ANY)
    hbm = pl.BlockSpec(memory_space=pltpu.HBM)
    shape = jax.ShapeDtypeStruct(electric.shape, f32)
    fields = pl.pallas_call(
        functools.partial(kernel, sizes),
        out_shape=(shape, shape),
        in_specs=[pl.BlockSpec(memory_space=pltpu.SMEM), hbm, hbm, hbm, hbm],
        out_specs=(any_space, any_space),
        scratch_shapes=[
            pltpu.VMEM((6, PAD + planes, wide, 2 * rows), f32),
            pltpu.VMEM((4, PML + 1, wide, 2 * rows), f32),
            pltpu.VMEM((wide, 2 * rows), f32),
            pltpu.VMEM((wide, 2 * rows), f32),
            pltpu.VMEM((wide, 2 * rows), f32),
            pltpu.VMEM((cols, rows), jnp.int32),
            pltpu.VMEM((6, planes, cols, rows), f32),
            pltpu.VMEM((2, planes // 2, 6, 2 * COLS, rows), f32),
            pltpu.VMEM((2, PML // 2, 4, 2 * COLS, rows), f32),
            pltpu.VMEM((2, 2 * COLS, rows), f32),
            pltpu.VMEM((2, deep // 2, 6, 2 * COLS, 2 * rows), f32),
            pltpu.VMEM((2, PML // 2, 4, 2 * COLS, 2 * rows), f32),
            pltpu.VMEM((2, 2 * COLS, 2 * rows), f32),
            pltpu.SemaphoreType.DMA((16,)),
            pltpu.SemaphoreType.DMA((40,)),
            pltpu.SemaphoreType.DMA((40,)),
            pltpu.SemaphoreType.DMA((8,)),
            pltpu.SemaphoreType.DMA((8, 2)),
        ],
        compiler_params=pltpu.CompilerParams(
            collective_id=0, has_side_effects=True, vmem_limit_bytes=60 * 2**20
        ),
    )(kerr_strength, electric, magnetic, aux_state, material)
    return pl.pallas_call(
        write_out,
        out_shape=(shape, shape),
        in_specs=[any_space, any_space],
        out_specs=(hbm, hbm),
        scratch_shapes=[pltpu.SemaphoreType.DMA((2, 3))],
    )(*fields)


def solution(mesh):
    sizes = tuple(mesh.shape[axis] for axis in ("gz", "gx", "gy"))
    in_specs = (
        P(None, "gz", "gx", "gy"),
        P(None, "gz", "gx", "gy"),
        P(None, None, None, "gx", "gy"),
        P("gx", "gy"),
        P(),
    )
    out_specs = (P(None, "gz", "gx", "gy"), P(None, "gz", "gx", "gy"))
    return jax.shard_map(
        functools.partial(shards, sizes),
        mesh=mesh, in_specs=in_specs, out_specs=out_specs, check_vma=False,
    )
```

```python
import functools

import jax
import jax.numpy as jnp
import numpy as np
from jax import lax
from jax.experimental import pallas as pl
from jax.experimental.pallas import tpu as pltpu
from jax.sharding import PartitionSpec as P

PML = 8
STEPS = 4
HALO = 2 * STEPS
COLS = STEPS
PAD = 4
GROUP = SPAN = 4
PAIRS = SPAN // 2

courant = 0.5
pml_rate = 3.0
eps_clad = 2.085
eps_core = 4.0

MESH = pl.DeviceIdType.MESH
DEPTH_RATES = [
    float(np.exp(np.float32(-pml_rate) * np.float32((m + 1) / PML) ** 3)) for m in range(PML)
]


def kernel(
    sizes,
    kerr_ref, elec, magn, aux, material,
    elec_out, magn_out,
    F, A, eps_ref, kap_ref, mat, mat_own, own_fields,
    pack, pack_aux, pack_mat,
    halo, halo_aux, halo_mat,
    local_sem, send_sem, recv_sem, z_send_sem, z_recv_sem,
):
    n_gz, n_gx, n_gy = sizes
    planes, cols, rows = elec.shape[1:]
    wide = cols + 2 * COLS
    half = planes // 2
    quads = half // 2
    pairs = planes // 2
    gz, gx, gy = lax.axis_index("gz"), lax.axis_index("gx"), lax.axis_index("gy")
    low_part, high_part = gy == 0, gy == 1
    has_pred = gz > 0
    takes_z = jnp.logical_and(high_part, gz < n_gz - 1)
    at_front, at_back = gz == 0, gz == n_gz - 1
    at_edge = jnp.logical_or(at_front, at_back)
    left = {"gx": lax.rem(gx + n_gx - 1, n_gx)}
    right = {"gx": lax.rem(gx + 1, n_gx)}
    other = {"gy": 1 - gy}
    pred = {"gz": jnp.maximum(gz - 1, 0), "gy": 1}
    succ = [{"gz": jnp.minimum(gz + 1, n_gz - 1), "gy": part} for part in (0, 1)]
    own, far = pl.ds(0, rows), pl.ds(rows, rows)
    z_lanes = pl.ds(pl.multiple_of((1 - gy) * rows, rows), rows)
    start = half * gy
    side = jnp.where(at_front, 0, 1)
    args = ((0, elec), (3, magn))

    def fields(lo, at, n, width, lanes):
        return F.at[pl.ds(lo, 3), pl.ds(PAD + at, n), pl.ds(0, width), lanes]

    def when(condition, work):
        pl.when(condition)(work)

    def each(copies, method):
        def work():
            for copy in copies:
                getattr(copy, method)()

        return work

    count = [0]

    def local(src, dst):
        count[0] += 1
        return pltpu.make_async_copy(src, dst, local_sem.at[count[0] - 1])

    stage_low = [local(r.at[:, pl.ds(0, half)], own_fields.at[pl.ds(lo, 3), pl.ds(0, half)]) for lo, r in args]
    stage_high = [local(r.at[:, pl.ds(half, half)], own_fields.at[pl.ds(lo, 3), pl.ds(half, half)]) for lo, r in args]
    load_mat = local(material, mat_own)
    load_aux = local(aux.at[:, side], A.at[:, pl.ds(0, PML), pl.ds(0, cols), own])
    load_low = [local(r.at[:, pl.ds(0, half)], fields(lo, 0, half, cols, own)) for lo, r in args]
    load_high = [local(r.at[:, pl.ds(half, half)], fields(lo, half - start, half, cols, own)) for lo, r in args]
    for copy in stage_low + stage_high + [load_mat]:
        copy.start()
    when(at_edge, each([load_aux], "start"))
    when(low_part, each(load_low, "start"))
    each(load_high, "start")()

    barrier = pltpu.get_barrier_semaphore()

    def greet(peers):
        def work():
            for peer in peers:
                pl.semaphore_signal(barrier, inc=1, device_id=peer, device_id_type=MESH)

        return work

    greet([left, right, other])()
    when(has_pred, greet([pred]))
    when(takes_z, greet(succ))

    numbered = [0]

    def remote(src, dst, peer):
        at = numbered[0]
        numbered[0] += 1
        return pltpu.make_async_remote_copy(
            src_ref=src, dst_ref=dst, send_sem=send_sem.at[at], recv_sem=recv_sem.at[at],
            device_id=peer, device_id_type=MESH,
        )

    z_numbered = [0]

    def z_remote(src, dst, sender):
        at = z_numbered[0]
        z_numbered[0] += 1
        return pltpu.make_async_remote_copy(
            src_ref=src, dst_ref=dst, send_sem=z_send_sem.at[at], recv_sem=z_recv_sem.at[at, sender],
            device_id=pred, device_id_type=MESH,
        )

    def staged(lo, at, n):
        return own_fields.at[pl.ds(lo, 3), pl.ds(at, n)]

    def tiles(d, at, n, lanes):
        return halo.at[d, pl.ds(at, n), :, :, lanes]

    both = ((0, left), (1, right))
    chunks = [(k * PAIRS, PAIRS) for k in range(pairs // PAIRS)]
    x_halo = [[remote(pack.at[d, pl.ds(at, n)], tiles(d, at, n, own), p) for d, p in both] for at, n in chunks]
    x_mat = [remote(pack_mat.at[d], halo_mat.at[d, :, own], p) for d, p in both]
    x_aux = [remote(pack_aux.at[d], halo_aux.at[d, :, :, :, own], p) for d, p in both]
    y_low = [remote(staged(lo, 0, half), fields(lo, 0, half, cols, far), other) for lo, r in args]
    y_high = [remote(staged(lo, half, half), fields(lo, start, half, cols, far), other) for lo, r in args]
    yx = [[remote(tiles(d, at, n, own), tiles(d, at, n, far), other) for d in (0, 1)] for at, n in chunks]
    y_aux = [remote(A.at[:, pl.ds(0, PML), pl.ds(0, cols), own], A.at[:, pl.ds(0, PML), pl.ds(0, cols), far], other)]
    yx_aux = [remote(halo_aux.at[d, :, :, :, own], halo_aux.at[d, :, :, :, far], other) for d in (0, 1)]
    y_mat = [remote(mat.at[pl.ds(0, cols), own], mat.at[pl.ds(0, cols), far], other)]
    yx_mat = [remote(halo_mat.at[d, :, own], halo_mat.at[d, :, far], other) for d in (0, 1)]

    def z_copies(sender, lanes):
        z_numbered[0] = 0
        sent, passed = [], []
        for k in range(half // SPAN):
            sent.append([
                z_remote(staged(lo, k * SPAN, SPAN), fields(lo, half + k * SPAN, SPAN, cols, lanes), sender)
                for lo, r in args
            ])
            at, n = chunks[k]
            passed.append([z_remote(tiles(d, at, n, own), tiles(d, pairs + at, n, lanes), sender) for d in (0, 1)])
        return sent, passed

    z_own, z_passed = z_copies(gy, z_lanes)
    z_from = [z_copies(0, far), z_copies(1, own)]

    def pack_pair(q, carry):
        for c in range(6):
            pack[0, q, c, 0:COLS] = own_fields[c, 2 * q, 0:COLS]
            pack[0, q, c, COLS:] = own_fields[c, 2 * q + 1, 0:COLS]
            pack[1, q, c, 0:COLS] = own_fields[c, 2 * q + 1, cols - COLS : cols]
            pack[1, q, c, COLS:] = own_fields[c, 2 * q, cols - COLS : cols]
        return carry

    def pack_aux_pair(q, carry):
        for c in range(4):
            pack_aux[0, q, c, 0:COLS] = A[c, 2 * q, 0:COLS, 0:rows]
            pack_aux[0, q, c, COLS:] = A[c, 2 * q + 1, 0:COLS, 0:rows]
            pack_aux[1, q, c, 0:COLS] = A[c, 2 * q + 1, cols - COLS : cols, 0:rows]
            pack_aux[1, q, c, COLS:] = A[c, 2 * q, cols - COLS : cols, 0:rows]
        return carry

    load_mat.wait()
    m = (mat_own[...] == 1).astype(jnp.float32)
    mat[0:cols, 0:rows] = m
    pack_mat[0] = m[0 : 2 * COLS]
    pack_mat[1] = m[cols - 2 * COLS : cols]
    each(stage_low, "wait")()
    lax.fori_loop(0, quads, pack_pair, 0)
    each(stage_high, "wait")()
    lax.fori_loop(quads, pairs, pack_pair, 0)

    @pl.when(at_edge)
    def _():
        load_aux.wait()
        lax.fori_loop(0, PML // 2, pack_aux_pair, 0)

    pl.semaphore_wait(barrier, 3 + has_pred.astype(jnp.int32) + 2 * takes_z.astype(jnp.int32))

    when(has_pred, each(z_own[0], "start"))
    each(x_mat + y_mat, "start")()
    when(at_front, each(x_aux + y_aux, "start"))
    for k, (at, n) in enumerate(chunks):
        if 2 * at == half:
            when(at_back, each(x_aux + y_aux, "start"))
        each(x_halo[k], "start")()
        if k == 0:
            when(high_part, each(y_low, "start"))
            each(y_high, "start")()

    def clear(lo, n):
        def plane(a, carry):
            for c in range(6):
                F[c, a] = jnp.zeros((wide, 2 * rows), jnp.float32)
            return carry

        lax.fori_loop(lo, lo + n, plane, 0)

    clear(0, PAD)
    when(jnp.logical_and(at_back, high_part), lambda: clear(PAD + half, half))

    def joined(r, l):
        low = lax.broadcasted_iota(jnp.int32, (2 * COLS, 2 * rows), 0) < COLS
        return jnp.where(low, r, l), pltpu.roll(jnp.where(low, l, r), COLS, 0)

    def unpack(q, carry):
        at = PAD + 2 * q - start
        for c in range(6):
            F[c, at, cols:wide], F[c, at + 1, cols:wide] = joined(halo[0, q, c], halo[1, q, c])
        return carry

    def unpack_aux(q, carry):
        for c in range(4):
            A[c, 2 * q, cols:wide], A[c, 2 * q + 1, cols:wide] = joined(halo_aux[0, q, c], halo_aux[1, q, c])
        return carry

    nx, ny = wide - 1, 2 * rows - 1

    def group(a, s, shift, absorbing):
        E = [[F[c, a + i] for c in range(3)] for i in range(GROUP + 1)]
        H = [[F[c, a + i] for c in range(3, 6)] for i in range(GROUP)]
        before = F[3, a - 1], F[4, a - 1]
        rates = []
        states = []
        if absorbing:
            for i in range(GROUP):
                k = a + i - shift
                inside = jnp.logical_and(k >= 0, k < PML)
                at = jnp.where(inside, k, PML)
                m = jnp.where(at_front, PML - 1 - k, k)
                b = jnp.float32(DEPTH_RATES[0])
                for j in range(1, PML):
                    b = jnp.where(m == j, jnp.float32(DEPTH_RATES[j]), b)
                rates.append((inside, at, b))
                states.append([A[c, at] for c in range(4)])

        new_states = []

        def absorb(c, i, g):
            if not absorbing:
                return g
            inside, at, b = rates[i]
            g_new = jnp.where(inside, b * (g + states[i][c]), g)
            new_states.append((c, at, g_new - g))
            return g_new

        new_h = []
        for i in range(GROUP):
            ex, ey, ez = E[i]
            slope_y = absorb(0, i, E[i + 1][1] - ey)
            slope_x = absorb(1, i, E[i + 1][0] - ex)
            hx = H[i][0] - courant * ((pltpu.roll(ez, ny, 1) - ez) - slope_y)
            hy = H[i][1] - courant * (slope_x - (pltpu.roll(ez, nx, 0) - ez))
            hz = H[i][2] - courant * ((pltpu.roll(ey, nx, 0) - ey) - (pltpu.roll(ex, ny, 1) - ex))
            new_h.append((hx, hy, hz))
        new_e = []
        for i in range(GROUP):
            ex, ey, ez = E[i]
            hx, hy, hz = new_h[i]
            below = before if i == 0 else new_h[i - 1]
            factor = courant / (eps_ref[...] + kap_ref[...] * (ex * ex + ey * ey + ez * ez))
            slope_hy = absorb(2, i, hy - below[1])
            slope_hx = absorb(3, i, hx - below[0])
            new_e.append((
                ex + factor * ((hz - pltpu.roll(hz, 1, 1)) - slope_hy),
                ey + factor * (slope_hx - (hz - pltpu.roll(hz, 1, 0))),
                ez + factor * ((hy - pltpu.roll(hy, 1, 0)) - (hx - pltpu.roll(hx, 1, 1))),
            ))
        for i in range(GROUP):
            for c in range(3):
                F[c, a + i] = new_e[i][c]
                F[3 + c, a + i] = new_h[i][c]
        for c, at, value in new_states:
            A[c, at] = value

    def sweep(s, lo):
        shift = PAD + s + jnp.where(at_front, 0, planes - PML) - start
        a = PAD + lo
        inside = jnp.logical_and(at_edge, jnp.logical_and(a + GROUP > shift, a < shift + PML))
        when(inside, lambda: group(a, s, shift, True))
        when(jnp.logical_not(inside), lambda: group(a, s, shift, False))

        @pl.when(jnp.logical_and(at_back, high_part))
        def _():
            def plane(p, carry):
                for c in range(3):
                    F[c, p] = jnp.zeros((wide, 2 * rows), jnp.float32)
                return carry

            lax.fori_loop(jnp.maximum(a, PAD + half + s), a + GROUP, plane, 0)

    def arrive(k):
        each(x_halo[k], "wait")()
        if k < half // SPAN:
            when(has_pred, each(z_passed[k], "start"))
            if k + 1 < half // SPAN:
                when(has_pred, each(z_own[k + 1], "start"))
            when(high_part, each(yx[k], "start"))
        else:
            each(yx[k], "start")()

    def pass_aux():
        each(x_aux, "wait")()
        each(yx_aux, "start")()

    def take_aux():
        each(y_aux + yx_aux, "wait")()
        lax.fori_loop(0, PML // 2, unpack_aux, 0)

    n_half = half // SPAN
    back_low = jnp.logical_and(at_back, low_part)
    back_high = jnp.logical_and(at_back, high_part)

    each(x_mat, "wait")()
    each(yx_mat, "start")()
    when(at_front, pass_aux)

    @pl.when(high_part)
    def _():
        for k in range(n_half):
            arrive(k)

    when(back_high, pass_aux)
    each(y_mat + yx_mat, "wait")()
    low = lax.broadcasted_iota(jnp.int32, (2 * COLS, 2 * rows), 0) < COLS
    mat[cols:wide] = jnp.where(low, halo_mat[0], halo_mat[1])
    core = mat[...] > 0.5
    eps_ref[...] = jnp.where(core, jnp.float32(eps_core), jnp.float32(eps_clad))
    kap_ref[...] = jnp.where(core, kerr_ref[1], kerr_ref[0])

    results = ((0, elec_out), (3, magn_out))
    store, hand = [], []
    for t in range(n_half):
        there = [r.at[:, pl.ds(start + t * SPAN, SPAN)] for _, r in results]
        store.append([local(fields(lo, STEPS + t * SPAN, SPAN, cols, own), r) for (lo, _), r in zip(results, there)])
        hand.append([remote(fields(lo, STEPS + t * SPAN, SPAN, cols, far), r, other) for (lo, _), r in zip(results, there)])

    def prepare(j):
        @pl.when(low_part)
        def _():
            if j == 0:
                each(load_low, "wait")()
            if j == n_half:
                each(load_high, "wait")()
                when(at_back, pass_aux)
            arrive(j)
            if j == 0:
                each(y_low, "wait_recv")()
                when(at_front, take_aux)
            if j == n_half:
                each(y_high, "wait_recv")()
                when(at_back, take_aux)
            each(yx[j], "wait_recv")()

        if j < n_half:
            @pl.when(high_part)
            def _():
                if j == 0:
                    each(load_high, "wait")()
                arrive(j + n_half)
                if j == 0:
                    each(y_high, "wait_recv")()
                    when(at_edge, take_aux)
                each(yx[j + n_half], "wait_recv")()
        else:
            @pl.when(takes_z)
            def _():
                for sent, passed in z_from:
                    each(sent[j - n_half] + passed[j - n_half], "wait_recv")()

    def stage(j, carry):
        for k in range(2 * n_half):
            when(j == k, functools.partial(prepare, k))

        @pl.when(jnp.logical_not(jnp.logical_and(back_high, j >= n_half)))
        def _():
            at = quads * gy + PAIRS * j
            lax.fori_loop(at, at + PAIRS, unpack, 0)

        def step(s, carry):
            sweep(s, SPAN * j - 1 - s)
            return carry

        lax.fori_loop(0, jnp.where(j == 0, STEPS // 2, STEPS), step, 0)
        for t in range(n_half):
            when(j == t + n_half, each(hand[t] + store[t], "start"))
        return carry

    lax.fori_loop(0, 2 * n_half, stage, 0)

    @pl.when(has_pred)
    def _():
        for k in range(n_half):
            each(z_own[k] + z_passed[k], "wait_send")()

    @pl.when(high_part)
    def _():
        each(y_low, "wait_send")()
        for k in range(n_half):
            each(yx[k], "wait_send")()

    each(y_high, "wait_send")()
    for k in range(n_half, 2 * n_half):
        each(yx[k], "wait_send")()
    for t in range(n_half):
        each(hand[t] + store[t], "wait")()


def write_out(e_ref, h_ref, elec_out, magn_out, held, in_sem, out_sem):
    refs = ((e_ref, elec_out), (h_ref, magn_out))
    parts = [(i, c) for i in range(2) for c in range(3)]
    into = [pltpu.make_async_copy(refs[i][0].at[c], held.at[i, c], in_sem.at[i, c]) for i, c in parts]
    back = [pltpu.make_async_copy(held.at[i, c], refs[i][1].at[c], out_sem.at[i, c]) for i, c in parts]
    for copy in into:
        copy.start()
    for first, second in zip(into, back):
        first.wait()
        second.start()
    for copy in back:
        copy.wait()


def shards(sizes, electric, magnetic, aux_state, material, kerr_strength):
    _, planes, cols, rows = electric.shape
    wide, deep = cols + 2 * COLS, planes + HALO
    f32 = jnp.float32
    any_space = pl.BlockSpec(memory_space=pl.ANY)
    hbm = pl.BlockSpec(memory_space=pltpu.HBM)
    shape = jax.ShapeDtypeStruct(electric.shape, f32)
    fields = pl.pallas_call(
        functools.partial(kernel, sizes),
        out_shape=(shape, shape),
        in_specs=[pl.BlockSpec(memory_space=pltpu.SMEM), hbm, hbm, hbm, hbm],
        out_specs=(any_space, any_space),
        scratch_shapes=[
            pltpu.VMEM((6, PAD + planes, wide, 2 * rows), f32),
            pltpu.VMEM((4, PML + 1, wide, 2 * rows), f32),
            pltpu.VMEM((wide, 2 * rows), f32),
            pltpu.VMEM((wide, 2 * rows), f32),
            pltpu.VMEM((wide, 2 * rows), f32),
            pltpu.VMEM((cols, rows), jnp.int32),
            pltpu.VMEM((6, planes, cols, rows), f32),
            pltpu.VMEM((2, planes // 2, 6, 2 * COLS, rows), f32),
            pltpu.VMEM((2, PML // 2, 4, 2 * COLS, rows), f32),
            pltpu.VMEM((2, 2 * COLS, rows), f32),
            pltpu.VMEM((2, deep // 2, 6, 2 * COLS, 2 * rows), f32),
            pltpu.VMEM((2, PML // 2, 4, 2 * COLS, 2 * rows), f32),
            pltpu.VMEM((2, 2 * COLS, 2 * rows), f32),
            pltpu.SemaphoreType.DMA((16,)),
            pltpu.SemaphoreType.DMA((40,)),
            pltpu.SemaphoreType.DMA((40,)),
            pltpu.SemaphoreType.DMA((8,)),
            pltpu.SemaphoreType.DMA((8, 2)),
        ],
        compiler_params=pltpu.CompilerParams(
            collective_id=0, has_side_effects=True, vmem_limit_bytes=60 * 2**20
        ),
    )(kerr_strength, electric, magnetic, aux_state, material)
    return pl.pallas_call(
        write_out,
        out_shape=(shape, shape),
        in_specs=[any_space, any_space],
        out_specs=(hbm, hbm),
        scratch_shapes=[
            pltpu.VMEM((2,) + electric.shape, f32),
            pltpu.SemaphoreType.DMA((2, 3)),
            pltpu.SemaphoreType.DMA((2, 3)),
        ],
        compiler_params=pltpu.CompilerParams(vmem_limit_bytes=60 * 2**20),
    )(*fields)


def solution(mesh):
    sizes = tuple(mesh.shape[axis] for axis in ("gz", "gx", "gy"))
    in_specs = (
        P(None, "gz", "gx", "gy"),
        P(None, "gz", "gx", "gy"),
        P(None, None, None, "gx", "gy"),
        P("gx", "gy"),
        P(),
    )
    out_specs = (P(None, "gz", "gx", "gy"), P(None, "gz", "gx", "gy"))
    return jax.shard_map(
        functools.partial(shards, sizes),
        mesh=mesh, in_specs=in_specs, out_specs=out_specs, check_vma=False,
    )
```

```python
import functools

import jax
import jax.numpy as jnp
import numpy as np
from jax import lax
from jax.experimental import pallas as pl
from jax.experimental.pallas import tpu as pltpu
from jax.sharding import PartitionSpec as P

PML = 8
STEPS = 4
HALO = 2 * STEPS
COLS = STEPS
PAD = 4
GROUP = 2
SPAN = 4
PAIRS = SPAN // 2

courant = 0.5
pml_rate = 3.0
eps_clad = 2.085
eps_core = 4.0

MESH = pl.DeviceIdType.MESH
DEPTH_RATES = [
    float(np.exp(np.float32(-pml_rate) * np.float32((m + 1) / PML) ** 3)) for m in range(PML)
]


def kernel(
    sizes,
    kerr_ref, elec, magn, aux, material,
    elec_out, magn_out,
    F, A, eps_ref, kap_ref, mat, mat_own, own_fields,
    pack, pack_aux, pack_mat,
    halo, halo_aux, halo_mat,
    local_sem, send_sem, recv_sem, z_send_sem, z_recv_sem,
):
    n_gz, n_gx, n_gy = sizes
    planes, cols, rows = elec.shape[1:]
    wide = cols + 2 * COLS
    half = planes // 2
    quads = half // 2
    pairs = planes // 2
    gz, gx, gy = lax.axis_index("gz"), lax.axis_index("gx"), lax.axis_index("gy")
    low_part, high_part = gy == 0, gy == 1
    has_pred = gz > 0
    takes_z = jnp.logical_and(high_part, gz < n_gz - 1)
    at_front, at_back = gz == 0, gz == n_gz - 1
    at_edge = jnp.logical_or(at_front, at_back)
    left = {"gx": lax.rem(gx + n_gx - 1, n_gx)}
    right = {"gx": lax.rem(gx + 1, n_gx)}
    other = {"gy": 1 - gy}
    pred = {"gz": jnp.maximum(gz - 1, 0), "gy": 1}
    succ = [{"gz": jnp.minimum(gz + 1, n_gz - 1), "gy": part} for part in (0, 1)]
    own, far = pl.ds(0, rows), pl.ds(rows, rows)
    z_lanes = pl.ds(pl.multiple_of((1 - gy) * rows, rows), rows)
    start = half * gy
    side = jnp.where(at_front, 0, 1)
    args = ((0, elec), (3, magn))

    def fields(lo, at, n, width, lanes):
        return F.at[pl.ds(lo, 3), pl.ds(PAD + at, n), pl.ds(0, width), lanes]

    def when(condition, work):
        pl.when(condition)(work)

    def each(copies, method):
        def work():
            for copy in copies:
                getattr(copy, method)()

        return work

    count = [0]

    def local(src, dst):
        count[0] += 1
        return pltpu.make_async_copy(src, dst, local_sem.at[count[0] - 1])

    stage_low = [local(r.at[:, pl.ds(0, half)], own_fields.at[pl.ds(lo, 3), pl.ds(0, half)]) for lo, r in args]
    stage_high = [local(r.at[:, pl.ds(half, half)], own_fields.at[pl.ds(lo, 3), pl.ds(half, half)]) for lo, r in args]
    load_mat = local(material, mat_own)
    load_aux = local(aux.at[:, side], A.at[:, pl.ds(0, PML), pl.ds(0, cols), own])
    load_low = [local(r.at[:, pl.ds(0, half)], fields(lo, 0, half, cols, own)) for lo, r in args]
    load_high = [local(r.at[:, pl.ds(half, half)], fields(lo, half - start, half, cols, own)) for lo, r in args]
    for copy in stage_low + stage_high + [load_mat]:
        copy.start()
    when(at_edge, each([load_aux], "start"))
    when(low_part, each(load_low, "start"))
    each(load_high, "start")()

    barrier = pltpu.get_barrier_semaphore()

    def greet(peers):
        def work():
            for peer in peers:
                pl.semaphore_signal(barrier, inc=1, device_id=peer, device_id_type=MESH)

        return work

    greet([left, right, other])()
    when(has_pred, greet([pred]))
    when(takes_z, greet(succ))

    numbered = [0]

    def remote(src, dst, peer):
        at = numbered[0]
        numbered[0] += 1
        return pltpu.make_async_remote_copy(
            src_ref=src, dst_ref=dst, send_sem=send_sem.at[at], recv_sem=recv_sem.at[at],
            device_id=peer, device_id_type=MESH,
        )

    z_numbered = [0]

    def z_remote(src, dst, sender):
        at = z_numbered[0]
        z_numbered[0] += 1
        return pltpu.make_async_remote_copy(
            src_ref=src, dst_ref=dst, send_sem=z_send_sem.at[at], recv_sem=z_recv_sem.at[at, sender],
            device_id=pred, device_id_type=MESH,
        )

    def staged(lo, at, n):
        return own_fields.at[pl.ds(lo, 3), pl.ds(at, n)]

    def tiles(d, at, n, lanes):
        return halo.at[d, pl.ds(at, n), :, :, lanes]

    both = ((0, left), (1, right))
    chunks = [(k * PAIRS, PAIRS) for k in range(pairs // PAIRS)]
    x_halo = [[remote(pack.at[d, pl.ds(at, n)], tiles(d, at, n, own), p) for d, p in both] for at, n in chunks]
    x_mat = [remote(pack_mat.at[d], halo_mat.at[d, :, own], p) for d, p in both]
    x_aux = [remote(pack_aux.at[d], halo_aux.at[d, :, :, :, own], p) for d, p in both]
    y_low = [remote(staged(lo, 0, half), fields(lo, 0, half, cols, far), other) for lo, r in args]
    y_high = [remote(staged(lo, half, half), fields(lo, start, half, cols, far), other) for lo, r in args]
    yx = [[remote(tiles(d, at, n, own), tiles(d, at, n, far), other) for d in (0, 1)] for at, n in chunks]
    y_aux = [remote(A.at[:, pl.ds(0, PML), pl.ds(0, cols), own], A.at[:, pl.ds(0, PML), pl.ds(0, cols), far], other)]
    yx_aux = [remote(halo_aux.at[d, :, :, :, own], halo_aux.at[d, :, :, :, far], other) for d in (0, 1)]
    y_mat = [remote(mat.at[pl.ds(0, cols), own], mat.at[pl.ds(0, cols), far], other)]
    yx_mat = [remote(halo_mat.at[d, :, own], halo_mat.at[d, :, far], other) for d in (0, 1)]

    def z_copies(sender, lanes):
        z_numbered[0] = 0
        sent, passed = [], []
        for k in range(half // SPAN):
            sent.append([
                z_remote(staged(lo, k * SPAN, SPAN), fields(lo, half + k * SPAN, SPAN, cols, lanes), sender)
                for lo, r in args
            ])
            at, n = chunks[k]
            passed.append([z_remote(tiles(d, at, n, own), tiles(d, pairs + at, n, lanes), sender) for d in (0, 1)])
        return sent, passed

    z_own, z_passed = z_copies(gy, z_lanes)
    z_from = [z_copies(0, far), z_copies(1, own)]

    def pack_pair(q, carry):
        for c in range(6):
            pack[0, q, c, 0:COLS] = own_fields[c, 2 * q, 0:COLS]
            pack[0, q, c, COLS:] = own_fields[c, 2 * q + 1, 0:COLS]
            pack[1, q, c, 0:COLS] = own_fields[c, 2 * q + 1, cols - COLS : cols]
            pack[1, q, c, COLS:] = own_fields[c, 2 * q, cols - COLS : cols]
        return carry

    def pack_aux_pair(q, carry):
        for c in range(4):
            pack_aux[0, q, c, 0:COLS] = A[c, 2 * q, 0:COLS, 0:rows]
            pack_aux[0, q, c, COLS:] = A[c, 2 * q + 1, 0:COLS, 0:rows]
            pack_aux[1, q, c, 0:COLS] = A[c, 2 * q + 1, cols - COLS : cols, 0:rows]
            pack_aux[1, q, c, COLS:] = A[c, 2 * q, cols - COLS : cols, 0:rows]
        return carry

    load_mat.wait()
    m = (mat_own[...] == 1).astype(jnp.float32)
    mat[0:cols, 0:rows] = m
    pack_mat[0] = m[0 : 2 * COLS]
    pack_mat[1] = m[cols - 2 * COLS : cols]
    each(stage_low, "wait")()
    lax.fori_loop(0, quads, pack_pair, 0)
    each(stage_high, "wait")()
    lax.fori_loop(quads, pairs, pack_pair, 0)

    @pl.when(at_edge)
    def _():
        load_aux.wait()
        lax.fori_loop(0, PML // 2, pack_aux_pair, 0)

    pl.semaphore_wait(barrier, 3 + has_pred.astype(jnp.int32) + 2 * takes_z.astype(jnp.int32))

    when(has_pred, each(z_own[0], "start"))
    each(x_mat + y_mat, "start")()
    when(at_front, each(x_aux + y_aux, "start"))
    for k, (at, n) in enumerate(chunks):
        if 2 * at == half:
            when(at_back, each(x_aux + y_aux, "start"))
        each(x_halo[k], "start")()
        if k == 0:
            when(high_part, each(y_low, "start"))
            each(y_high, "start")()

    def clear(lo, n):
        def plane(a, carry):
            for c in range(6):
                F[c, a] = jnp.zeros((wide, 2 * rows), jnp.float32)
            return carry

        lax.fori_loop(lo, lo + n, plane, 0)

    clear(0, PAD)
    when(jnp.logical_and(at_back, high_part), lambda: clear(PAD + half, half))

    def joined(r, l):
        low = lax.broadcasted_iota(jnp.int32, (2 * COLS, 2 * rows), 0) < COLS
        return jnp.where(low, r, l), pltpu.roll(jnp.where(low, l, r), COLS, 0)

    def unpack(q, carry):
        at = PAD + 2 * q - start
        for c in range(6):
            F[c, at, cols:wide], F[c, at + 1, cols:wide] = joined(halo[0, q, c], halo[1, q, c])
        return carry

    def unpack_aux(q, carry):
        for c in range(4):
            A[c, 2 * q, cols:wide], A[c, 2 * q + 1, cols:wide] = joined(halo_aux[0, q, c], halo_aux[1, q, c])
        return carry

    nx, ny = wide - 1, 2 * rows - 1

    def group(a, s, shift, absorbing):
        E = [[F[c, a + i] for c in range(3)] for i in range(GROUP + 1)]
        H = [[F[c, a + i] for c in range(3, 6)] for i in range(GROUP)]
        before = F[3, a - 1], F[4, a - 1]
        rates = []
        states = []
        if absorbing:
            for i in range(GROUP):
                k = a + i - shift
                inside = jnp.logical_and(k >= 0, k < PML)
                at = jnp.where(inside, k, PML)
                m = jnp.where(at_front, PML - 1 - k, k)
                b = jnp.float32(DEPTH_RATES[0])
                for j in range(1, PML):
                    b = jnp.where(m == j, jnp.float32(DEPTH_RATES[j]), b)
                rates.append((inside, at, b))
                states.append([A[c, at] for c in range(4)])

        new_states = []

        def absorb(c, i, g):
            if not absorbing:
                return g
            inside, at, b = rates[i]
            g_new = jnp.where(inside, b * (g + states[i][c]), g)
            new_states.append((c, at, g_new - g))
            return g_new

        new_h = []
        for i in range(GROUP):
            ex, ey, ez = E[i]
            slope_y = absorb(0, i, E[i + 1][1] - ey)
            slope_x = absorb(1, i, E[i + 1][0] - ex)
            hx = H[i][0] - courant * ((pltpu.roll(ez, ny, 1) - ez) - slope_y)
            hy = H[i][1] - courant * (slope_x - (pltpu.roll(ez, nx, 0) - ez))
            hz = H[i][2] - courant * ((pltpu.roll(ey, nx, 0) - ey) - (pltpu.roll(ex, ny, 1) - ex))
            new_h.append((hx, hy, hz))
        new_e = []
        for i in range(GROUP):
            ex, ey, ez = E[i]
            hx, hy, hz = new_h[i]
            below = before if i == 0 else new_h[i - 1]
            factor = courant / (eps_ref[...] + kap_ref[...] * (ex * ex + ey * ey + ez * ez))
            slope_hy = absorb(2, i, hy - below[1])
            slope_hx = absorb(3, i, hx - below[0])
            new_e.append((
                ex + factor * ((hz - pltpu.roll(hz, 1, 1)) - slope_hy),
                ey + factor * (slope_hx - (hz - pltpu.roll(hz, 1, 0))),
                ez + factor * ((hy - pltpu.roll(hy, 1, 0)) - (hx - pltpu.roll(hx, 1, 1))),
            ))
        for i in range(GROUP):
            for c in range(3):
                F[c, a + i] = new_e[i][c]
                F[3 + c, a + i] = new_h[i][c]
        for c, at, value in new_states:
            A[c, at] = value

    def sweep(s, lo):
        shift = PAD + s + jnp.where(at_front, 0, planes - PML) - start
        a = PAD + lo
        inside = jnp.logical_and(at_edge, jnp.logical_and(a + GROUP > shift, a < shift + PML))
        when(inside, lambda: group(a, s, shift, True))
        when(jnp.logical_not(inside), lambda: group(a, s, shift, False))

        @pl.when(jnp.logical_and(at_back, high_part))
        def _():
            def plane(p, carry):
                for c in range(3):
                    F[c, p] = jnp.zeros((wide, 2 * rows), jnp.float32)
                return carry

            lax.fori_loop(jnp.maximum(a, PAD + half + s), a + GROUP, plane, 0)

    def arrive(k):
        each(x_halo[k], "wait")()
        if k < half // SPAN:
            when(has_pred, each(z_passed[k], "start"))
            if k + 1 < half // SPAN:
                when(has_pred, each(z_own[k + 1], "start"))
            when(high_part, each(yx[k], "start"))
        else:
            each(yx[k], "start")()

    def pass_aux():
        each(x_aux, "wait")()
        each(yx_aux, "start")()

    def take_aux():
        each(y_aux + yx_aux, "wait")()
        lax.fori_loop(0, PML // 2, unpack_aux, 0)

    n_half = half // SPAN
    back_low = jnp.logical_and(at_back, low_part)
    back_high = jnp.logical_and(at_back, high_part)

    each(x_mat, "wait")()
    each(yx_mat, "start")()
    when(at_front, pass_aux)

    @pl.when(high_part)
    def _():
        for k in range(n_half):
            arrive(k)

    when(back_high, pass_aux)
    each(y_mat + yx_mat, "wait")()
    low = lax.broadcasted_iota(jnp.int32, (2 * COLS, 2 * rows), 0) < COLS
    mat[cols:wide] = jnp.where(low, halo_mat[0], halo_mat[1])
    core = mat[...] > 0.5
    eps_ref[...] = jnp.where(core, jnp.float32(eps_core), jnp.float32(eps_clad))
    kap_ref[...] = jnp.where(core, kerr_ref[1], kerr_ref[0])

    results = ((0, elec_out), (3, magn_out))
    store, hand = [], []
    for t in range(n_half):
        there = [r.at[:, pl.ds(start + t * SPAN, SPAN)] for _, r in results]
        store.append([local(fields(lo, STEPS + t * SPAN, SPAN, cols, own), r) for (lo, _), r in zip(results, there)])
        hand.append([remote(fields(lo, STEPS + t * SPAN, SPAN, cols, far), r, other) for (lo, _), r in zip(results, there)])

    def prepare(j):
        @pl.when(low_part)
        def _():
            if j == 0:
                each(load_low, "wait")()
            if j == n_half:
                each(load_high, "wait")()
                when(at_back, pass_aux)
            arrive(j)
            if j == 0:
                each(y_low, "wait_recv")()
                when(at_front, take_aux)
            if j == n_half:
                each(y_high, "wait_recv")()
                when(at_back, take_aux)
            each(yx[j], "wait_recv")()

        if j < n_half:
            @pl.when(high_part)
            def _():
                if j == 0:
                    each(load_high, "wait")()
                arrive(j + n_half)
                if j == 0:
                    each(y_high, "wait_recv")()
                    when(at_edge, take_aux)
                each(yx[j + n_half], "wait_recv")()
        else:
            @pl.when(takes_z)
            def _():
                for sent, passed in z_from:
                    each(sent[j - n_half] + passed[j - n_half], "wait_recv")()

    def stage(j, carry):
        for k in range(2 * n_half):
            when(j == k, functools.partial(prepare, k))

        @pl.when(jnp.logical_not(jnp.logical_and(back_high, j >= n_half)))
        def _():
            at = quads * gy + PAIRS * j
            lax.fori_loop(at, at + PAIRS, unpack, 0)

        def step(s, carry):
            for i in range(SPAN // GROUP):
                sweep(s, SPAN * j - 1 - s + GROUP * i)
            return carry

        lax.fori_loop(0, jnp.where(j == 0, STEPS // 2, STEPS), step, 0)
        for t in range(n_half):
            when(j == t + n_half, each(hand[t] + store[t], "start"))
        return carry

    lax.fori_loop(0, 2 * n_half, stage, 0)

    @pl.when(has_pred)
    def _():
        for k in range(n_half):
            each(z_own[k] + z_passed[k], "wait_send")()

    @pl.when(high_part)
    def _():
        each(y_low, "wait_send")()
        for k in range(n_half):
            each(yx[k], "wait_send")()

    each(y_high, "wait_send")()
    for k in range(n_half, 2 * n_half):
        each(yx[k], "wait_send")()
    for t in range(n_half):
        each(hand[t] + store[t], "wait")()


def write_out(e_ref, h_ref, elec_out, magn_out, held, in_sem, out_sem):
    refs = ((e_ref, elec_out), (h_ref, magn_out))
    parts = [(i, c) for i in range(2) for c in range(3)]
    into = [pltpu.make_async_copy(refs[i][0].at[c], held.at[i, c], in_sem.at[i, c]) for i, c in parts]
    back = [pltpu.make_async_copy(held.at[i, c], refs[i][1].at[c], out_sem.at[i, c]) for i, c in parts]
    for copy in into:
        copy.start()
    for first, second in zip(into, back):
        first.wait()
        second.start()
    for copy in back:
        copy.wait()


def shards(sizes, electric, magnetic, aux_state, material, kerr_strength):
    _, planes, cols, rows = electric.shape
    wide, deep = cols + 2 * COLS, planes + HALO
    f32 = jnp.float32
    any_space = pl.BlockSpec(memory_space=pl.ANY)
    hbm = pl.BlockSpec(memory_space=pltpu.HBM)
    shape = jax.ShapeDtypeStruct(electric.shape, f32)
    fields = pl.pallas_call(
        functools.partial(kernel, sizes),
        out_shape=(shape, shape),
        in_specs=[pl.BlockSpec(memory_space=pltpu.SMEM), hbm, hbm, hbm, hbm],
        out_specs=(any_space, any_space),
        scratch_shapes=[
            pltpu.VMEM((6, PAD + planes, wide, 2 * rows), f32),
            pltpu.VMEM((4, PML + 1, wide, 2 * rows), f32),
            pltpu.VMEM((wide, 2 * rows), f32),
            pltpu.VMEM((wide, 2 * rows), f32),
            pltpu.VMEM((wide, 2 * rows), f32),
            pltpu.VMEM((cols, rows), jnp.int32),
            pltpu.VMEM((6, planes, cols, rows), f32),
            pltpu.VMEM((2, planes // 2, 6, 2 * COLS, rows), f32),
            pltpu.VMEM((2, PML // 2, 4, 2 * COLS, rows), f32),
            pltpu.VMEM((2, 2 * COLS, rows), f32),
            pltpu.VMEM((2, deep // 2, 6, 2 * COLS, 2 * rows), f32),
            pltpu.VMEM((2, PML // 2, 4, 2 * COLS, 2 * rows), f32),
            pltpu.VMEM((2, 2 * COLS, 2 * rows), f32),
            pltpu.SemaphoreType.DMA((16,)),
            pltpu.SemaphoreType.DMA((40,)),
            pltpu.SemaphoreType.DMA((40,)),
            pltpu.SemaphoreType.DMA((8,)),
            pltpu.SemaphoreType.DMA((8, 2)),
        ],
        compiler_params=pltpu.CompilerParams(
            collective_id=0, has_side_effects=True, vmem_limit_bytes=60 * 2**20
        ),
    )(kerr_strength, electric, magnetic, aux_state, material)
    return pl.pallas_call(
        write_out,
        out_shape=(shape, shape),
        in_specs=[any_space, any_space],
        out_specs=(hbm, hbm),
        scratch_shapes=[
            pltpu.VMEM((2,) + electric.shape, f32),
            pltpu.SemaphoreType.DMA((2, 3)),
            pltpu.SemaphoreType.DMA((2, 3)),
        ],
        compiler_params=pltpu.CompilerParams(vmem_limit_bytes=60 * 2**20),
    )(*fields)


def solution(mesh):
    sizes = tuple(mesh.shape[axis] for axis in ("gz", "gx", "gy"))
    in_specs = (
        P(None, "gz", "gx", "gy"),
        P(None, "gz", "gx", "gy"),
        P(None, None, None, "gx", "gy"),
        P("gx", "gy"),
        P(),
    )
    out_specs = (P(None, "gz", "gx", "gy"), P(None, "gz", "gx", "gy"))
    return jax.shard_map(
        functools.partial(shards, sizes),
        mesh=mesh, in_specs=in_specs, out_specs=out_specs, check_vma=False,
    )
```

```python
import functools

import jax
import jax.numpy as jnp
import numpy as np
from jax import lax
from jax.experimental import pallas as pl
from jax.experimental.pallas import tpu as pltpu
from jax.sharding import PartitionSpec as P

PML = 8
STEPS = 4
HALO = 2 * STEPS
COLS = STEPS
PAD = 4
GROUP = SPAN = 4
PAIRS = SPAN // 2
AHEAD = 2

courant = 0.5
pml_rate = 3.0
eps_clad = 2.085
eps_core = 4.0

MESH = pl.DeviceIdType.MESH
DEPTH_RATES = [
    float(np.exp(np.float32(-pml_rate) * np.float32((m + 1) / PML) ** 3)) for m in range(PML)
]


def kernel(
    sizes,
    kerr_ref, elec, magn, aux, material,
    elec_out, magn_out,
    F, A, eps_ref, kap_ref, mat, mat_own, own_fields,
    pack, pack_aux, pack_mat,
    halo, halo_aux, halo_mat,
    local_sem, send_sem, recv_sem, z_send_sem, z_recv_sem,
):
    n_gz, n_gx, n_gy = sizes
    planes, cols, rows = elec.shape[1:]
    wide = cols + 2 * COLS
    half = planes // 2
    quads = half // 2
    pairs = planes // 2
    gz, gx, gy = lax.axis_index("gz"), lax.axis_index("gx"), lax.axis_index("gy")
    low_part, high_part = gy == 0, gy == 1
    has_pred = gz > 0
    takes_z = jnp.logical_and(high_part, gz < n_gz - 1)
    at_front, at_back = gz == 0, gz == n_gz - 1
    at_edge = jnp.logical_or(at_front, at_back)
    left = {"gx": lax.rem(gx + n_gx - 1, n_gx)}
    right = {"gx": lax.rem(gx + 1, n_gx)}
    other = {"gy": 1 - gy}
    pred = {"gz": jnp.maximum(gz - 1, 0), "gy": 1}
    succ = [{"gz": jnp.minimum(gz + 1, n_gz - 1), "gy": part} for part in (0, 1)]
    own, far = pl.ds(0, rows), pl.ds(rows, rows)
    z_lanes = pl.ds(pl.multiple_of((1 - gy) * rows, rows), rows)
    start = half * gy
    side = jnp.where(at_front, 0, 1)
    args = ((0, elec), (3, magn))

    def fields(lo, at, n, width, lanes):
        return F.at[pl.ds(lo, 3), pl.ds(PAD + at, n), pl.ds(0, width), lanes]

    def when(condition, work):
        pl.when(condition)(work)

    def each(copies, method):
        def work():
            for copy in copies:
                getattr(copy, method)()

        return work

    count = [0]

    def local(src, dst):
        count[0] += 1
        return pltpu.make_async_copy(src, dst, local_sem.at[count[0] - 1])

    stage_low = [local(r.at[:, pl.ds(0, half)], own_fields.at[pl.ds(lo, 3), pl.ds(0, half)]) for lo, r in args]
    stage_high = [local(r.at[:, pl.ds(half, half)], own_fields.at[pl.ds(lo, 3), pl.ds(half, half)]) for lo, r in args]
    load_mat = local(material, mat_own)
    load_aux = local(aux.at[:, side], A.at[:, pl.ds(0, PML), pl.ds(0, cols), own])
    load_low = [local(r.at[:, pl.ds(0, half)], fields(lo, 0, half, cols, own)) for lo, r in args]
    load_high = [local(r.at[:, pl.ds(half, half)], fields(lo, half - start, half, cols, own)) for lo, r in args]
    for copy in stage_low + stage_high + [load_mat]:
        copy.start()
    when(at_edge, each([load_aux], "start"))
    when(low_part, each(load_low, "start"))
    each(load_high, "start")()

    barrier = pltpu.get_barrier_semaphore()

    def greet(peers):
        def work():
            for peer in peers:
                pl.semaphore_signal(barrier, inc=1, device_id=peer, device_id_type=MESH)

        return work

    greet([left, right, other])()
    when(has_pred, greet([pred]))
    when(takes_z, greet(succ))

    numbered = [0]

    def remote(src, dst, peer):
        at = numbered[0]
        numbered[0] += 1
        return pltpu.make_async_remote_copy(
            src_ref=src, dst_ref=dst, send_sem=send_sem.at[at], recv_sem=recv_sem.at[at],
            device_id=peer, device_id_type=MESH,
        )

    z_numbered = [0]

    def z_remote(src, dst, sender):
        at = z_numbered[0]
        z_numbered[0] += 1
        return pltpu.make_async_remote_copy(
            src_ref=src, dst_ref=dst, send_sem=z_send_sem.at[at], recv_sem=z_recv_sem.at[at, sender],
            device_id=pred, device_id_type=MESH,
        )

    def staged(lo, at, n):
        return own_fields.at[pl.ds(lo, 3), pl.ds(at, n)]

    def tiles(d, at, n, lanes):
        return halo.at[d, pl.ds(at, n), :, :, lanes]

    both = ((0, left), (1, right))
    chunks = [(k * PAIRS, PAIRS) for k in range(pairs // PAIRS)]
    x_halo = [[remote(pack.at[d, pl.ds(at, n)], tiles(d, at, n, own), p) for d, p in both] for at, n in chunks]
    x_mat = [remote(pack_mat.at[d], halo_mat.at[d, :, own], p) for d, p in both]
    x_aux = [remote(pack_aux.at[d], halo_aux.at[d, :, :, :, own], p) for d, p in both]
    y_low = [remote(staged(lo, 0, half), fields(lo, 0, half, cols, far), other) for lo, r in args]
    y_high = [remote(staged(lo, half, half), fields(lo, start, half, cols, far), other) for lo, r in args]
    yx = [[remote(tiles(d, at, n, own), tiles(d, at, n, far), other) for d in (0, 1)] for at, n in chunks]
    y_aux = [remote(A.at[:, pl.ds(0, PML), pl.ds(0, cols), own], A.at[:, pl.ds(0, PML), pl.ds(0, cols), far], other)]
    yx_aux = [remote(halo_aux.at[d, :, :, :, own], halo_aux.at[d, :, :, :, far], other) for d in (0, 1)]
    y_mat = [remote(mat.at[pl.ds(0, cols), own], mat.at[pl.ds(0, cols), far], other)]
    yx_mat = [remote(halo_mat.at[d, :, own], halo_mat.at[d, :, far], other) for d in (0, 1)]

    def z_copies(sender, lanes):
        z_numbered[0] = 0
        sent, passed = [], []
        for k in range(half // SPAN):
            sent.append([
                z_remote(staged(lo, k * SPAN, SPAN), fields(lo, half + k * SPAN, SPAN, cols, lanes), sender)
                for lo, r in args
            ])
            at, n = chunks[k]
            passed.append([z_remote(tiles(d, at, n, own), tiles(d, pairs + at, n, lanes), sender) for d in (0, 1)])
        return sent, passed

    z_own, z_passed = z_copies(gy, z_lanes)
    z_from = [z_copies(0, far), z_copies(1, own)]

    def pack_pair(q, carry):
        for c in range(6):
            pack[0, q, c, 0:COLS] = own_fields[c, 2 * q, 0:COLS]
            pack[0, q, c, COLS:] = own_fields[c, 2 * q + 1, 0:COLS]
            pack[1, q, c, 0:COLS] = own_fields[c, 2 * q + 1, cols - COLS : cols]
            pack[1, q, c, COLS:] = own_fields[c, 2 * q, cols - COLS : cols]
        return carry

    def pack_aux_pair(q, carry):
        for c in range(4):
            pack_aux[0, q, c, 0:COLS] = A[c, 2 * q, 0:COLS, 0:rows]
            pack_aux[0, q, c, COLS:] = A[c, 2 * q + 1, 0:COLS, 0:rows]
            pack_aux[1, q, c, 0:COLS] = A[c, 2 * q + 1, cols - COLS : cols, 0:rows]
            pack_aux[1, q, c, COLS:] = A[c, 2 * q, cols - COLS : cols, 0:rows]
        return carry

    load_mat.wait()
    m = (mat_own[...] == 1).astype(jnp.float32)
    mat[0:cols, 0:rows] = m
    pack_mat[0] = m[0 : 2 * COLS]
    pack_mat[1] = m[cols - 2 * COLS : cols]
    each(stage_low, "wait")()
    lax.fori_loop(0, quads, pack_pair, 0)
    each(stage_high, "wait")()
    lax.fori_loop(quads, pairs, pack_pair, 0)

    @pl.when(at_edge)
    def _():
        load_aux.wait()
        lax.fori_loop(0, PML // 2, pack_aux_pair, 0)

    pl.semaphore_wait(barrier, 3 + has_pred.astype(jnp.int32) + 2 * takes_z.astype(jnp.int32))

    when(has_pred, each(z_own[0], "start"))
    each(x_mat + y_mat, "start")()
    when(at_front, each(x_aux + y_aux, "start"))
    for k in range(AHEAD):
        each(x_halo[k], "start")()
    when(high_part, each(y_low, "start"))
    each(y_high, "start")()

    def clear(lo, n):
        def plane(a, carry):
            for c in range(6):
                F[c, a] = jnp.zeros((wide, 2 * rows), jnp.float32)
            return carry

        lax.fori_loop(lo, lo + n, plane, 0)

    clear(0, PAD)
    when(jnp.logical_and(at_back, high_part), lambda: clear(PAD + half, half))

    def joined(r, l):
        low = lax.broadcasted_iota(jnp.int32, (2 * COLS, 2 * rows), 0) < COLS
        return jnp.where(low, r, l), pltpu.roll(jnp.where(low, l, r), COLS, 0)

    def unpack(q, carry):
        at = PAD + 2 * q - start
        for c in range(6):
            F[c, at, cols:wide], F[c, at + 1, cols:wide] = joined(halo[0, q, c], halo[1, q, c])
        return carry

    def unpack_aux(q, carry):
        for c in range(4):
            A[c, 2 * q, cols:wide], A[c, 2 * q + 1, cols:wide] = joined(halo_aux[0, q, c], halo_aux[1, q, c])
        return carry

    nx, ny = wide - 1, 2 * rows - 1

    def group(a, s, shift, absorbing):
        E = [[F[c, a + i] for c in range(3)] for i in range(GROUP + 1)]
        H = [[F[c, a + i] for c in range(3, 6)] for i in range(GROUP)]
        before = F[3, a - 1], F[4, a - 1]
        rates = []
        states = []
        if absorbing:
            for i in range(GROUP):
                k = a + i - shift
                inside = jnp.logical_and(k >= 0, k < PML)
                at = jnp.where(inside, k, PML)
                m = jnp.where(at_front, PML - 1 - k, k)
                b = jnp.float32(DEPTH_RATES[0])
                for j in range(1, PML):
                    b = jnp.where(m == j, jnp.float32(DEPTH_RATES[j]), b)
                rates.append((inside, at, b))
                states.append([A[c, at] for c in range(4)])

        new_states = []

        def absorb(c, i, g):
            if not absorbing:
                return g
            inside, at, b = rates[i]
            g_new = jnp.where(inside, b * (g + states[i][c]), g)
            new_states.append((c, at, g_new - g))
            return g_new

        new_h = []
        for i in range(GROUP):
            ex, ey, ez = E[i]
            slope_y = absorb(0, i, E[i + 1][1] - ey)
            slope_x = absorb(1, i, E[i + 1][0] - ex)
            hx = H[i][0] - courant * ((pltpu.roll(ez, ny, 1) - ez) - slope_y)
            hy = H[i][1] - courant * (slope_x - (pltpu.roll(ez, nx, 0) - ez))
            hz = H[i][2] - courant * ((pltpu.roll(ey, nx, 0) - ey) - (pltpu.roll(ex, ny, 1) - ex))
            new_h.append((hx, hy, hz))
        new_e = []
        for i in range(GROUP):
            ex, ey, ez = E[i]
            hx, hy, hz = new_h[i]
            below = before if i == 0 else new_h[i - 1]
            factor = courant / (eps_ref[...] + kap_ref[...] * (ex * ex + ey * ey + ez * ez))
            slope_hy = absorb(2, i, hy - below[1])
            slope_hx = absorb(3, i, hx - below[0])
            new_e.append((
                ex + factor * ((hz - pltpu.roll(hz, 1, 1)) - slope_hy),
                ey + factor * (slope_hx - (hz - pltpu.roll(hz, 1, 0))),
                ez + factor * ((hy - pltpu.roll(hy, 1, 0)) - (hx - pltpu.roll(hx, 1, 1))),
            ))
        for i in range(GROUP):
            for c in range(3):
                F[c, a + i] = new_e[i][c]
                F[3 + c, a + i] = new_h[i][c]
        for c, at, value in new_states:
            A[c, at] = value

    def sweep(s, lo):
        shift = PAD + s + jnp.where(at_front, 0, planes - PML) - start
        a = PAD + lo
        inside = jnp.logical_and(at_edge, jnp.logical_and(a + GROUP > shift, a < shift + PML))
        when(inside, lambda: group(a, s, shift, True))
        when(jnp.logical_not(inside), lambda: group(a, s, shift, False))

        @pl.when(jnp.logical_and(at_back, high_part))
        def _():
            def plane(p, carry):
                for c in range(3):
                    F[c, p] = jnp.zeros((wide, 2 * rows), jnp.float32)
                return carry

            lax.fori_loop(jnp.maximum(a, PAD + half + s), a + GROUP, plane, 0)

    def arrive(k):
        each(x_halo[k], "wait")()
        if k == 0:
            when(at_back, each(x_aux + y_aux, "start"))
        if k + AHEAD < len(x_halo):
            each(x_halo[k + AHEAD], "start")()
        if k < half // SPAN:
            when(has_pred, each(z_passed[k], "start"))
            if k + 1 < half // SPAN:
                when(has_pred, each(z_own[k + 1], "start"))
            when(high_part, each(yx[k], "start"))
        else:
            each(yx[k], "start")()

    def pass_aux():
        each(x_aux, "wait")()
        each(yx_aux, "start")()

    def take_aux():
        each(y_aux + yx_aux, "wait")()
        lax.fori_loop(0, PML // 2, unpack_aux, 0)

    n_half = half // SPAN
    back_low = jnp.logical_and(at_back, low_part)
    back_high = jnp.logical_and(at_back, high_part)

    each(x_mat, "wait")()
    each(yx_mat, "start")()
    when(at_front, pass_aux)

    @pl.when(high_part)
    def _():
        for k in range(n_half):
            arrive(k)

    when(back_high, pass_aux)
    each(y_mat + yx_mat, "wait")()
    low = lax.broadcasted_iota(jnp.int32, (2 * COLS, 2 * rows), 0) < COLS
    mat[cols:wide] = jnp.where(low, halo_mat[0], halo_mat[1])
    core = mat[...] > 0.5
    eps_ref[...] = jnp.where(core, jnp.float32(eps_core), jnp.float32(eps_clad))
    kap_ref[...] = jnp.where(core, kerr_ref[1], kerr_ref[0])

    results = ((0, elec_out), (3, magn_out))
    store, hand = [], []
    for t in range(n_half):
        there = [r.at[:, pl.ds(start + t * SPAN, SPAN)] for _, r in results]
        store.append([local(fields(lo, STEPS + t * SPAN, SPAN, cols, own), r) for (lo, _), r in zip(results, there)])
        hand.append([remote(fields(lo, STEPS + t * SPAN, SPAN, cols, far), r, other) for (lo, _), r in zip(results, there)])

    def prepare(j):
        @pl.when(low_part)
        def _():
            if j == 0:
                each(load_low, "wait")()
            if j == n_half:
                each(load_high, "wait")()
                when(at_back, pass_aux)
            arrive(j)
            if j == 0:
                each(y_low, "wait_recv")()
                when(at_front, take_aux)
            if j == n_half:
                each(y_high, "wait_recv")()
                when(at_back, take_aux)
            each(yx[j], "wait_recv")()

        if j < n_half:
            @pl.when(high_part)
            def _():
                if j == 0:
                    each(load_high, "wait")()
                arrive(j + n_half)
                if j == 0:
                    each(y_high, "wait_recv")()
                    when(at_edge, take_aux)
                each(yx[j + n_half], "wait_recv")()
        else:
            @pl.when(takes_z)
            def _():
                for sent, passed in z_from:
                    each(sent[j - n_half] + passed[j - n_half], "wait_recv")()

    def stage(j, carry):
        for k in range(2 * n_half):
            when(j == k, functools.partial(prepare, k))

        @pl.when(jnp.logical_not(jnp.logical_and(back_high, j >= n_half)))
        def _():
            at = quads * gy + PAIRS * j
            lax.fori_loop(at, at + PAIRS, unpack, 0)

        def step(s, carry):
            sweep(s, SPAN * j - 1 - s)
            return carry

        lax.fori_loop(0, jnp.where(j == 0, STEPS // 2, STEPS), step, 0)
        for t in range(n_half):
            when(j == t + n_half, each(hand[t] + store[t], "start"))
        return carry

    lax.fori_loop(0, 2 * n_half, stage, 0)

    @pl.when(has_pred)
    def _():
        for k in range(n_half):
            each(z_own[k] + z_passed[k], "wait_send")()

    @pl.when(high_part)
    def _():
        each(y_low, "wait_send")()
        for k in range(n_half):
            each(yx[k], "wait_send")()

    each(y_high, "wait_send")()
    for k in range(n_half, 2 * n_half):
        each(yx[k], "wait_send")()
    for t in range(n_half):
        each(hand[t] + store[t], "wait")()


def write_out(e_ref, h_ref, elec_out, magn_out, held, in_sem, out_sem):
    refs = ((e_ref, elec_out), (h_ref, magn_out))
    parts = [(i, c) for i in range(2) for c in range(3)]
    into = [pltpu.make_async_copy(refs[i][0].at[c], held.at[i, c], in_sem.at[i, c]) for i, c in parts]
    back = [pltpu.make_async_copy(held.at[i, c], refs[i][1].at[c], out_sem.at[i, c]) for i, c in parts]
    for copy in into:
        copy.start()
    for first, second in zip(into, back):
        first.wait()
        second.start()
    for copy in back:
        copy.wait()


def shards(sizes, electric, magnetic, aux_state, material, kerr_strength):
    _, planes, cols, rows = electric.shape
    wide, deep = cols + 2 * COLS, planes + HALO
    f32 = jnp.float32
    any_space = pl.BlockSpec(memory_space=pl.ANY)
    hbm = pl.BlockSpec(memory_space=pltpu.HBM)
    shape = jax.ShapeDtypeStruct(electric.shape, f32)
    fields = pl.pallas_call(
        functools.partial(kernel, sizes),
        out_shape=(shape, shape),
        in_specs=[pl.BlockSpec(memory_space=pltpu.SMEM), hbm, hbm, hbm, hbm],
        out_specs=(any_space, any_space),
        scratch_shapes=[
            pltpu.VMEM((6, PAD + planes, wide, 2 * rows), f32),
            pltpu.VMEM((4, PML + 1, wide, 2 * rows), f32),
            pltpu.VMEM((wide, 2 * rows), f32),
            pltpu.VMEM((wide, 2 * rows), f32),
            pltpu.VMEM((wide, 2 * rows), f32),
            pltpu.VMEM((cols, rows), jnp.int32),
            pltpu.VMEM((6, planes, cols, rows), f32),
            pltpu.VMEM((2, planes // 2, 6, 2 * COLS, rows), f32),
            pltpu.VMEM((2, PML // 2, 4, 2 * COLS, rows), f32),
            pltpu.VMEM((2, 2 * COLS, rows), f32),
            pltpu.VMEM((2, deep // 2, 6, 2 * COLS, 2 * rows), f32),
            pltpu.VMEM((2, PML // 2, 4, 2 * COLS, 2 * rows), f32),
            pltpu.VMEM((2, 2 * COLS, 2 * rows), f32),
            pltpu.SemaphoreType.DMA((16,)),
            pltpu.SemaphoreType.DMA((40,)),
            pltpu.SemaphoreType.DMA((40,)),
            pltpu.SemaphoreType.DMA((8,)),
            pltpu.SemaphoreType.DMA((8, 2)),
        ],
        compiler_params=pltpu.CompilerParams(
            collective_id=0, has_side_effects=True, vmem_limit_bytes=60 * 2**20
        ),
    )(kerr_strength, electric, magnetic, aux_state, material)
    return pl.pallas_call(
        write_out,
        out_shape=(shape, shape),
        in_specs=[any_space, any_space],
        out_specs=(hbm, hbm),
        scratch_shapes=[
            pltpu.VMEM((2,) + electric.shape, f32),
            pltpu.SemaphoreType.DMA((2, 3)),
            pltpu.SemaphoreType.DMA((2, 3)),
        ],
        compiler_params=pltpu.CompilerParams(vmem_limit_bytes=60 * 2**20),
    )(*fields)


def solution(mesh):
    sizes = tuple(mesh.shape[axis] for axis in ("gz", "gx", "gy"))
    in_specs = (
        P(None, "gz", "gx", "gy"),
        P(None, "gz", "gx", "gy"),
        P(None, None, None, "gx", "gy"),
        P("gx", "gy"),
        P(),
    )
    out_specs = (P(None, "gz", "gx", "gy"), P(None, "gz", "gx", "gy"))
    return jax.shard_map(
        functools.partial(shards, sizes),
        mesh=mesh, in_specs=in_specs, out_specs=out_specs, check_vma=False,
    )
```

```python
import functools

import jax
import jax.numpy as jnp
import numpy as np
from jax import lax
from jax.experimental import pallas as pl
from jax.experimental.pallas import tpu as pltpu
from jax.sharding import PartitionSpec as P

PML = 8
STEPS = 4
HALO = 2 * STEPS
COLS = STEPS
PAD = 4
GROUP = SPAN = 4
STRIDE = 2
PAIRS = SPAN // 2
AHEAD = 2

courant = 0.5
pml_rate = 3.0
eps_clad = 2.085
eps_core = 4.0

MESH = pl.DeviceIdType.MESH
DEPTH_RATES = [
    float(np.exp(np.float32(-pml_rate) * np.float32((m + 1) / PML) ** 3)) for m in range(PML)
]


def kernel(
    sizes,
    kerr_ref, elec, magn, aux, material,
    elec_out, magn_out,
    F, A, eps_ref, kap_ref, mat, mat_own, own_fields,
    pack, pack_aux, pack_mat,
    halo, halo_aux, halo_mat,
    local_sem, send_sem, recv_sem, z_send_sem, z_recv_sem,
):
    n_gz, n_gx, n_gy = sizes
    planes, cols, rows = elec.shape[1:]
    wide = cols + 2 * COLS
    half = planes // 2
    quads = half // 2
    pairs = planes // 2
    gz, gx, gy = lax.axis_index("gz"), lax.axis_index("gx"), lax.axis_index("gy")
    low_part, high_part = gy == 0, gy == 1
    has_pred = gz > 0
    takes_z = jnp.logical_and(high_part, gz < n_gz - 1)
    at_front, at_back = gz == 0, gz == n_gz - 1
    at_edge = jnp.logical_or(at_front, at_back)
    left = {"gx": lax.rem(gx + n_gx - 1, n_gx)}
    right = {"gx": lax.rem(gx + 1, n_gx)}
    other = {"gy": 1 - gy}
    pred = {"gz": jnp.maximum(gz - 1, 0), "gy": 1}
    succ = [{"gz": jnp.minimum(gz + 1, n_gz - 1), "gy": part} for part in (0, 1)]
    own, far = pl.ds(0, rows), pl.ds(rows, rows)
    z_lanes = pl.ds(pl.multiple_of((1 - gy) * rows, rows), rows)
    back_high = jnp.logical_and(at_back, high_part)
    start = half * gy
    side = jnp.where(at_front, 0, 1)
    args = ((0, elec), (3, magn))

    def fields(lo, at, n, width, lanes):
        return F.at[pl.ds(lo, 3), pl.ds(PAD + at, n), pl.ds(0, width), lanes]

    def when(condition, work):
        pl.when(condition)(work)

    def each(copies, method):
        def work():
            for copy in copies:
                getattr(copy, method)()

        return work

    count = [0]

    def local(src, dst):
        count[0] += 1
        return pltpu.make_async_copy(src, dst, local_sem.at[count[0] - 1])

    stage_low = [local(r.at[:, pl.ds(0, half)], own_fields.at[pl.ds(lo, 3), pl.ds(0, half)]) for lo, r in args]
    stage_high = [local(r.at[:, pl.ds(half, half)], own_fields.at[pl.ds(lo, 3), pl.ds(half, half)]) for lo, r in args]
    load_mat = local(material, mat_own)
    load_aux = local(aux.at[:, side], A.at[:, pl.ds(0, PML), pl.ds(0, cols), own])
    load_low = [local(r.at[:, pl.ds(0, half)], fields(lo, 0, half, cols, own)) for lo, r in args]
    load_high = [local(r.at[:, pl.ds(half, half)], fields(lo, half - start, half, cols, own)) for lo, r in args]
    for copy in stage_low + stage_high + [load_mat]:
        copy.start()
    when(at_edge, each([load_aux], "start"))
    when(low_part, each(load_low, "start"))
    each(load_high, "start")()

    barrier = pltpu.get_barrier_semaphore()

    def greet(peers):
        def work():
            for peer in peers:
                pl.semaphore_signal(barrier, inc=1, device_id=peer, device_id_type=MESH)

        return work

    greet([left, right, other])()
    when(has_pred, greet([pred]))
    when(takes_z, greet(succ))

    numbered = [0]

    def remote(src, dst, peer):
        at = numbered[0]
        numbered[0] += 1
        return pltpu.make_async_remote_copy(
            src_ref=src, dst_ref=dst, send_sem=send_sem.at[at], recv_sem=recv_sem.at[at],
            device_id=peer, device_id_type=MESH,
        )

    z_numbered = [0]

    def z_remote(src, dst, sender):
        at = z_numbered[0]
        z_numbered[0] += 1
        return pltpu.make_async_remote_copy(
            src_ref=src, dst_ref=dst, send_sem=z_send_sem.at[at], recv_sem=z_recv_sem.at[at, sender],
            device_id=pred, device_id_type=MESH,
        )

    def staged(lo, at, n):
        return own_fields.at[pl.ds(lo, 3), pl.ds(at, n)]

    def tiles(d, at, n, lanes):
        return halo.at[d, pl.ds(at, n), :, :, lanes]

    both = ((0, left), (1, right))
    chunks = [(k * PAIRS, PAIRS) for k in range(pairs // PAIRS)]
    x_halo = [[remote(pack.at[d, pl.ds(at, n)], tiles(d, at, n, own), p) for d, p in both] for at, n in chunks]
    x_mat = [remote(pack_mat.at[d], halo_mat.at[d, :, own], p) for d, p in both]
    x_aux = [remote(pack_aux.at[d], halo_aux.at[d, :, :, :, own], p) for d, p in both]
    y_low = [remote(staged(lo, 0, half), fields(lo, 0, half, cols, far), other) for lo, r in args]
    y_high = [remote(staged(lo, half, half), fields(lo, start, half, cols, far), other) for lo, r in args]
    yx = [[remote(tiles(d, at, n, own), tiles(d, at, n, far), other) for d in (0, 1)] for at, n in chunks]
    y_aux = [remote(A.at[:, pl.ds(0, PML), pl.ds(0, cols), own], A.at[:, pl.ds(0, PML), pl.ds(0, cols), far], other)]
    yx_aux = [remote(halo_aux.at[d, :, :, :, own], halo_aux.at[d, :, :, :, far], other) for d in (0, 1)]
    y_mat = [remote(mat.at[pl.ds(0, cols), own], mat.at[pl.ds(0, cols), far], other)]
    yx_mat = [remote(halo_mat.at[d, :, own], halo_mat.at[d, :, far], other) for d in (0, 1)]

    def z_copies(sender, lanes):
        z_numbered[0] = 0
        sent, passed = [], []
        for k in range(half // SPAN):
            sent.append([
                z_remote(staged(lo, k * SPAN, SPAN), fields(lo, half + k * SPAN, SPAN, cols, lanes), sender)
                for lo, r in args
            ])
            at, n = chunks[k]
            passed.append([z_remote(tiles(d, at, n, own), tiles(d, pairs + at, n, lanes), sender) for d in (0, 1)])
        return sent, passed

    z_own, z_passed = z_copies(gy, z_lanes)
    z_from = [z_copies(0, far), z_copies(1, own)]

    def pack_pair(q, carry):
        for c in range(6):
            pack[0, q, c, 0:COLS] = own_fields[c, 2 * q, 0:COLS]
            pack[0, q, c, COLS:] = own_fields[c, 2 * q + 1, 0:COLS]
            pack[1, q, c, 0:COLS] = own_fields[c, 2 * q + 1, cols - COLS : cols]
            pack[1, q, c, COLS:] = own_fields[c, 2 * q, cols - COLS : cols]
        return carry

    def pack_aux_pair(q, carry):
        for c in range(4):
            pack_aux[0, q, c, 0:COLS] = A[c, 2 * q, 0:COLS, 0:rows]
            pack_aux[0, q, c, COLS:] = A[c, 2 * q + 1, 0:COLS, 0:rows]
            pack_aux[1, q, c, 0:COLS] = A[c, 2 * q + 1, cols - COLS : cols, 0:rows]
            pack_aux[1, q, c, COLS:] = A[c, 2 * q, cols - COLS : cols, 0:rows]
        return carry

    load_mat.wait()
    m = (mat_own[...] == 1).astype(jnp.float32)
    mat[0:cols, 0:rows] = m
    pack_mat[0] = m[0 : 2 * COLS]
    pack_mat[1] = m[cols - 2 * COLS : cols]
    each(stage_low, "wait")()
    lax.fori_loop(0, quads, pack_pair, 0)
    each(stage_high, "wait")()
    lax.fori_loop(quads, pairs, pack_pair, 0)

    @pl.when(at_edge)
    def _():
        load_aux.wait()
        lax.fori_loop(0, PML // 2, pack_aux_pair, 0)

    pl.semaphore_wait(barrier, 3 + has_pred.astype(jnp.int32) + 2 * takes_z.astype(jnp.int32))

    when(has_pred, each(z_own[0], "start"))
    each(x_mat + y_mat, "start")()
    when(at_front, each(x_aux + y_aux, "start"))
    for k in range(AHEAD):
        each(x_halo[k], "start")()
    when(high_part, each(y_low, "start"))
    each(y_high, "start")()

    def clear(lo, n):
        def plane(a, carry):
            for c in range(6):
                F[c, a] = jnp.zeros((wide, 2 * rows), jnp.float32)
            return carry

        lax.fori_loop(lo, lo + n, plane, 0)

    clear(0, PAD)
    for c in range(4):
        A[c, PML] = jnp.zeros((wide, 2 * rows), jnp.float32)
    when(jnp.logical_and(at_back, high_part), lambda: clear(PAD + half, half))

    def joined(r, l):
        low = lax.broadcasted_iota(jnp.int32, (2 * COLS, 2 * rows), 0) < COLS
        return jnp.where(low, r, l), pltpu.roll(jnp.where(low, l, r), COLS, 0)

    def unpack(q, carry):
        at = PAD + 2 * q - start
        for c in range(6):
            F[c, at, cols:wide], F[c, at + 1, cols:wide] = joined(halo[0, q, c], halo[1, q, c])
        return carry

    def unpack_aux(q, carry):
        for c in range(4):
            A[c, 2 * q, cols:wide], A[c, 2 * q + 1, cols:wide] = joined(halo_aux[0, q, c], halo_aux[1, q, c])
        return carry

    nx, ny = wide - 1, 2 * rows - 1

    def steps(base, s, absorbing):
        known = {}

        def load(c, at):
            return known[c, at] if (c, at) in known else F[c, base + at]

        def advance(i):
            low = -i
            E = [[load(c, low + p) for c in range(3)] for p in range(GROUP + 1)]
            H = [[load(c, low + p) for c in range(3, 6)] for p in range(GROUP)]
            before = load(3, low - 1), load(4, low - 1)
            rates = []
            if absorbing:
                shift = PAD + s + i + jnp.where(at_front, 0, planes - PML) - start
                for p in range(GROUP):
                    k = base + low + p - shift
                    inside = jnp.logical_and(k >= 0, k < PML)
                    m = jnp.where(at_front, PML - 1 - k, k)
                    b = jnp.float32(1.0)
                    for j in range(PML):
                        b = jnp.where(m == j, jnp.float32(DEPTH_RATES[j]), b)
                    beyond = jnp.logical_and(back_high, base + low + p >= PAD + half + s + i)
                    rates.append((jnp.where(inside, k, PML), b, beyond))
            new_states = []
            states = [[A[c, at] for c in range(4)] for at, _, _ in rates]

            def absorb(c, p, g):
                if not absorbing:
                    return g
                at, b, _ = rates[p]
                g_new = b * (g + states[p][c])
                new_states.append((c, at, g_new - g))
                return g_new

            new_h, new_e = [], []
            for p in range(GROUP):
                ex, ey, ez = E[p]
                slope_y = absorb(0, p, E[p + 1][1] - ey)
                slope_x = absorb(1, p, E[p + 1][0] - ex)
                hx = H[p][0] - courant * ((pltpu.roll(ez, ny, 1) - ez) - slope_y)
                hy = H[p][1] - courant * (slope_x - (pltpu.roll(ez, nx, 0) - ez))
                hz = H[p][2] - courant * ((pltpu.roll(ey, nx, 0) - ey) - (pltpu.roll(ex, ny, 1) - ex))
                new_h.append((hx, hy, hz))
            for p in range(GROUP):
                ex, ey, ez = E[p]
                hx, hy, hz = new_h[p]
                below = before if p == 0 else new_h[p - 1]
                factor = courant / (eps_ref[...] + kap_ref[...] * (ex * ex + ey * ey + ez * ez))
                if absorbing:
                    factor = jnp.where(rates[p][2], 0.0, factor)
                slope_hy = absorb(2, p, hy - below[1])
                slope_hx = absorb(3, p, hx - below[0])
                new_e.append((
                    ex + factor * ((hz - pltpu.roll(hz, 1, 1)) - slope_hy),
                    ey + factor * (slope_hx - (hz - pltpu.roll(hz, 1, 0))),
                    ez + factor * ((hy - pltpu.roll(hy, 1, 0)) - (hx - pltpu.roll(hx, 1, 1))),
                ))
            for p in range(GROUP):
                for c, value in enumerate(new_e[p] + new_h[p]):
                    known[c, low + p] = value
                    F[c, base + low + p] = value
            for c, at, value in new_states:
                A[c, at] = value

        for i in range(STRIDE):
            advance(i)

    def arrive(k):
        each(x_halo[k], "wait")()
        if k == 0:
            when(at_back, each(x_aux + y_aux, "start"))
        if k + AHEAD < len(x_halo):
            each(x_halo[k + AHEAD], "start")()
        if k < half // SPAN:
            when(has_pred, each(z_passed[k], "start"))
            if k + 1 < half // SPAN:
                when(has_pred, each(z_own[k + 1], "start"))
            when(high_part, each(yx[k], "start"))
        else:
            each(yx[k], "start")()

    def pass_aux():
        each(x_aux, "wait")()
        each(yx_aux, "start")()

    def take_aux():
        each(y_aux + yx_aux, "wait")()
        lax.fori_loop(0, PML // 2, unpack_aux, 0)

    n_half = half // SPAN
    each(x_mat, "wait")()
    each(yx_mat, "start")()
    when(at_front, pass_aux)

    @pl.when(high_part)
    def _():
        for k in range(n_half):
            arrive(k)

    when(back_high, pass_aux)
    each(y_mat + yx_mat, "wait")()
    low = lax.broadcasted_iota(jnp.int32, (2 * COLS, 2 * rows), 0) < COLS
    mat[cols:wide] = jnp.where(low, halo_mat[0], halo_mat[1])
    core = mat[...] > 0.5
    eps_ref[...] = jnp.where(core, jnp.float32(eps_core), jnp.float32(eps_clad))
    kap_ref[...] = jnp.where(core, kerr_ref[1], kerr_ref[0])

    results = ((0, elec_out), (3, magn_out))
    store, hand = [], []
    for t in range(n_half):
        there = [r.at[:, pl.ds(start + t * SPAN, SPAN)] for _, r in results]
        store.append([local(fields(lo, STEPS + t * SPAN, SPAN, cols, own), r) for (lo, _), r in zip(results, there)])
        hand.append([remote(fields(lo, STEPS + t * SPAN, SPAN, cols, far), r, other) for (lo, _), r in zip(results, there)])

    def prepare(j):
        @pl.when(low_part)
        def _():
            if j == 0:
                each(load_low, "wait")()
            if j == n_half:
                each(load_high, "wait")()
                when(at_back, pass_aux)
            arrive(j)
            if j == 0:
                each(y_low, "wait_recv")()
                when(at_front, take_aux)
            if j == n_half:
                each(y_high, "wait_recv")()
                when(at_back, take_aux)
            each(yx[j], "wait_recv")()

        if j < n_half:
            @pl.when(high_part)
            def _():
                if j == 0:
                    each(load_high, "wait")()
                arrive(j + n_half)
                if j == 0:
                    each(y_high, "wait_recv")()
                    when(at_edge, take_aux)
                each(yx[j + n_half], "wait_recv")()
        else:
            @pl.when(takes_z)
            def _():
                for sent, passed in z_from:
                    each(sent[j - n_half] + passed[j - n_half], "wait_recv")()

    def stage(j, carry):
        for k in range(2 * n_half):
            when(j == k, functools.partial(prepare, k))

        @pl.when(jnp.logical_not(jnp.logical_and(back_high, j >= n_half)))
        def _():
            at = quads * gy + PAIRS * j
            lax.fori_loop(at, at + PAIRS, unpack, 0)

        def some_steps(r, carry):
            s = STRIDE * r
            base = PAD + SPAN * j - 1 - s
            when(at_edge, lambda: steps(base, s, True))
            when(jnp.logical_not(at_edge), lambda: steps(base, s, False))
            return carry

        lax.fori_loop(0, jnp.where(j == 0, STEPS // 2, STEPS) // STRIDE, some_steps, 0)
        for t in range(n_half):
            when(j == t + n_half, each(hand[t] + store[t], "start"))
        return carry

    lax.fori_loop(0, 2 * n_half, stage, 0)

    @pl.when(has_pred)
    def _():
        for k in range(n_half):
            each(z_own[k] + z_passed[k], "wait_send")()

    @pl.when(high_part)
    def _():
        each(y_low, "wait_send")()
        for k in range(n_half):
            each(yx[k], "wait_send")()

    each(y_high, "wait_send")()
    for k in range(n_half, 2 * n_half):
        each(yx[k], "wait_send")()
    for t in range(n_half):
        each(hand[t] + store[t], "wait")()


def write_out(e_ref, h_ref, elec_out, magn_out, held, in_sem, out_sem):
    refs = ((e_ref, elec_out), (h_ref, magn_out))
    parts = [(i, c) for i in range(2) for c in range(3)]
    into = [pltpu.make_async_copy(refs[i][0].at[c], held.at[i, c], in_sem.at[i, c]) for i, c in parts]
    back = [pltpu.make_async_copy(held.at[i, c], refs[i][1].at[c], out_sem.at[i, c]) for i, c in parts]
    for copy in into:
        copy.start()
    for first, second in zip(into, back):
        first.wait()
        second.start()
    for copy in back:
        copy.wait()


def shards(sizes, electric, magnetic, aux_state, material, kerr_strength):
    _, planes, cols, rows = electric.shape
    wide, deep = cols + 2 * COLS, planes + HALO
    f32 = jnp.float32
    any_space = pl.BlockSpec(memory_space=pl.ANY)
    hbm = pl.BlockSpec(memory_space=pltpu.HBM)
    shape = jax.ShapeDtypeStruct(electric.shape, f32)
    fields = pl.pallas_call(
        functools.partial(kernel, sizes),
        out_shape=(shape, shape),
        in_specs=[pl.BlockSpec(memory_space=pltpu.SMEM), hbm, hbm, hbm, hbm],
        out_specs=(any_space, any_space),
        scratch_shapes=[
            pltpu.VMEM((6, PAD + planes, wide, 2 * rows), f32),
            pltpu.VMEM((4, PML + 1, wide, 2 * rows), f32),
            pltpu.VMEM((wide, 2 * rows), f32),
            pltpu.VMEM((wide, 2 * rows), f32),
            pltpu.VMEM((wide, 2 * rows), f32),
            pltpu.VMEM((cols, rows), jnp.int32),
            pltpu.VMEM((6, planes, cols, rows), f32),
            pltpu.VMEM((2, planes // 2, 6, 2 * COLS, rows), f32),
            pltpu.VMEM((2, PML // 2, 4, 2 * COLS, rows), f32),
            pltpu.VMEM((2, 2 * COLS, rows), f32),
            pltpu.VMEM((2, deep // 2, 6, 2 * COLS, 2 * rows), f32),
            pltpu.VMEM((2, PML // 2, 4, 2 * COLS, 2 * rows), f32),
            pltpu.VMEM((2, 2 * COLS, 2 * rows), f32),
            pltpu.SemaphoreType.DMA((16,)),
            pltpu.SemaphoreType.DMA((40,)),
            pltpu.SemaphoreType.DMA((40,)),
            pltpu.SemaphoreType.DMA((8,)),
            pltpu.SemaphoreType.DMA((8, 2)),
        ],
        compiler_params=pltpu.CompilerParams(
            collective_id=0, has_side_effects=True, vmem_limit_bytes=60 * 2**20
        ),
    )(kerr_strength, electric, magnetic, aux_state, material)
    return pl.pallas_call(
        write_out,
        out_shape=(shape, shape),
        in_specs=[any_space, any_space],
        out_specs=(hbm, hbm),
        scratch_shapes=[
            pltpu.VMEM((2,) + electric.shape, f32),
            pltpu.SemaphoreType.DMA((2, 3)),
            pltpu.SemaphoreType.DMA((2, 3)),
        ],
        compiler_params=pltpu.CompilerParams(vmem_limit_bytes=60 * 2**20),
    )(*fields)


def solution(mesh):
    sizes = tuple(mesh.shape[axis] for axis in ("gz", "gx", "gy"))
    in_specs = (
        P(None, "gz", "gx", "gy"),
        P(None, "gz", "gx", "gy"),
        P(None, None, None, "gx", "gy"),
        P("gx", "gy"),
        P(),
    )
    out_specs = (P(None, "gz", "gx", "gy"), P(None, "gz", "gx", "gy"))
    return jax.shard_map(
        functools.partial(shards, sizes),
        mesh=mesh, in_specs=in_specs, out_specs=out_specs, check_vma=False,
    )
```

```python
import functools

import jax
import jax.numpy as jnp
import numpy as np
from jax import lax
from jax.experimental import pallas as pl
from jax.experimental.pallas import tpu as pltpu
from jax.sharding import PartitionSpec as P

PML = 8
STEPS = 4
HALO = 2 * STEPS
COLS = STEPS
PAD = 4
GROUP = SPAN = 4
STRIDE = 2
PAIRS = SPAN // 2
AHEAD = 2

courant = 0.5
pml_rate = 3.0
eps_clad = 2.085
eps_core = 4.0

MESH = pl.DeviceIdType.MESH
DEPTH_RATES = [
    float(np.exp(np.float32(-pml_rate) * np.float32((m + 1) / PML) ** 3)) for m in range(PML)
]


def kernel(
    sizes,
    kerr_ref, elec, magn, aux, material,
    elec_out, magn_out,
    F, A, eps_ref, kap_ref, mat, mat_own, own_fields,
    pack, pack_aux, pack_mat,
    halo, halo_aux, halo_mat,
    local_sem, send_sem, recv_sem, z_send_sem, z_recv_sem,
):
    n_gz, n_gx, n_gy = sizes
    planes, cols, rows = elec.shape[1:]
    wide = cols + 2 * COLS
    half = planes // 2
    quads = half // 2
    pairs = planes // 2
    gz, gx, gy = lax.axis_index("gz"), lax.axis_index("gx"), lax.axis_index("gy")
    low_part, high_part = gy == 0, gy == 1
    has_pred = gz > 0
    takes_z = jnp.logical_and(high_part, gz < n_gz - 1)
    at_front, at_back = gz == 0, gz == n_gz - 1
    at_edge = jnp.logical_or(at_front, at_back)
    left = {"gx": lax.rem(gx + n_gx - 1, n_gx)}
    right = {"gx": lax.rem(gx + 1, n_gx)}
    other = {"gy": 1 - gy}
    pred = {"gz": jnp.maximum(gz - 1, 0), "gy": 1}
    succ = [{"gz": jnp.minimum(gz + 1, n_gz - 1), "gy": part} for part in (0, 1)]
    own, far = 0, 1
    back_high = jnp.logical_and(at_back, high_part)
    start = half * gy
    side = jnp.where(at_front, 0, 1)
    args = ((0, elec), (3, magn))

    def fields(lo, at, n, width, part):
        return F.at[part, pl.ds(lo, 3), pl.ds(PAD + at, n), pl.ds(0, width)]

    def when(condition, work):
        pl.when(condition)(work)

    def each(copies, method):
        def work():
            for copy in copies:
                getattr(copy, method)()

        return work

    count = [0]

    def local(src, dst):
        count[0] += 1
        return pltpu.make_async_copy(src, dst, local_sem.at[count[0] - 1])

    stage_low = [local(r.at[:, pl.ds(0, half)], own_fields.at[pl.ds(lo, 3), pl.ds(0, half)]) for lo, r in args]
    stage_high = [local(r.at[:, pl.ds(half, half)], own_fields.at[pl.ds(lo, 3), pl.ds(half, half)]) for lo, r in args]
    load_mat = local(material, mat_own)
    load_aux = local(aux.at[:, side], A.at[own, :, pl.ds(0, PML), pl.ds(0, cols)])
    load_low = [local(r.at[:, pl.ds(0, half)], fields(lo, 0, half, cols, own)) for lo, r in args]
    load_high = [local(r.at[:, pl.ds(half, half)], fields(lo, half - start, half, cols, own)) for lo, r in args]
    for copy in stage_low + stage_high + [load_mat]:
        copy.start()
    when(at_edge, each([load_aux], "start"))
    when(low_part, each(load_low, "start"))
    each(load_high, "start")()

    barrier = pltpu.get_barrier_semaphore()

    def greet(peers):
        def work():
            for peer in peers:
                pl.semaphore_signal(barrier, inc=1, device_id=peer, device_id_type=MESH)

        return work

    greet([left, right, other])()
    when(has_pred, greet([pred]))
    when(takes_z, greet(succ))

    numbered = [0]

    def remote(src, dst, peer):
        at = numbered[0]
        numbered[0] += 1
        return pltpu.make_async_remote_copy(
            src_ref=src, dst_ref=dst, send_sem=send_sem.at[at], recv_sem=recv_sem.at[at],
            device_id=peer, device_id_type=MESH,
        )

    z_numbered = [0]

    def z_remote(src, dst, sender):
        at = z_numbered[0]
        z_numbered[0] += 1
        return pltpu.make_async_remote_copy(
            src_ref=src, dst_ref=dst, send_sem=z_send_sem.at[at], recv_sem=z_recv_sem.at[at, sender],
            device_id=pred, device_id_type=MESH,
        )

    def staged(lo, at, n):
        return own_fields.at[pl.ds(lo, 3), pl.ds(at, n)]

    def tiles(d, at, n, part):
        return halo.at[part, d, pl.ds(at, n)]

    both = ((0, left), (1, right))
    chunks = [(k * PAIRS, PAIRS) for k in range(pairs // PAIRS)]
    x_halo = [[remote(pack.at[d, pl.ds(at, n)], tiles(d, at, n, own), p) for d, p in both] for at, n in chunks]
    x_mat = [remote(pack_mat.at[d], halo_mat.at[own, d], p) for d, p in both]
    x_aux = [remote(pack_aux.at[d], halo_aux.at[own, d], p) for d, p in both]
    y_low = [remote(staged(lo, 0, half), fields(lo, 0, half, cols, far), other) for lo, r in args]
    y_high = [remote(staged(lo, half, half), fields(lo, start, half, cols, far), other) for lo, r in args]
    yx = [[remote(tiles(d, at, n, own), tiles(d, at, n, far), other) for d in (0, 1)] for at, n in chunks]
    y_aux = [remote(A.at[own, :, pl.ds(0, PML), pl.ds(0, cols)], A.at[far, :, pl.ds(0, PML), pl.ds(0, cols)], other)]
    yx_aux = [remote(halo_aux.at[own, d], halo_aux.at[far, d], other) for d in (0, 1)]
    y_mat = [remote(mat.at[own, pl.ds(0, cols)], mat.at[far, pl.ds(0, cols)], other)]
    yx_mat = [remote(halo_mat.at[own, d], halo_mat.at[far, d], other) for d in (0, 1)]

    def z_copies(sender, part):
        z_numbered[0] = 0
        sent, passed = [], []
        for k in range(half // SPAN):
            sent.append([
                z_remote(staged(lo, k * SPAN, SPAN), fields(lo, half + k * SPAN, SPAN, cols, part), sender)
                for lo, r in args
            ])
            at, n = chunks[k]
            passed.append([z_remote(tiles(d, at, n, own), tiles(d, pairs + at, n, part), sender) for d in (0, 1)])
        return sent, passed

    z_own, z_passed = z_copies(gy, 1 - gy)
    z_from = [z_copies(0, far), z_copies(1, own)]

    def pack_pair(q, carry):
        for c in range(6):
            pack[0, q, c, 0:COLS] = own_fields[c, 2 * q, 0:COLS]
            pack[0, q, c, COLS:] = own_fields[c, 2 * q + 1, 0:COLS]
            pack[1, q, c, 0:COLS] = own_fields[c, 2 * q + 1, cols - COLS : cols]
            pack[1, q, c, COLS:] = own_fields[c, 2 * q, cols - COLS : cols]
        return carry

    def pack_aux_pair(q, carry):
        for c in range(4):
            pack_aux[0, q, c, 0:COLS] = A[0, c, 2 * q, 0:COLS]
            pack_aux[0, q, c, COLS:] = A[0, c, 2 * q + 1, 0:COLS]
            pack_aux[1, q, c, 0:COLS] = A[0, c, 2 * q + 1, cols - COLS : cols]
            pack_aux[1, q, c, COLS:] = A[0, c, 2 * q, cols - COLS : cols]
        return carry

    load_mat.wait()
    m = (mat_own[...] == 1).astype(jnp.float32)
    mat[0, 0:cols] = m
    pack_mat[0] = m[0 : 2 * COLS]
    pack_mat[1] = m[cols - 2 * COLS : cols]
    each(stage_low, "wait")()
    lax.fori_loop(0, quads, pack_pair, 0)
    each(stage_high, "wait")()
    lax.fori_loop(quads, pairs, pack_pair, 0)

    @pl.when(at_edge)
    def _():
        load_aux.wait()
        lax.fori_loop(0, PML // 2, pack_aux_pair, 0)

    pl.semaphore_wait(barrier, 3 + has_pred.astype(jnp.int32) + 2 * takes_z.astype(jnp.int32))

    when(has_pred, each(z_own[0], "start"))
    each(x_mat + y_mat, "start")()
    when(at_front, each(x_aux + y_aux, "start"))
    for k in range(AHEAD):
        each(x_halo[k], "start")()
    when(high_part, each(y_low, "start"))
    each(y_high, "start")()

    def clear(lo, n):
        def plane(a, carry):
            for h in range(2):
                for c in range(6):
                    F[h, c, a] = jnp.zeros((wide, rows), jnp.float32)
            return carry

        lax.fori_loop(lo, lo + n, plane, 0)

    clear(0, PAD)
    for h in range(2):
        for c in range(4):
            A[h, c, PML] = jnp.zeros((wide, rows), jnp.float32)
    when(jnp.logical_and(at_back, high_part), lambda: clear(PAD + half, half))

    def joined(r, l):
        low = lax.broadcasted_iota(jnp.int32, (2 * COLS, rows), 0) < COLS
        return jnp.where(low, r, l), pltpu.roll(jnp.where(low, l, r), COLS, 0)

    def unpack(q, carry):
        at = PAD + 2 * q - start
        for h in range(2):
            for c in range(6):
                F[h, c, at, cols:wide], F[h, c, at + 1, cols:wide] = joined(halo[h, 0, q, c], halo[h, 1, q, c])
        return carry

    def unpack_aux(q, carry):
        for h in range(2):
            for c in range(4):
                A[h, c, 2 * q, cols:wide], A[h, c, 2 * q + 1, cols:wide] = joined(
                    halo_aux[h, 0, q, c], halo_aux[h, 1, q, c]
                )
        return carry

    nx, ny = wide - 1, 2 * rows - 1

    def whole(ref, c, at):
        return jnp.concatenate([ref[0, c, at], ref[1, c, at]], 1)

    def put(ref, c, at, value):
        ref[0, c, at] = value[:, 0:rows]
        ref[1, c, at] = value[:, rows:]

    def steps(base, s, absorbing):
        known = {}

        def load(c, at):
            return known[c, at] if (c, at) in known else whole(F, c, base + at)

        def advance(i):
            low = -i
            E = [[load(c, low + p) for c in range(3)] for p in range(GROUP + 1)]
            H = [[load(c, low + p) for c in range(3, 6)] for p in range(GROUP)]
            before = load(3, low - 1), load(4, low - 1)
            rates = []
            if absorbing:
                shift = PAD + s + i + jnp.where(at_front, 0, planes - PML) - start
                for p in range(GROUP):
                    k = base + low + p - shift
                    inside = jnp.logical_and(k >= 0, k < PML)
                    m = jnp.where(at_front, PML - 1 - k, k)
                    b = jnp.float32(1.0)
                    for j in range(PML):
                        b = jnp.where(m == j, jnp.float32(DEPTH_RATES[j]), b)
                    beyond = jnp.logical_and(back_high, base + low + p >= PAD + half + s + i)
                    rates.append((jnp.where(inside, k, PML), b, beyond))
            new_states = []
            states = [[whole(A, c, at) for c in range(4)] for at, _, _ in rates]

            def absorb(c, p, g):
                if not absorbing:
                    return g
                at, b, _ = rates[p]
                g_new = b * (g + states[p][c])
                new_states.append((c, at, g_new - g))
                return g_new

            new_h, new_e = [], []
            for p in range(GROUP):
                ex, ey, ez = E[p]
                slope_y = absorb(0, p, E[p + 1][1] - ey)
                slope_x = absorb(1, p, E[p + 1][0] - ex)
                hx = H[p][0] - courant * ((pltpu.roll(ez, ny, 1) - ez) - slope_y)
                hy = H[p][1] - courant * (slope_x - (pltpu.roll(ez, nx, 0) - ez))
                hz = H[p][2] - courant * ((pltpu.roll(ey, nx, 0) - ey) - (pltpu.roll(ex, ny, 1) - ex))
                new_h.append((hx, hy, hz))
            for p in range(GROUP):
                ex, ey, ez = E[p]
                hx, hy, hz = new_h[p]
                below = before if p == 0 else new_h[p - 1]
                factor = courant / (eps_ref[...] + kap_ref[...] * (ex * ex + ey * ey + ez * ez))
                if absorbing:
                    factor = jnp.where(rates[p][2], 0.0, factor)
                slope_hy = absorb(2, p, hy - below[1])
                slope_hx = absorb(3, p, hx - below[0])
                new_e.append((
                    ex + factor * ((hz - pltpu.roll(hz, 1, 1)) - slope_hy),
                    ey + factor * (slope_hx - (hz - pltpu.roll(hz, 1, 0))),
                    ez + factor * ((hy - pltpu.roll(hy, 1, 0)) - (hx - pltpu.roll(hx, 1, 1))),
                ))
            for p in range(GROUP):
                for c, value in enumerate(new_e[p] + new_h[p]):
                    known[c, low + p] = value
                    put(F, c, base + low + p, value)
            for c, at, value in new_states:
                put(A, c, at, value)

        for i in range(STRIDE):
            advance(i)

    def arrive(k):
        each(x_halo[k], "wait")()
        if k == 0:
            when(at_back, each(x_aux + y_aux, "start"))
        if k + AHEAD < len(x_halo):
            each(x_halo[k + AHEAD], "start")()
        if k < half // SPAN:
            when(has_pred, each(z_passed[k], "start"))
            if k + 1 < half // SPAN:
                when(has_pred, each(z_own[k + 1], "start"))
            when(high_part, each(yx[k], "start"))
        else:
            each(yx[k], "start")()

    def pass_aux():
        each(x_aux, "wait")()
        each(yx_aux, "start")()

    def take_aux():
        each(y_aux + yx_aux, "wait")()
        lax.fori_loop(0, PML // 2, unpack_aux, 0)

    n_half = half // SPAN
    each(x_mat, "wait")()
    each(yx_mat, "start")()
    when(at_front, pass_aux)

    @pl.when(high_part)
    def _():
        for k in range(n_half):
            arrive(k)

    when(back_high, pass_aux)
    each(y_mat + yx_mat, "wait")()
    low = lax.broadcasted_iota(jnp.int32, (2 * COLS, rows), 0) < COLS
    for h in range(2):
        mat[h, cols:wide] = jnp.where(low, halo_mat[h, 0], halo_mat[h, 1])
    core = jnp.concatenate([mat[0], mat[1]], 1) > 0.5
    eps_ref[...] = jnp.where(core, jnp.float32(eps_core), jnp.float32(eps_clad))
    kap_ref[...] = jnp.where(core, kerr_ref[1], kerr_ref[0])

    results = ((0, elec_out), (3, magn_out))
    store, hand = [], []
    for t in range(n_half):
        there = [r.at[:, pl.ds(start + t * SPAN, SPAN)] for _, r in results]
        store.append([local(fields(lo, STEPS + t * SPAN, SPAN, cols, own), r) for (lo, _), r in zip(results, there)])
        hand.append([remote(fields(lo, STEPS + t * SPAN, SPAN, cols, far), r, other) for (lo, _), r in zip(results, there)])

    def prepare(j):
        @pl.when(low_part)
        def _():
            if j == 0:
                each(load_low, "wait")()
            if j == n_half:
                each(load_high, "wait")()
                when(at_back, pass_aux)
            arrive(j)
            if j == 0:
                each(y_low, "wait_recv")()
                when(at_front, take_aux)
            if j == n_half:
                each(y_high, "wait_recv")()
                when(at_back, take_aux)
            each(yx[j], "wait_recv")()

        if j < n_half:
            @pl.when(high_part)
            def _():
                if j == 0:
                    each(load_high, "wait")()
                arrive(j + n_half)
                if j == 0:
                    each(y_high, "wait_recv")()
                    when(at_edge, take_aux)
                each(yx[j + n_half], "wait_recv")()
        else:
            @pl.when(takes_z)
            def _():
                for sent, passed in z_from:
                    each(sent[j - n_half] + passed[j - n_half], "wait_recv")()

    def stage(j, carry):
        for k in range(2 * n_half):
            when(j == k, functools.partial(prepare, k))

        @pl.when(jnp.logical_not(jnp.logical_and(back_high, j >= n_half)))
        def _():
            at = quads * gy + PAIRS * j
            lax.fori_loop(at, at + PAIRS, unpack, 0)

        def some_steps(r, carry):
            s = STRIDE * r
            base = PAD + SPAN * j - 1 - s
            when(at_edge, lambda: steps(base, s, True))
            when(jnp.logical_not(at_edge), lambda: steps(base, s, False))
            return carry

        lax.fori_loop(0, jnp.where(j == 0, STEPS // 2, STEPS) // STRIDE, some_steps, 0)
        for t in range(n_half):
            when(j == t + n_half, each(hand[t] + store[t], "start"))
        return carry

    lax.fori_loop(0, 2 * n_half, stage, 0)

    @pl.when(has_pred)
    def _():
        for k in range(n_half):
            each(z_own[k] + z_passed[k], "wait_send")()

    @pl.when(high_part)
    def _():
        each(y_low, "wait_send")()
        for k in range(n_half):
            each(yx[k], "wait_send")()

    each(y_high, "wait_send")()
    for k in range(n_half, 2 * n_half):
        each(yx[k], "wait_send")()
    for t in range(n_half):
        each(hand[t] + store[t], "wait")()


def write_out(e_ref, h_ref, elec_out, magn_out, held, in_sem, out_sem):
    refs = ((e_ref, elec_out), (h_ref, magn_out))
    parts = [(i, c) for i in range(2) for c in range(3)]
    into = [pltpu.make_async_copy(refs[i][0].at[c], held.at[i, c], in_sem.at[i, c]) for i, c in parts]
    back = [pltpu.make_async_copy(held.at[i, c], refs[i][1].at[c], out_sem.at[i, c]) for i, c in parts]
    for copy in into:
        copy.start()
    for first, second in zip(into, back):
        first.wait()
        second.start()
    for copy in back:
        copy.wait()


def shards(sizes, electric, magnetic, aux_state, material, kerr_strength):
    _, planes, cols, rows = electric.shape
    wide, deep = cols + 2 * COLS, planes + HALO
    f32 = jnp.float32
    any_space = pl.BlockSpec(memory_space=pl.ANY)
    hbm = pl.BlockSpec(memory_space=pltpu.HBM)
    shape = jax.ShapeDtypeStruct(electric.shape, f32)
    fields = pl.pallas_call(
        functools.partial(kernel, sizes),
        out_shape=(shape, shape),
        in_specs=[pl.BlockSpec(memory_space=pltpu.SMEM), hbm, hbm, hbm, hbm],
        out_specs=(any_space, any_space),
        scratch_shapes=[
            pltpu.VMEM((2, 6, PAD + planes, wide, rows), f32),
            pltpu.VMEM((2, 4, PML + 1, wide, rows), f32),
            pltpu.VMEM((wide, 2 * rows), f32),
            pltpu.VMEM((wide, 2 * rows), f32),
            pltpu.VMEM((2, wide, rows), f32),
            pltpu.VMEM((cols, rows), jnp.int32),
            pltpu.VMEM((6, planes, cols, rows), f32),
            pltpu.VMEM((2, planes // 2, 6, 2 * COLS, rows), f32),
            pltpu.VMEM((2, PML // 2, 4, 2 * COLS, rows), f32),
            pltpu.VMEM((2, 2 * COLS, rows), f32),
            pltpu.VMEM((2, 2, deep // 2, 6, 2 * COLS, rows), f32),
            pltpu.VMEM((2, 2, PML // 2, 4, 2 * COLS, rows), f32),
            pltpu.VMEM((2, 2, 2 * COLS, rows), f32),
            pltpu.SemaphoreType.DMA((16,)),
            pltpu.SemaphoreType.DMA((40,)),
            pltpu.SemaphoreType.DMA((40,)),
            pltpu.SemaphoreType.DMA((8,)),
            pltpu.SemaphoreType.DMA((8, 2)),
        ],
        compiler_params=pltpu.CompilerParams(
            collective_id=0, has_side_effects=True, vmem_limit_bytes=60 * 2**20
        ),
    )(kerr_strength, electric, magnetic, aux_state, material)
    return pl.pallas_call(
        write_out,
        out_shape=(shape, shape),
        in_specs=[any_space, any_space],
        out_specs=(hbm, hbm),
        scratch_shapes=[
            pltpu.VMEM((2,) + electric.shape, f32),
            pltpu.SemaphoreType.DMA((2, 3)),
            pltpu.SemaphoreType.DMA((2, 3)),
        ],
        compiler_params=pltpu.CompilerParams(vmem_limit_bytes=60 * 2**20),
    )(*fields)


def solution(mesh):
    sizes = tuple(mesh.shape[axis] for axis in ("gz", "gx", "gy"))
    in_specs = (
        P(None, "gz", "gx", "gy"),
        P(None, "gz", "gx", "gy"),
        P(None, None, None, "gx", "gy"),
        P("gx", "gy"),
        P(),
    )
    out_specs = (P(None, "gz", "gx", "gy"), P(None, "gz", "gx", "gy"))
    return jax.shard_map(
        functools.partial(shards, sizes),
        mesh=mesh, in_specs=in_specs, out_specs=out_specs, check_vma=False,
    )
```

```python
import functools

import jax
import jax.numpy as jnp
import numpy as np
from jax import lax
from jax.experimental import pallas as pl
from jax.experimental.pallas import tpu as pltpu
from jax.sharding import PartitionSpec as P

PML = 8
STEPS = 4
HALO = 2 * STEPS
COLS = STEPS
LEAD = 8
PAD = 4
GROUP = SPAN = 4
STRIDE = 2
PAIRS = SPAN // 2
AHEAD = 2

courant = 0.5
pml_rate = 3.0
eps_clad = 2.085
eps_core = 4.0

MESH = pl.DeviceIdType.MESH
DEPTH_RATES = [
    float(np.exp(np.float32(-pml_rate) * np.float32((m + 1) / PML) ** 3)) for m in range(PML)
]


def kernel(
    sizes,
    kerr_ref, elec, magn, aux, material,
    elec_out, magn_out,
    F, A, eps_ref, kap_ref, mat, mat_own, own_fields,
    pack, pack_aux, pack_mat,
    halo, halo_aux, halo_mat,
    local_sem, send_sem, recv_sem, z_send_sem, z_recv_sem,
):
    n_gz, n_gx, n_gy = sizes
    planes, cols, rows = elec.shape[1:]
    wide = cols + 2 * COLS
    half = planes // 2
    quads = half // 2
    pairs = planes // 2
    gz, gx, gy = lax.axis_index("gz"), lax.axis_index("gx"), lax.axis_index("gy")
    low_part, high_part = gy == 0, gy == 1
    has_pred = gz > 0
    takes_z = jnp.logical_and(high_part, gz < n_gz - 1)
    at_front, at_back = gz == 0, gz == n_gz - 1
    at_edge = jnp.logical_or(at_front, at_back)
    left = {"gx": lax.rem(gx + n_gx - 1, n_gx)}
    right = {"gx": lax.rem(gx + 1, n_gx)}
    other = {"gy": 1 - gy}
    pred = {"gz": jnp.maximum(gz - 1, 0), "gy": 1}
    succ = [{"gz": jnp.minimum(gz + 1, n_gz - 1), "gy": part} for part in (0, 1)]
    own, far = 0, 1
    back_high = jnp.logical_and(at_back, high_part)
    start = half * gy
    side = jnp.where(at_front, 0, 1)
    args = ((0, elec), (3, magn))

    def fields(lo, at, n, width, part):
        return F.at[part, pl.ds(lo, 3), pl.ds(PAD + at, n), pl.ds(LEAD, width)]

    def when(condition, work):
        pl.when(condition)(work)

    def each(copies, method):
        def work():
            for copy in copies:
                getattr(copy, method)()

        return work

    count = [0]

    def local(src, dst):
        count[0] += 1
        return pltpu.make_async_copy(src, dst, local_sem.at[count[0] - 1])

    stage_low = [local(r.at[:, pl.ds(0, half)], own_fields.at[pl.ds(lo, 3), pl.ds(0, half)]) for lo, r in args]
    stage_high = [local(r.at[:, pl.ds(half, half)], own_fields.at[pl.ds(lo, 3), pl.ds(half, half)]) for lo, r in args]
    load_mat = local(material, mat_own)
    load_aux = local(aux.at[:, side], A.at[own, :, pl.ds(0, PML), pl.ds(0, cols)])
    load_low = [local(r.at[:, pl.ds(0, half)], fields(lo, 0, half, cols, own)) for lo, r in args]
    load_high = [local(r.at[:, pl.ds(half, half)], fields(lo, half - start, half, cols, own)) for lo, r in args]
    for copy in stage_low + stage_high + [load_mat]:
        copy.start()
    when(at_edge, each([load_aux], "start"))
    when(low_part, each(load_low, "start"))
    each(load_high, "start")()

    barrier = pltpu.get_barrier_semaphore()

    def greet(peers):
        def work():
            for peer in peers:
                pl.semaphore_signal(barrier, inc=1, device_id=peer, device_id_type=MESH)

        return work

    greet([left, right, other])()
    when(has_pred, greet([pred]))
    when(takes_z, greet(succ))

    numbered = [0]

    def remote(src, dst, peer):
        at = numbered[0]
        numbered[0] += 1
        return pltpu.make_async_remote_copy(
            src_ref=src, dst_ref=dst, send_sem=send_sem.at[at], recv_sem=recv_sem.at[at],
            device_id=peer, device_id_type=MESH,
        )

    z_numbered = [0]

    def z_remote(src, dst, sender):
        at = z_numbered[0]
        z_numbered[0] += 1
        return pltpu.make_async_remote_copy(
            src_ref=src, dst_ref=dst, send_sem=z_send_sem.at[at], recv_sem=z_recv_sem.at[at, sender],
            device_id=pred, device_id_type=MESH,
        )

    def staged(lo, at, n):
        return own_fields.at[pl.ds(lo, 3), pl.ds(at, n)]

    def tiles(d, at, n, part):
        return halo.at[part, d, pl.ds(at, n)]

    both = ((0, left), (1, right))
    chunks = [(k * PAIRS, PAIRS) for k in range(pairs // PAIRS)]
    x_halo = [[remote(pack.at[d, pl.ds(at, n)], tiles(d, at, n, own), p) for d, p in both] for at, n in chunks]
    x_mat = [remote(pack_mat.at[d], halo_mat.at[own, d], p) for d, p in both]
    x_aux = [remote(pack_aux.at[d], halo_aux.at[own, d], p) for d, p in both]
    y_low = [remote(staged(lo, 0, half), fields(lo, 0, half, cols, far), other) for lo, r in args]
    y_high = [remote(staged(lo, half, half), fields(lo, start, half, cols, far), other) for lo, r in args]
    yx = [[remote(tiles(d, at, n, own), tiles(d, at, n, far), other) for d in (0, 1)] for at, n in chunks]
    y_aux = [remote(A.at[own, :, pl.ds(0, PML), pl.ds(0, cols)], A.at[far, :, pl.ds(0, PML), pl.ds(0, cols)], other)]
    yx_aux = [remote(halo_aux.at[own, d], halo_aux.at[far, d], other) for d in (0, 1)]
    y_mat = [remote(mat.at[own, pl.ds(0, cols)], mat.at[far, pl.ds(0, cols)], other)]
    yx_mat = [remote(halo_mat.at[own, d], halo_mat.at[far, d], other) for d in (0, 1)]

    def z_copies(sender, part):
        z_numbered[0] = 0
        sent, passed = [], []
        for k in range(half // SPAN):
            sent.append([
                z_remote(staged(lo, k * SPAN, SPAN), fields(lo, half + k * SPAN, SPAN, cols, part), sender)
                for lo, r in args
            ])
            at, n = chunks[k]
            passed.append([z_remote(tiles(d, at, n, own), tiles(d, pairs + at, n, part), sender) for d in (0, 1)])
        return sent, passed

    z_own, z_passed = z_copies(gy, 1 - gy)
    z_from = [z_copies(0, far), z_copies(1, own)]

    def pack_pair(q, carry):
        for c in range(6):
            pack[0, q, c, 0:COLS] = own_fields[c, 2 * q, 0:COLS]
            pack[0, q, c, COLS:] = own_fields[c, 2 * q + 1, 0:COLS]
            pack[1, q, c, 0:COLS] = own_fields[c, 2 * q + 1, cols - COLS : cols]
            pack[1, q, c, COLS:] = own_fields[c, 2 * q, cols - COLS : cols]
        return carry

    def pack_aux_pair(q, carry):
        for c in range(4):
            pack_aux[0, q, c, 0:COLS] = A[0, c, 2 * q, 0:COLS]
            pack_aux[0, q, c, COLS:] = A[0, c, 2 * q + 1, 0:COLS]
            pack_aux[1, q, c, 0:COLS] = A[0, c, 2 * q + 1, cols - COLS : cols]
            pack_aux[1, q, c, COLS:] = A[0, c, 2 * q, cols - COLS : cols]
        return carry

    load_mat.wait()
    m = (mat_own[...] == 1).astype(jnp.float32)
    mat[0, 0:cols] = m
    pack_mat[0] = m[0 : 2 * COLS]
    pack_mat[1] = m[cols - 2 * COLS : cols]
    each(stage_low, "wait")()
    lax.fori_loop(0, quads, pack_pair, 0)
    each(stage_high, "wait")()
    lax.fori_loop(quads, pairs, pack_pair, 0)

    @pl.when(at_edge)
    def _():
        load_aux.wait()
        lax.fori_loop(0, PML // 2, pack_aux_pair, 0)

    pl.semaphore_wait(barrier, 3 + has_pred.astype(jnp.int32) + 2 * takes_z.astype(jnp.int32))

    when(has_pred, each(z_own[0], "start"))
    each(x_mat + y_mat, "start")()
    when(at_front, each(x_aux + y_aux, "start"))
    for k in range(AHEAD):
        each(x_halo[k], "start")()
    when(high_part, each(y_low, "start"))
    each(y_high, "start")()

    def clear(lo, n):
        def plane(a, carry):
            for h in range(2):
                for c in range(6):
                    F[h, c, a] = jnp.zeros((LEAD + wide + LEAD, rows), jnp.float32)
            return carry

        lax.fori_loop(lo, lo + n, plane, 0)

    clear(0, PAD)
    for h in range(2):
        for c in range(4):
            A[h, c, PML] = jnp.zeros((wide, rows), jnp.float32)
    when(jnp.logical_and(at_back, high_part), lambda: clear(PAD + half, half))

    def joined(r, l):
        low = lax.broadcasted_iota(jnp.int32, (2 * COLS, rows), 0) < COLS
        return jnp.where(low, r, l), pltpu.roll(jnp.where(low, l, r), COLS, 0)

    def unpack(q, carry):
        at = PAD + 2 * q - start
        for h in range(2):
            for c in range(6):
                halves = joined(halo[h, 0, q, c], halo[h, 1, q, c])
                for i in range(2):
                    F[h, c, at + i, LEAD + cols : LEAD + wide] = halves[i]
                    if c in (1, 2):
                        F[h, c, at + i, LEAD + wide : LEAD + wide + 1] = F[h, c, at + i, LEAD : LEAD + 1]
        return carry

    def unpack_aux(q, carry):
        for h in range(2):
            for c in range(4):
                A[h, c, 2 * q, cols:wide], A[h, c, 2 * q + 1, cols:wide] = joined(
                    halo_aux[h, 0, q, c], halo_aux[h, 1, q, c]
                )
        return carry

    ny = 2 * rows - 1

    def whole(ref, c, at):
        return jnp.concatenate([ref[0, c, at], ref[1, c, at]], 1)

    def put(ref, c, at, value):
        ref[0, c, at] = value[:, 0:rows]
        ref[1, c, at] = value[:, rows:]

    def plane_of(c, at, by=0):
        first = LEAD + by
        return jnp.concatenate([F[h, c, at, first : first + wide] for h in range(2)], 1)

    def put_plane(c, at, value):
        for h in range(2):
            part = value[:, h * rows : (h + 1) * rows]
            F[h, c, at, LEAD : LEAD + wide] = part
            if c in (1, 2):
                F[h, c, at, LEAD + wide : LEAD + wide + 1] = part[0:1]
            if c in (4, 5):
                F[h, c, at, LEAD - 1 : LEAD] = part[wide - 1 : wide]

    def steps(base, s, absorbing):
        known = {}

        def load(c, at):
            return known[c, at] if (c, at) in known else plane_of(c, base + at)

        def advance(i):
            low = -i
            E = [[load(c, low + p) for c in range(3)] for p in range(GROUP + 1)]
            H = [[load(c, low + p) for c in range(3, 6)] for p in range(GROUP)]
            before = load(3, low - 1), load(4, low - 1)
            ahead = [[plane_of(c, base + low + p, 1) for c in (1, 2)] for p in range(GROUP)]
            rates = []
            if absorbing:
                shift = PAD + s + i + jnp.where(at_front, 0, planes - PML) - start
                for p in range(GROUP):
                    k = base + low + p - shift
                    inside = jnp.logical_and(k >= 0, k < PML)
                    m = jnp.where(at_front, PML - 1 - k, k)
                    b = jnp.float32(1.0)
                    for j in range(PML):
                        b = jnp.where(m == j, jnp.float32(DEPTH_RATES[j]), b)
                    beyond = jnp.logical_and(back_high, base + low + p >= PAD + half + s + i)
                    rates.append((jnp.where(inside, k, PML), b, beyond))
            new_states = []
            states = [[whole(A, c, at) for c in range(4)] for at, _, _ in rates]

            def absorb(c, p, g):
                if not absorbing:
                    return g
                at, b, _ = rates[p]
                g_new = b * (g + states[p][c])
                new_states.append((c, at, g_new - g))
                return g_new

            new_h, new_e = [], []
            for p in range(GROUP):
                ex, ey, ez = E[p]
                slope_y = absorb(0, p, E[p + 1][1] - ey)
                slope_x = absorb(1, p, E[p + 1][0] - ex)
                hx = H[p][0] - courant * ((pltpu.roll(ez, ny, 1) - ez) - slope_y)
                hy = H[p][1] - courant * (slope_x - (ahead[p][1] - ez))
                hz = H[p][2] - courant * ((ahead[p][0] - ey) - (pltpu.roll(ex, ny, 1) - ex))
                new_h.append((hx, hy, hz))
                for c in range(3):
                    put_plane(3 + c, base + low + p, new_h[p][c])
            for p in range(GROUP):
                ex, ey, ez = E[p]
                hx, hy, hz = new_h[p]
                below = before if p == 0 else new_h[p - 1]
                hy_b, hz_b = plane_of(4, base + low + p, -1), plane_of(5, base + low + p, -1)
                factor = courant / (eps_ref[...] + kap_ref[...] * (ex * ex + ey * ey + ez * ez))
                if absorbing:
                    factor = jnp.where(rates[p][2], 0.0, factor)
                slope_hy = absorb(2, p, hy - below[1])
                slope_hx = absorb(3, p, hx - below[0])
                new_e.append((
                    ex + factor * ((hz - pltpu.roll(hz, 1, 1)) - slope_hy),
                    ey + factor * (slope_hx - (hz - hz_b)),
                    ez + factor * ((hy - hy_b) - (hx - pltpu.roll(hx, 1, 1))),
                ))
            for p in range(GROUP):
                for c, value in enumerate(new_e[p] + new_h[p]):
                    known[c, low + p] = value
                    if c < 3:
                        put_plane(c, base + low + p, value)
            for c, at, value in new_states:
                put(A, c, at, value)

        for i in range(STRIDE):
            advance(i)

    def arrive(k):
        each(x_halo[k], "wait")()
        if k == 0:
            when(at_back, each(x_aux + y_aux, "start"))
        if k + AHEAD < len(x_halo):
            each(x_halo[k + AHEAD], "start")()
        if k < half // SPAN:
            when(has_pred, each(z_passed[k], "start"))
            if k + 1 < half // SPAN:
                when(has_pred, each(z_own[k + 1], "start"))
            when(high_part, each(yx[k], "start"))
        else:
            each(yx[k], "start")()

    def pass_aux():
        each(x_aux, "wait")()
        each(yx_aux, "start")()

    def take_aux():
        each(y_aux + yx_aux, "wait")()
        lax.fori_loop(0, PML // 2, unpack_aux, 0)

    n_half = half // SPAN
    each(x_mat, "wait")()
    each(yx_mat, "start")()
    when(at_front, pass_aux)

    @pl.when(high_part)
    def _():
        for k in range(n_half):
            arrive(k)

    when(back_high, pass_aux)
    each(y_mat + yx_mat, "wait")()
    low = lax.broadcasted_iota(jnp.int32, (2 * COLS, rows), 0) < COLS
    for h in range(2):
        mat[h, cols:wide] = jnp.where(low, halo_mat[h, 0], halo_mat[h, 1])
    core = jnp.concatenate([mat[0], mat[1]], 1) > 0.5
    eps_ref[...] = jnp.where(core, jnp.float32(eps_core), jnp.float32(eps_clad))
    kap_ref[...] = jnp.where(core, kerr_ref[1], kerr_ref[0])

    results = ((0, elec_out), (3, magn_out))
    store, hand = [], []
    for t in range(n_half):
        there = [r.at[:, pl.ds(start + t * SPAN, SPAN)] for _, r in results]
        store.append([local(fields(lo, STEPS + t * SPAN, SPAN, cols, own), r) for (lo, _), r in zip(results, there)])
        hand.append([remote(fields(lo, STEPS + t * SPAN, SPAN, cols, far), r, other) for (lo, _), r in zip(results, there)])

    def prepare(j):
        @pl.when(low_part)
        def _():
            if j == 0:
                each(load_low, "wait")()
            if j == n_half:
                each(load_high, "wait")()
                when(at_back, pass_aux)
            arrive(j)
            if j == 0:
                each(y_low, "wait_recv")()
                when(at_front, take_aux)
            if j == n_half:
                each(y_high, "wait_recv")()
                when(at_back, take_aux)
            each(yx[j], "wait_recv")()

        if j < n_half:
            @pl.when(high_part)
            def _():
                if j == 0:
                    each(load_high, "wait")()
                arrive(j + n_half)
                if j == 0:
                    each(y_high, "wait_recv")()
                    when(at_edge, take_aux)
                each(yx[j + n_half], "wait_recv")()
        else:
            @pl.when(takes_z)
            def _():
                for sent, passed in z_from:
                    each(sent[j - n_half] + passed[j - n_half], "wait_recv")()

    def stage(j, carry):
        for k in range(2 * n_half):
            when(j == k, functools.partial(prepare, k))

        @pl.when(jnp.logical_not(jnp.logical_and(back_high, j >= n_half)))
        def _():
            at = quads * gy + PAIRS * j
            lax.fori_loop(at, at + PAIRS, unpack, 0)

        def some_steps(r, carry):
            s = STRIDE * r
            base = PAD + SPAN * j - 1 - s
            when(at_edge, lambda: steps(base, s, True))
            when(jnp.logical_not(at_edge), lambda: steps(base, s, False))
            return carry

        lax.fori_loop(0, jnp.where(j == 0, STEPS // 2, STEPS) // STRIDE, some_steps, 0)
        for t in range(n_half):
            when(j == t + n_half, each(hand[t] + store[t], "start"))
        return carry

    lax.fori_loop(0, 2 * n_half, stage, 0)

    @pl.when(has_pred)
    def _():
        for k in range(n_half):
            each(z_own[k] + z_passed[k], "wait_send")()

    @pl.when(high_part)
    def _():
        each(y_low, "wait_send")()
        for k in range(n_half):
            each(yx[k], "wait_send")()

    each(y_high, "wait_send")()
    for k in range(n_half, 2 * n_half):
        each(yx[k], "wait_send")()
    for t in range(n_half):
        each(hand[t] + store[t], "wait")()


def write_out(e_ref, h_ref, elec_out, magn_out, held, in_sem, out_sem):
    refs = ((e_ref, elec_out), (h_ref, magn_out))
    parts = [(i, c) for i in range(2) for c in range(3)]
    into = [pltpu.make_async_copy(refs[i][0].at[c], held.at[i, c], in_sem.at[i, c]) for i, c in parts]
    back = [pltpu.make_async_copy(held.at[i, c], refs[i][1].at[c], out_sem.at[i, c]) for i, c in parts]
    for copy in into:
        copy.start()
    for first, second in zip(into, back):
        first.wait()
        second.start()
    for copy in back:
        copy.wait()


def shards(sizes, electric, magnetic, aux_state, material, kerr_strength):
    _, planes, cols, rows = electric.shape
    wide, deep = cols + 2 * COLS, planes + HALO
    f32 = jnp.float32
    any_space = pl.BlockSpec(memory_space=pl.ANY)
    hbm = pl.BlockSpec(memory_space=pltpu.HBM)
    shape = jax.ShapeDtypeStruct(electric.shape, f32)
    fields = pl.pallas_call(
        functools.partial(kernel, sizes),
        out_shape=(shape, shape),
        in_specs=[pl.BlockSpec(memory_space=pltpu.SMEM), hbm, hbm, hbm, hbm],
        out_specs=(any_space, any_space),
        scratch_shapes=[
            pltpu.VMEM((2, 6, PAD + planes, LEAD + wide + LEAD, rows), f32),
            pltpu.VMEM((2, 4, PML + 1, wide, rows), f32),
            pltpu.VMEM((wide, 2 * rows), f32),
            pltpu.VMEM((wide, 2 * rows), f32),
            pltpu.VMEM((2, wide, rows), f32),
            pltpu.VMEM((cols, rows), jnp.int32),
            pltpu.VMEM((6, planes, cols, rows), f32),
            pltpu.VMEM((2, planes // 2, 6, 2 * COLS, rows), f32),
            pltpu.VMEM((2, PML // 2, 4, 2 * COLS, rows), f32),
            pltpu.VMEM((2, 2 * COLS, rows), f32),
            pltpu.VMEM((2, 2, deep // 2, 6, 2 * COLS, rows), f32),
            pltpu.VMEM((2, 2, PML // 2, 4, 2 * COLS, rows), f32),
            pltpu.VMEM((2, 2, 2 * COLS, rows), f32),
            pltpu.SemaphoreType.DMA((16,)),
            pltpu.SemaphoreType.DMA((40,)),
            pltpu.SemaphoreType.DMA((40,)),
            pltpu.SemaphoreType.DMA((8,)),
            pltpu.SemaphoreType.DMA((8, 2)),
        ],
        compiler_params=pltpu.CompilerParams(
            collective_id=0, has_side_effects=True, vmem_limit_bytes=60 * 2**20
        ),
    )(kerr_strength, electric, magnetic, aux_state, material)
    return pl.pallas_call(
        write_out,
        out_shape=(shape, shape),
        in_specs=[any_space, any_space],
        out_specs=(hbm, hbm),
        scratch_shapes=[
            pltpu.VMEM((2,) + electric.shape, f32),
            pltpu.SemaphoreType.DMA((2, 3)),
            pltpu.SemaphoreType.DMA((2, 3)),
        ],
        compiler_params=pltpu.CompilerParams(vmem_limit_bytes=60 * 2**20),
    )(*fields)


def solution(mesh):
    sizes = tuple(mesh.shape[axis] for axis in ("gz", "gx", "gy"))
    in_specs = (
        P(None, "gz", "gx", "gy"),
        P(None, "gz", "gx", "gy"),
        P(None, None, None, "gx", "gy"),
        P("gx", "gy"),
        P(),
    )
    out_specs = (P(None, "gz", "gx", "gy"), P(None, "gz", "gx", "gy"))
    return jax.shard_map(
        functools.partial(shards, sizes),
        mesh=mesh, in_specs=in_specs, out_specs=out_specs, check_vma=False,
    )
```

```python
import functools

import jax
import jax.numpy as jnp
import numpy as np
from jax import lax
from jax.experimental import pallas as pl
from jax.experimental.pallas import tpu as pltpu
from jax.sharding import PartitionSpec as P

PML = 8
STEPS = 4
HALO = 2 * STEPS
COLS = STEPS
PAD = 4
GROUP = SPAN = 4
PAIRS = SPAN // 2
AHEAD = 2

courant = 0.5
pml_rate = 3.0
eps_clad = 2.085
eps_core = 4.0

MESH = pl.DeviceIdType.MESH
DEPTH_RATES = [
    float(np.exp(np.float32(-pml_rate) * np.float32((m + 1) / PML) ** 3)) for m in range(PML)
]


def kernel(
    sizes,
    kerr_ref, elec, magn, aux, material,
    elec_out, magn_out,
    F, A, eps_ref, kap_ref, mat, mat_own, own_fields, handed,
    pack, pack_aux, pack_mat,
    halo, halo_aux, halo_mat,
    local_sem, send_sem, recv_sem, z_send_sem, z_recv_sem,
):
    n_gz, n_gx, n_gy = sizes
    planes, cols, rows = elec.shape[1:]
    wide = cols + 2 * COLS
    half = planes // 2
    quads = half // 2
    pairs = planes // 2
    gz, gx, gy = lax.axis_index("gz"), lax.axis_index("gx"), lax.axis_index("gy")
    low_part, high_part = gy == 0, gy == 1
    has_pred = gz > 0
    takes_z = jnp.logical_and(high_part, gz < n_gz - 1)
    at_front, at_back = gz == 0, gz == n_gz - 1
    at_edge = jnp.logical_or(at_front, at_back)
    left = {"gx": lax.rem(gx + n_gx - 1, n_gx)}
    right = {"gx": lax.rem(gx + 1, n_gx)}
    other = {"gy": 1 - gy}
    pred = {"gz": jnp.maximum(gz - 1, 0), "gy": 1}
    succ = [{"gz": jnp.minimum(gz + 1, n_gz - 1), "gy": part} for part in (0, 1)]
    own, far = pl.ds(0, rows), pl.ds(rows, rows)
    z_lanes = pl.ds(pl.multiple_of((1 - gy) * rows, rows), rows)
    start = half * gy
    side = jnp.where(at_front, 0, 1)
    args = ((0, elec), (3, magn))

    def fields(lo, at, n, width, lanes):
        return F.at[pl.ds(lo, 3), pl.ds(PAD + at, n), pl.ds(0, width), lanes]

    def when(condition, work):
        pl.when(condition)(work)

    def each(copies, method):
        def work():
            for copy in copies:
                getattr(copy, method)()

        return work

    count = [0]

    def local(src, dst):
        count[0] += 1
        return pltpu.make_async_copy(src, dst, local_sem.at[count[0] - 1])

    stage_low = [local(r.at[:, pl.ds(0, half)], own_fields.at[pl.ds(lo, 3), pl.ds(0, half)]) for lo, r in args]
    stage_high = [local(r.at[:, pl.ds(half, half)], own_fields.at[pl.ds(lo, 3), pl.ds(half, half)]) for lo, r in args]
    load_mat = local(material, mat_own)
    load_aux = local(aux.at[:, side], A.at[:, pl.ds(0, PML), pl.ds(0, cols), own])
    load_low = [local(r.at[:, pl.ds(0, half)], fields(lo, 0, half, cols, own)) for lo, r in args]
    load_high = [local(r.at[:, pl.ds(half, half)], fields(lo, half - start, half, cols, own)) for lo, r in args]
    for copy in stage_low + stage_high + [load_mat]:
        copy.start()
    when(at_edge, each([load_aux], "start"))
    when(low_part, each(load_low, "start"))
    each(load_high, "start")()

    barrier = pltpu.get_barrier_semaphore()

    def greet(peers):
        def work():
            for peer in peers:
                pl.semaphore_signal(barrier, inc=1, device_id=peer, device_id_type=MESH)

        return work

    greet([left, right, other])()
    when(has_pred, greet([pred]))
    when(takes_z, greet(succ))

    numbered = [0]

    def remote(src, dst, peer):
        at = numbered[0]
        numbered[0] += 1
        return pltpu.make_async_remote_copy(
            src_ref=src, dst_ref=dst, send_sem=send_sem.at[at], recv_sem=recv_sem.at[at],
            device_id=peer, device_id_type=MESH,
        )

    z_numbered = [0]

    def z_remote(src, dst, sender):
        at = z_numbered[0]
        z_numbered[0] += 1
        return pltpu.make_async_remote_copy(
            src_ref=src, dst_ref=dst, send_sem=z_send_sem.at[at], recv_sem=z_recv_sem.at[at, sender],
            device_id=pred, device_id_type=MESH,
        )

    def staged(lo, at, n):
        return own_fields.at[pl.ds(lo, 3), pl.ds(at, n)]

    def tiles(d, at, n, lanes):
        return halo.at[d, pl.ds(at, n), :, :, lanes]

    both = ((0, left), (1, right))
    chunks = [(k * PAIRS, PAIRS) for k in range(pairs // PAIRS)]
    x_halo = [[remote(pack.at[d, pl.ds(at, n)], tiles(d, at, n, own), p) for d, p in both] for at, n in chunks]
    x_mat = [remote(pack_mat.at[d], halo_mat.at[d, :, own], p) for d, p in both]
    x_aux = [remote(pack_aux.at[d], halo_aux.at[d, :, :, :, own], p) for d, p in both]
    y_low = [remote(staged(lo, 0, half), fields(lo, 0, half, cols, far), other) for lo, r in args]
    y_high = [remote(staged(lo, half, half), fields(lo, start, half, cols, far), other) for lo, r in args]
    yx = [[remote(tiles(d, at, n, own), tiles(d, at, n, far), other) for d in (0, 1)] for at, n in chunks]
    y_aux = [remote(A.at[:, pl.ds(0, PML), pl.ds(0, cols), own], A.at[:, pl.ds(0, PML), pl.ds(0, cols), far], other)]
    yx_aux = [remote(halo_aux.at[d, :, :, :, own], halo_aux.at[d, :, :, :, far], other) for d in (0, 1)]
    y_mat = [remote(mat.at[pl.ds(0, cols), own], mat.at[pl.ds(0, cols), far], other)]
    yx_mat = [remote(halo_mat.at[d, :, own], halo_mat.at[d, :, far], other) for d in (0, 1)]

    def z_copies(sender, lanes):
        z_numbered[0] = 0
        sent, passed = [], []
        for k in range(half // SPAN):
            sent.append([
                z_remote(staged(lo, k * SPAN, SPAN), fields(lo, half + k * SPAN, SPAN, cols, lanes), sender)
                for lo, r in args
            ])
            at, n = chunks[k]
            passed.append([z_remote(tiles(d, at, n, own), tiles(d, pairs + at, n, lanes), sender) for d in (0, 1)])
        return sent, passed

    z_own, z_passed = z_copies(gy, z_lanes)
    z_from = [z_copies(0, far), z_copies(1, own)]

    def pack_pair(q, carry):
        for c in range(6):
            pack[0, q, c, 0:COLS] = own_fields[c, 2 * q, 0:COLS]
            pack[0, q, c, COLS:] = own_fields[c, 2 * q + 1, 0:COLS]
            pack[1, q, c, 0:COLS] = own_fields[c, 2 * q + 1, cols - COLS : cols]
            pack[1, q, c, COLS:] = own_fields[c, 2 * q, cols - COLS : cols]
        return carry

    def pack_aux_pair(q, carry):
        for c in range(4):
            pack_aux[0, q, c, 0:COLS] = A[c, 2 * q, 0:COLS, 0:rows]
            pack_aux[0, q, c, COLS:] = A[c, 2 * q + 1, 0:COLS, 0:rows]
            pack_aux[1, q, c, 0:COLS] = A[c, 2 * q + 1, cols - COLS : cols, 0:rows]
            pack_aux[1, q, c, COLS:] = A[c, 2 * q, cols - COLS : cols, 0:rows]
        return carry

    load_mat.wait()
    m = (mat_own[...] == 1).astype(jnp.float32)
    mat[0:cols, 0:rows] = m
    pack_mat[0] = m[0 : 2 * COLS]
    pack_mat[1] = m[cols - 2 * COLS : cols]
    each(stage_low, "wait")()
    lax.fori_loop(0, quads, pack_pair, 0)
    each(stage_high, "wait")()
    lax.fori_loop(quads, pairs, pack_pair, 0)

    @pl.when(at_edge)
    def _():
        load_aux.wait()
        lax.fori_loop(0, PML // 2, pack_aux_pair, 0)

    pl.semaphore_wait(barrier, 3 + has_pred.astype(jnp.int32) + 2 * takes_z.astype(jnp.int32))

    when(has_pred, each(z_own[0], "start"))
    each(x_mat + y_mat, "start")()
    when(at_front, each(x_aux + y_aux, "start"))
    for k in range(AHEAD):
        each(x_halo[k], "start")()
    when(high_part, each(y_low, "start"))
    each(y_high, "start")()

    def clear(lo, n):
        def plane(a, carry):
            for c in range(6):
                F[c, a] = jnp.zeros((wide, 2 * rows), jnp.float32)
            return carry

        lax.fori_loop(lo, lo + n, plane, 0)

    clear(0, PAD)
    when(jnp.logical_and(at_back, high_part), lambda: clear(PAD + half, half))

    def joined(r, l):
        low = lax.broadcasted_iota(jnp.int32, (2 * COLS, 2 * rows), 0) < COLS
        return jnp.where(low, r, l), pltpu.roll(jnp.where(low, l, r), COLS, 0)

    def unpack(q, carry):
        at = PAD + 2 * q - start
        for c in range(6):
            F[c, at, cols:wide], F[c, at + 1, cols:wide] = joined(halo[0, q, c], halo[1, q, c])
        return carry

    def unpack_aux(q, carry):
        for c in range(4):
            A[c, 2 * q, cols:wide], A[c, 2 * q + 1, cols:wide] = joined(halo_aux[0, q, c], halo_aux[1, q, c])
        return carry

    nx, ny = wide - 1, 2 * rows - 1

    def group(a, s, shift, absorbing):
        E = [[F[c, a + i] for c in range(3)] for i in range(GROUP + 1)]
        H = [[F[c, a + i] for c in range(3, 6)] for i in range(GROUP)]
        before = F[3, a - 1], F[4, a - 1]
        rates = []
        states = []
        if absorbing:
            for i in range(GROUP):
                k = a + i - shift
                inside = jnp.logical_and(k >= 0, k < PML)
                at = jnp.where(inside, k, PML)
                m = jnp.where(at_front, PML - 1 - k, k)
                b = jnp.float32(DEPTH_RATES[0])
                for j in range(1, PML):
                    b = jnp.where(m == j, jnp.float32(DEPTH_RATES[j]), b)
                rates.append((inside, at, b))
                states.append([A[c, at] for c in range(4)])

        new_states = []

        def absorb(c, i, g):
            if not absorbing:
                return g
            inside, at, b = rates[i]
            g_new = jnp.where(inside, b * (g + states[i][c]), g)
            new_states.append((c, at, g_new - g))
            return g_new

        new_h = []
        for i in range(GROUP):
            ex, ey, ez = E[i]
            slope_y = absorb(0, i, E[i + 1][1] - ey)
            slope_x = absorb(1, i, E[i + 1][0] - ex)
            hx = H[i][0] - courant * ((pltpu.roll(ez, ny, 1) - ez) - slope_y)
            hy = H[i][1] - courant * (slope_x - (pltpu.roll(ez, nx, 0) - ez))
            hz = H[i][2] - courant * ((pltpu.roll(ey, nx, 0) - ey) - (pltpu.roll(ex, ny, 1) - ex))
            new_h.append((hx, hy, hz))
        new_e = []
        for i in range(GROUP):
            ex, ey, ez = E[i]
            hx, hy, hz = new_h[i]
            below = before if i == 0 else new_h[i - 1]
            factor = courant / (eps_ref[...] + kap_ref[...] * (ex * ex + ey * ey + ez * ez))
            slope_hy = absorb(2, i, hy - below[1])
            slope_hx = absorb(3, i, hx - below[0])
            new_e.append((
                ex + factor * ((hz - pltpu.roll(hz, 1, 1)) - slope_hy),
                ey + factor * (slope_hx - (hz - pltpu.roll(hz, 1, 0))),
                ez + factor * ((hy - pltpu.roll(hy, 1, 0)) - (hx - pltpu.roll(hx, 1, 1))),
            ))
        for i in range(GROUP):
            for c in range(3):
                F[c, a + i] = new_e[i][c]
                F[3 + c, a + i] = new_h[i][c]
        for c, at, value in new_states:
            A[c, at] = value

    def sweep(s, lo):
        shift = PAD + s + jnp.where(at_front, 0, planes - PML) - start
        a = PAD + lo
        inside = jnp.logical_and(at_edge, jnp.logical_and(a + GROUP > shift, a < shift + PML))
        when(inside, lambda: group(a, s, shift, True))
        when(jnp.logical_not(inside), lambda: group(a, s, shift, False))

        @pl.when(jnp.logical_and(at_back, high_part))
        def _():
            def plane(p, carry):
                for c in range(3):
                    F[c, p] = jnp.zeros((wide, 2 * rows), jnp.float32)
                return carry

            lax.fori_loop(jnp.maximum(a, PAD + half + s), a + GROUP, plane, 0)

    def arrive(k):
        each(x_halo[k], "wait")()
        if k == 0:
            when(at_back, each(x_aux + y_aux, "start"))
        if k + AHEAD < len(x_halo):
            each(x_halo[k + AHEAD], "start")()
        if k < half // SPAN:
            when(has_pred, each(z_passed[k], "start"))
            if k + 1 < half // SPAN:
                when(has_pred, each(z_own[k + 1], "start"))
            when(high_part, each(yx[k], "start"))
        else:
            each(yx[k], "start")()

    def pass_aux():
        each(x_aux, "wait")()
        each(yx_aux, "start")()

    def take_aux():
        each(y_aux + yx_aux, "wait")()
        lax.fori_loop(0, PML // 2, unpack_aux, 0)

    n_half = half // SPAN
    back_low = jnp.logical_and(at_back, low_part)
    back_high = jnp.logical_and(at_back, high_part)

    each(x_mat, "wait")()
    each(yx_mat, "start")()
    when(at_front, pass_aux)

    @pl.when(high_part)
    def _():
        for k in range(n_half):
            arrive(k)

    when(back_high, pass_aux)
    each(y_mat + yx_mat, "wait")()
    low = lax.broadcasted_iota(jnp.int32, (2 * COLS, 2 * rows), 0) < COLS
    mat[cols:wide] = jnp.where(low, halo_mat[0], halo_mat[1])
    core = mat[...] > 0.5
    eps_ref[...] = jnp.where(core, jnp.float32(eps_core), jnp.float32(eps_clad))
    kap_ref[...] = jnp.where(core, kerr_ref[1], kerr_ref[0])

    results = ((0, elec_out), (3, magn_out))
    store, hand, store_handed = [], [], []
    for t in range(n_half):
        there = [r.at[:, pl.ds(start + t * SPAN, SPAN)] for _, r in results]
        store.append([local(fields(lo, STEPS + t * SPAN, SPAN, cols, own), r) for (lo, _), r in zip(results, there)])
        landed = [handed.at[pl.ds(lo, 3), pl.ds(t * SPAN, SPAN)] for lo, _ in results]
        hand.append([remote(fields(lo, STEPS + t * SPAN, SPAN, cols, far), r, other) for (lo, _), r in zip(results, landed)])
        theirs = [r.at[:, pl.ds(half - start + t * SPAN, SPAN)] for _, r in results]
        store_handed.append([local(src, r) for src, r in zip(landed, theirs)])

    def prepare(j):
        @pl.when(low_part)
        def _():
            if j == 0:
                each(load_low, "wait")()
            if j == n_half:
                each(load_high, "wait")()
                when(at_back, pass_aux)
            arrive(j)
            if j == 0:
                each(y_low, "wait_recv")()
                when(at_front, take_aux)
            if j == n_half:
                each(y_high, "wait_recv")()
                when(at_back, take_aux)
            each(yx[j], "wait_recv")()

        if j < n_half:
            @pl.when(high_part)
            def _():
                if j == 0:
                    each(load_high, "wait")()
                arrive(j + n_half)
                if j == 0:
                    each(y_high, "wait_recv")()
                    when(at_edge, take_aux)
                each(yx[j + n_half], "wait_recv")()
        else:
            @pl.when(takes_z)
            def _():
                for sent, passed in z_from:
                    each(sent[j - n_half] + passed[j - n_half], "wait_recv")()

    def stage(j, carry):
        for k in range(2 * n_half):
            when(j == k, functools.partial(prepare, k))

        @pl.when(jnp.logical_not(jnp.logical_and(back_high, j >= n_half)))
        def _():
            at = quads * gy + PAIRS * j
            lax.fori_loop(at, at + PAIRS, unpack, 0)

        def step(s, carry):
            sweep(s, SPAN * j - 1 - s)
            return carry

        lax.fori_loop(0, jnp.where(j == 0, STEPS // 2, STEPS), step, 0)
        for t in range(n_half):
            when(j == t + n_half, each(hand[t] + store[t], "start"))
        return carry

    lax.fori_loop(0, 2 * n_half, stage, 0)

    @pl.when(has_pred)
    def _():
        for k in range(n_half):
            each(z_own[k] + z_passed[k], "wait_send")()

    @pl.when(high_part)
    def _():
        each(y_low, "wait_send")()
        for k in range(n_half):
            each(yx[k], "wait_send")()

    each(y_high, "wait_send")()
    for k in range(n_half, 2 * n_half):
        each(yx[k], "wait_send")()
    for t in range(n_half):
        for copy, on in zip(hand[t], store_handed[t]):
            copy.wait_recv()
            on.start()
    for t in range(n_half):
        each(hand[t], "wait_send")()
        each(store[t] + store_handed[t], "wait")()


def write_out(e_ref, h_ref, elec_out, magn_out, held, in_sem, out_sem):
    refs = ((e_ref, elec_out), (h_ref, magn_out))
    parts = [(i, c) for i in range(2) for c in range(3)]
    into = [pltpu.make_async_copy(refs[i][0].at[c], held.at[i, c], in_sem.at[i, c]) for i, c in parts]
    back = [pltpu.make_async_copy(held.at[i, c], refs[i][1].at[c], out_sem.at[i, c]) for i, c in parts]
    for copy in into:
        copy.start()
    for first, second in zip(into, back):
        first.wait()
        second.start()
    for copy in back:
        copy.wait()


def shards(sizes, electric, magnetic, aux_state, material, kerr_strength):
    _, planes, cols, rows = electric.shape
    wide, deep = cols + 2 * COLS, planes + HALO
    f32 = jnp.float32
    any_space = pl.BlockSpec(memory_space=pl.ANY)
    hbm = pl.BlockSpec(memory_space=pltpu.HBM)
    shape = jax.ShapeDtypeStruct(electric.shape, f32)
    fields = pl.pallas_call(
        functools.partial(kernel, sizes),
        out_shape=(shape, shape),
        in_specs=[pl.BlockSpec(memory_space=pltpu.SMEM), hbm, hbm, hbm, hbm],
        out_specs=(any_space, any_space),
        scratch_shapes=[
            pltpu.VMEM((6, PAD + planes, wide, 2 * rows), f32),
            pltpu.VMEM((4, PML + 1, wide, 2 * rows), f32),
            pltpu.VMEM((wide, 2 * rows), f32),
            pltpu.VMEM((wide, 2 * rows), f32),
            pltpu.VMEM((wide, 2 * rows), f32),
            pltpu.VMEM((cols, rows), jnp.int32),
            pltpu.VMEM((6, planes, cols, rows), f32),
            pltpu.VMEM((6, planes // 2, cols, rows), f32),
            pltpu.VMEM((2, planes // 2, 6, 2 * COLS, rows), f32),
            pltpu.VMEM((2, PML // 2, 4, 2 * COLS, rows), f32),
            pltpu.VMEM((2, 2 * COLS, rows), f32),
            pltpu.VMEM((2, deep // 2, 6, 2 * COLS, 2 * rows), f32),
            pltpu.VMEM((2, PML // 2, 4, 2 * COLS, 2 * rows), f32),
            pltpu.VMEM((2, 2 * COLS, 2 * rows), f32),
            pltpu.SemaphoreType.DMA((24,)),
            pltpu.SemaphoreType.DMA((40,)),
            pltpu.SemaphoreType.DMA((40,)),
            pltpu.SemaphoreType.DMA((8,)),
            pltpu.SemaphoreType.DMA((8, 2)),
        ],
        compiler_params=pltpu.CompilerParams(
            collective_id=0, has_side_effects=True, vmem_limit_bytes=60 * 2**20
        ),
    )(kerr_strength, electric, magnetic, aux_state, material)
    return pl.pallas_call(
        write_out,
        out_shape=(shape, shape),
        in_specs=[any_space, any_space],
        out_specs=(hbm, hbm),
        scratch_shapes=[
            pltpu.VMEM((2,) + electric.shape, f32),
            pltpu.SemaphoreType.DMA((2, 3)),
            pltpu.SemaphoreType.DMA((2, 3)),
        ],
        compiler_params=pltpu.CompilerParams(vmem_limit_bytes=60 * 2**20),
    )(*fields)


def solution(mesh):
    sizes = tuple(mesh.shape[axis] for axis in ("gz", "gx", "gy"))
    in_specs = (
        P(None, "gz", "gx", "gy"),
        P(None, "gz", "gx", "gy"),
        P(None, None, None, "gx", "gy"),
        P("gx", "gy"),
        P(),
    )
    out_specs = (P(None, "gz", "gx", "gy"), P(None, "gz", "gx", "gy"))
    return jax.shard_map(
        functools.partial(shards, sizes),
        mesh=mesh, in_specs=in_specs, out_specs=out_specs, check_vma=False,
    )
```
